32 devices in a mesh: seq: 8 (over z, x), shard: 4 (over y, core).
Axes of the slice: x: 2, y: 2, z: 4, core: 2. Of those that a mesh axis runs over, the one named last changes fastest.
Arguments:
- tokens: bfloat16 [32768, 640], P(('seq', 'shard')), may hold values from -6 to 6
- query_weight: bfloat16 [640, 1024], P('shard')
- key_weight: bfloat16 [640, 256], P('shard')
- value_weight: bfloat16 [640, 256], P('shard'), may hold values from -0.25 to 0.25
- out_weight: bfloat16 [1024, 640], P('shard'), may hold values from -0.1875 to 0.1875
- gate_weight: bfloat16 [640, 2048], P('shard'), may hold values from -0.25 to 0.25
- up_weight: bfloat16 [640, 2048], P('shard'), may hold values from -0.25 to 0.25
- down_weight: bfloat16 [2048, 640], P('shard'), may hold values from -0.125 to 0.125
- input_gain: bfloat16 [640], P('shard'), may hold values from 0.25 to 1.75
- query_gain: bfloat16 [256], P('shard'), may hold values from 0.5 to 2
- key_gain: bfloat16 [256], P('shard'), may hold values from 0.5 to 2
- attended_gain: bfloat16 [640], P('shard'), may hold values from 0.25 to 1.75
- middle_gain: bfloat16 [640], P('shard'), may hold values from 0.25 to 1.75
- output_gain: bfloat16 [640], P('shard'), may hold values from 0.25 to 1.75
- cotangent: bfloat16 [32768, 640], P(('seq', 'shard')), may hold values from -12 to 12
Outputs:
- block_out: bfloat16 [32768, 640], P(('seq', 'shard'))
- grad_tokens: bfloat16 [32768, 640], P(('seq', 'shard'))
- grad_query_weight: float32 [640, 1024], P('shard')
- grad_key_weight: float32 [640, 256], P('shard')
- grad_value_weight: float32 [640, 256], P('shard')
- grad_out_weight: float32 [1024, 640], P('shard')
- grad_gate_weight: float32 [640, 2048], P('shard')
- grad_up_weight: float32 [640, 2048], P('shard')
- grad_down_weight: float32 [2048, 640], P('shard')
- grad_input_gain: float32 [640], P('shard')
- grad_query_gain: float32 [256], P('shard')
- grad_key_gain: float32 [256], P('shard')
- grad_attended_gain: float32 [640], P('shard')
- grad_middle_gain: float32 [640], P('shard')
- grad_output_gain: float32 [640], P('shard')
The draws below stay inside these ranges and needn't reach their ends.
All inputs are finite; a program needn't handle non-finite values.
Results may differ from the reference program's by a relative error of at most 0.025.
Values may be sent and summed in bfloat16 or wider, within the bound.
No kernel may reach another device: no remote copies, remote signals or barrier semaphores. Data moves between devices by JAX's collectives and lax.ppermute only.
A program may use at most 256 MiB of HBM per device.

```python
import math
import jax
import jax.numpy as jnp
from jax import lax

D = 640
HEADS = 4
HEAD_DIM = 256
FF = 2048
WINDOW = 512
TOKENS = 32768
SEQ_LEN = 8192
NSEQ = 4


def draw_key_weight(key, part):
    base = jnp.clip(jax.random.normal(jax.random.fold_in(key, 11), (D, HEAD_DIM), jnp.float32), -4.0, 4.0)
    return (base * D ** (-0.5)).astype(jnp.bfloat16)


def draw_query_weight(key, part):
    noise = jnp.clip(jax.random.normal(jax.random.fold_in(key, 13), (D, HEADS * HEAD_DIM), jnp.float32), -4.0, 4.0)
    return (noise * D ** (-0.5)).astype(jnp.bfloat16)


def log_spread(key, lowest, highest):
    uniform_draw = jax.random.uniform(key, (HEAD_DIM,), jnp.float32)
    return jnp.exp(math.log(lowest) + uniform_draw * (math.log(highest) - math.log(lowest)))


def draw_query_gain(key, part):
    return log_spread(jax.random.fold_in(key, 21), 0.5, 2.0).astype(jnp.bfloat16)


def draw_key_gain(key, part):
    return log_spread(jax.random.fold_in(key, 23), 0.5, 2.0).astype(jnp.bfloat16)


def draw_cotangent(key, part):
    rising = jnp.exp(jnp.arange(TOKENS, dtype=jnp.float32) * (math.log(3.0) / TOKENS))[:, None]
    return (jnp.clip(jax.random.normal(jax.random.fold_in(key, 31), (TOKENS, D), jnp.float32), -4.0, 4.0) * rising).astype(jnp.bfloat16)


def block_scale(rng, extent, cuts, smallest, top_value):
    def one(axis_at, blocks):
        steps = jax.random.uniform(jax.random.fold_in(jax.random.fold_in(rng, 6), axis_at), (blocks,), jnp.float32, smallest / len(cuts), top_value / len(cuts))
        return jnp.repeat(jnp.exp(steps), extent[axis_at] // blocks).reshape((-1,) + (1,) * (len(extent) - axis_at - 1))

    loudness = one(*cuts[0])
    for cut in cuts[1:]:
        loudness = loudness * one(*cut)
    return loudness


def bell_draw(own_key, dims, spread, reach, split=(), held_as=jnp.bfloat16):
    values = spread * jax.random.normal(own_key, dims, jnp.float32)
    if split:
        values = values * block_scale(own_key, dims, split, -0.22, 0.18)
    return jnp.clip(values, -reach, reach).astype(held_as)


def setup_inputs(seed: int = 0) -> dict:
    keys = jax.random.split(jax.random.key(seed), 16)
    return {
        "tokens": bell_draw(keys[0], (TOKENS, D), 1.0, 6.0, ((0, 32),)),
        "query_weight": draw_query_weight(jax.random.fold_in(keys[15], 71), 0),
        "key_weight": draw_key_weight(jax.random.fold_in(keys[15], 71), 0),
        "value_weight": bell_draw(keys[3], (D, HEAD_DIM), D ** -0.5, 0.25, ((0, 4),)),
        "out_weight": bell_draw(keys[4], (HEADS * HEAD_DIM, D), (HEADS * HEAD_DIM) ** -0.5, 0.1875, ((0, 4),)),
        "gate_weight": bell_draw(keys[5], (D, FF), D ** -0.5, 0.25, ((0, 4),)),
        "up_weight": bell_draw(keys[6], (D, FF), D ** -0.5, 0.25, ((0, 4),)),
        "down_weight": bell_draw(keys[7], (FF, D), FF ** -0.5, 0.125, ((0, 4),)),
        "input_gain": jnp.clip(1.0 + 0.15 * jax.random.normal(keys[8], (D,), jnp.float32), 0.25, 1.75).astype(jnp.bfloat16),
        "query_gain": draw_query_gain(jax.random.fold_in(keys[15], 71), 0),
        "key_gain": draw_key_gain(jax.random.fold_in(keys[15], 71), 0),
        "attended_gain": jnp.clip(1.0 + 0.15 * jax.random.normal(keys[11], (D,), jnp.float32), 0.25, 1.75).astype(jnp.bfloat16),
        "middle_gain": jnp.clip(1.0 + 0.15 * jax.random.normal(keys[12], (D,), jnp.float32), 0.25, 1.75).astype(jnp.bfloat16),
        "output_gain": jnp.clip(1.0 + 0.15 * jax.random.normal(keys[13], (D,), jnp.float32), 0.25, 1.75).astype(jnp.bfloat16),
        "cotangent": draw_cotangent(jax.random.fold_in(keys[15], 71), 0),
    }


EPS = 1e-06
ROPE_BASE = 10000.0
MASKED = -1e+30

def normalize(values_in, weights):
    factor = lax.rsqrt(lax.optimization_barrier(jnp.mean(values_in * values_in, axis=-1, keepdims=True)) + EPS)
    return values_in * factor * weights

def normalize_back(values_in, weights, incoming):
    factor = lax.rsqrt(lax.optimization_barrier(jnp.mean(values_in * values_in, axis=-1, keepdims=True)) + EPS)
    united = values_in * factor
    scaled = incoming * weights
    result = factor * (scaled - united * lax.optimization_barrier(jnp.mean(scaled * united, axis=-1, keepdims=True)))
    return (result, incoming * united)

def column_total(terms):
    return lax.optimization_barrier(jnp.sum(terms.reshape(-1, terms.shape[-1]), axis=0))

def rotary_tables(positions):
    halfway = HEAD_DIM // 2
    frequencies = ROPE_BASE ** (-(jnp.arange(halfway, dtype=jnp.float32) * 2.0 / HEAD_DIM))
    angles = positions.astype(jnp.float32)[:, None] * frequencies[None, :]
    return (jnp.cos(angles), jnp.sin(angles))

def rotate(values_in, cosine_table, sine_table):
    halfway = values_in.shape[-1] // 2
    first_half = values_in[..., :halfway]
    second_half = values_in[..., halfway:]
    return jnp.concatenate([first_half * cosine_table - second_half * sine_table, second_half * cosine_table + first_half * sine_table], axis=-1)

def rotate_back(values_in, cosine_table, sine_table):
    halfway = values_in.shape[-1] // 2
    first_half = values_in[..., :halfway]
    second_half = values_in[..., halfway:]
    return jnp.concatenate([first_half * cosine_table + second_half * sine_table, second_half * cosine_table - first_half * sine_table], axis=-1)

def gelu_pair(gate_proj):
    activated, pullback = jax.vjp(lambda inner: jax.nn.gelu(inner, approximate=True), gate_proj)
    return (activated, pullback(jnp.ones_like(gate_proj))[0])

def widen(narrow):
    return lax.optimization_barrier(narrow).astype(jnp.float32)

def block_scores(queries, keys_block, query_pos, key_pos):
    scores = jnp.einsum('qhd,kd->hqk', queries, keys_block) * HEAD_DIM ** (-0.5)
    distance_grid = query_pos[:, None] - key_pos[None, :]
    allowed = (distance_grid >= 0) & (distance_grid < WINDOW) & (key_pos[None, :] >= 0)
    return jnp.where(allowed[None], scores, MASKED)

def sequence_pass(tokens_seq, cotangent_seq, matrices, gains):
    query_weight, key_weight, value_weight, out_weight, gate_weight, up_weight, down_weight = matrices
    input_gain, query_gain, key_gain, attended_gain, middle_gain, output_gain = gains
    length = tokens_seq.shape[0]
    block_rows = min(length, 512)
    block_count = length // block_rows
    positions = jnp.arange(length, dtype=jnp.int32)
    cosine_table, sine_table = rotary_tables(positions)
    inputs = tokens_seq.astype(jnp.float32)
    normed_in = normalize(inputs, input_gain).astype(jnp.bfloat16)
    query_proj = jnp.dot(normed_in, query_weight, preferred_element_type=jnp.float32).reshape(length, HEADS, HEAD_DIM)
    key_raw = jnp.dot(normed_in, key_weight, preferred_element_type=jnp.float32)
    value_raw = jnp.dot(normed_in, value_weight, preferred_element_type=jnp.float32)
    query_rot = rotate(normalize(query_proj, query_gain), cosine_table[:, None], sine_table[:, None]).astype(jnp.bfloat16)
    key_rot = rotate(normalize(key_raw, key_gain), cosine_table, sine_table).astype(jnp.bfloat16)
    value_rnd = value_raw.astype(jnp.bfloat16)
    key_padded = jnp.concatenate([jnp.zeros((WINDOW, HEAD_DIM), jnp.bfloat16), key_rot], axis=0)
    value_padded = jnp.concatenate([jnp.zeros((WINDOW, HEAD_DIM), jnp.bfloat16), value_rnd], axis=0)
    begin_rows = jnp.arange(block_count, dtype=jnp.int32) * block_rows

    def window_of(begin_row):
        queries = widen(lax.dynamic_slice_in_dim(query_rot, begin_row, block_rows, 0))
        keys_block = widen(lax.dynamic_slice_in_dim(key_padded, begin_row, block_rows + WINDOW, 0))
        values_block = widen(lax.dynamic_slice_in_dim(value_padded, begin_row, block_rows + WINDOW, 0))
        query_pos = begin_row + jnp.arange(block_rows, dtype=jnp.int32)
        key_pos = begin_row - WINDOW + jnp.arange(block_rows + WINDOW, dtype=jnp.int32)
        return (queries, keys_block, values_block, block_scores(queries, keys_block, query_pos, key_pos))

    def forward_block(unused, begin_row):
        queries, keys_block, values_block, scores = window_of(begin_row)
        highest = lax.optimization_barrier(jnp.max(scores, axis=-1, keepdims=True))
        logsum = highest + jnp.log(lax.optimization_barrier(jnp.sum(jnp.exp(scores - highest), axis=-1, keepdims=True)))
        weighting = jnp.exp(scores - logsum).astype(jnp.bfloat16)
        mixture = jnp.einsum('hqk,kd->qhd', widen(weighting), values_block)
        return (unused, (mixture.astype(jnp.bfloat16), logsum))
    _, (attended_blocks, logsums) = lax.scan(forward_block, jnp.zeros((), jnp.float32), begin_rows)
    attended = attended_blocks.reshape(length, HEADS * HEAD_DIM)
    attn_proj = jnp.dot(attended, out_weight, preferred_element_type=jnp.float32)
    middle = inputs + normalize(attn_proj, attended_gain)
    normed_mid = normalize(middle, middle_gain).astype(jnp.bfloat16)
    gate_proj = jnp.dot(normed_mid, gate_weight, preferred_element_type=jnp.float32)
    up_proj = jnp.dot(normed_mid, up_weight, preferred_element_type=jnp.float32)
    activated, gelu_slope = gelu_pair(gate_proj)
    hidden = (activated * up_proj).astype(jnp.bfloat16)
    down_proj = jnp.dot(hidden, down_weight, preferred_element_type=jnp.float32)
    block_out = (middle + normalize(down_proj, output_gain)).astype(jnp.bfloat16)
    incoming = cotangent_seq.astype(jnp.float32)
    d_down, output_terms = normalize_back(down_proj, output_gain, incoming)
    d_down_rnd = d_down.astype(jnp.bfloat16)
    grad_down = jnp.dot(hidden.T, d_down_rnd, preferred_element_type=jnp.float32)
    d_hidden = jnp.dot(d_down_rnd, down_weight.T, preferred_element_type=jnp.float32)
    d_gate = (d_hidden * up_proj * gelu_slope).astype(jnp.bfloat16)
    d_up = (d_hidden * activated).astype(jnp.bfloat16)
    grad_gate = jnp.dot(normed_mid.T, d_gate, preferred_element_type=jnp.float32)
    grad_up = jnp.dot(normed_mid.T, d_up, preferred_element_type=jnp.float32)
    d_normed_mid = jnp.dot(d_gate, gate_weight.T, preferred_element_type=jnp.float32) + jnp.dot(d_up, up_weight.T, preferred_element_type=jnp.float32)
    d_middle_part, middle_terms = normalize_back(middle, middle_gain, d_normed_mid)
    d_middle = incoming + d_middle_part
    d_attn, attended_terms = normalize_back(attn_proj, attended_gain, d_middle)
    d_attn_rnd = d_attn.astype(jnp.bfloat16)
    grad_out = jnp.dot(attended.T, d_attn_rnd, preferred_element_type=jnp.float32)
    d_attended = jnp.dot(d_attn_rnd, out_weight.T, preferred_element_type=jnp.float32).astype(jnp.bfloat16)
    d_attended_blocks = d_attended.reshape(block_count, block_rows, HEADS, HEAD_DIM)

    def backward_block(accumulated, block_inputs):
        begin_row, logsum, d_out_block = block_inputs
        key_acc, value_acc = accumulated
        queries, keys_block, values_block, scores = window_of(begin_row)
        weighting = jnp.exp(scores - logsum)
        weighting_rnd = weighting.astype(jnp.bfloat16)
        d_out_wide = widen(d_out_block)
        d_weighting = jnp.einsum('qhd,kd->hqk', d_out_wide, values_block)
        row_dot = lax.optimization_barrier(jnp.sum(weighting * d_weighting, axis=-1, keepdims=True))
        d_scores = widen((weighting * (d_weighting - row_dot) * HEAD_DIM ** (-0.5)).astype(jnp.bfloat16))
        d_query_block = jnp.einsum('hqk,kd->qhd', d_scores, keys_block)
        d_key_block = jnp.einsum('hqk,qhd->kd', d_scores, queries)
        d_value_block = jnp.einsum('hqk,qhd->kd', widen(weighting_rnd), d_out_wide)
        key_acc = lax.dynamic_update_slice_in_dim(key_acc, lax.dynamic_slice_in_dim(key_acc, begin_row, block_rows + WINDOW, 0) + d_key_block, begin_row, 0)
        value_acc = lax.dynamic_update_slice_in_dim(value_acc, lax.dynamic_slice_in_dim(value_acc, begin_row, block_rows + WINDOW, 0) + d_value_block, begin_row, 0)
        return ((key_acc, value_acc), d_query_block)
    empty = jnp.zeros((length + WINDOW, HEAD_DIM), jnp.float32)
    (key_acc, value_acc), d_query_blocks = lax.scan(backward_block, (empty, empty), (begin_rows, logsums, d_attended_blocks))
    d_query_rot = d_query_blocks.reshape(length, HEADS, HEAD_DIM)
    d_query, query_terms = normalize_back(query_proj, query_gain, rotate_back(d_query_rot, cosine_table[:, None], sine_table[:, None]))
    d_key, key_terms = normalize_back(key_raw, key_gain, rotate_back(key_acc[WINDOW:], cosine_table, sine_table))
    d_query_rnd = d_query.reshape(length, HEADS * HEAD_DIM).astype(jnp.bfloat16)
    d_key_rnd = d_key.astype(jnp.bfloat16)
    d_value_rnd = value_acc[WINDOW:].astype(jnp.bfloat16)
    grad_query = jnp.dot(normed_in.T, d_query_rnd, preferred_element_type=jnp.float32)
    grad_key = jnp.dot(normed_in.T, d_key_rnd, preferred_element_type=jnp.float32)
    grad_value = jnp.dot(normed_in.T, d_value_rnd, preferred_element_type=jnp.float32)
    d_normed_in = jnp.dot(d_query_rnd, query_weight.T, preferred_element_type=jnp.float32) + jnp.dot(d_key_rnd, key_weight.T, preferred_element_type=jnp.float32) + jnp.dot(d_value_rnd, value_weight.T, preferred_element_type=jnp.float32)
    d_inputs, input_terms = normalize_back(inputs, input_gain, d_normed_in)
    grad_tokens = (d_middle + d_inputs).astype(jnp.bfloat16)
    gradients = (grad_query, grad_key, grad_value, grad_out, grad_gate, grad_up, grad_down, column_total(input_terms), column_total(query_terms), column_total(key_terms), column_total(attended_terms), column_total(middle_terms), column_total(output_terms))
    return (block_out, grad_tokens, gradients)

def reference(tokens, query_weight, key_weight, value_weight, out_weight, gate_weight, up_weight, down_weight, input_gain, query_gain, key_gain, attended_gain, middle_gain, output_gain, cotangent):
    matrices = (query_weight, key_weight, value_weight, out_weight, gate_weight, up_weight, down_weight)
    gains = tuple((single.astype(jnp.float32) for single in (input_gain, query_gain, key_gain, attended_gain, middle_gain, output_gain)))
    shaped_tokens = tokens.reshape(NSEQ, SEQ_LEN, D)
    shaped_cotangent = cotangent.reshape(NSEQ, SEQ_LEN, D)
    starting = tuple((jnp.zeros(single.shape, jnp.float32) for single in matrices + gains))

    def one_sequence(totals, sequence_pair):
        block_out, grad_tokens, gradients = sequence_pass(sequence_pair[0], sequence_pair[1], matrices, gains)
        return (tuple((earlier + latest for earlier, latest in zip(totals, gradients))), (block_out, grad_tokens))
    totals, (outputs, input_grads) = lax.scan(one_sequence, starting, (shaped_tokens, shaped_cotangent))
    return (outputs.reshape(TOKENS, D), input_grads.reshape(TOKENS, D), totals[0], totals[1], totals[2], totals[3], totals[4], totals[5], totals[6], totals[7], totals[8], totals[9], totals[10], totals[11], totals[12])
```

```python
import jax
import jax.numpy as jnp
from jax import lax
from jax.experimental import pallas as pl
from jax.experimental.pallas import tpu as pltpu
from jax.sharding import PartitionSpec as P

D = 640
HEADS = 4
HEAD_DIM = 256
FF = 2048
WINDOW = 512
SEQ_CAP = 8192
HALF = 512
QB = 256
ROWS = HEADS * QB
CHUNK = 512

EPS = 1e-06
ROPE_BASE = 10000.0
LOG2E = 1.4426950408889634
LN2 = 0.6931471805599453
SCALE = HEAD_DIM**-0.5

F32 = jnp.float32
BF16 = jnp.bfloat16
VM = pl.BlockSpec(memory_space=pltpu.VMEM)
SM = pl.BlockSpec(memory_space=pltpu.SMEM)
HB = pl.BlockSpec(memory_space=pl.ANY)
NN = (((1,), (0,)), ((), ()))
NT = (((1,), (1,)), ((), ()))
TN = (((0,), (0,)), ((), ()))


def dot(a, b, dims=NN):
    return lax.dot_general(a, b, dims, preferred_element_type=F32)


def params():
    return pltpu.CompilerParams(vmem_limit_bytes=60 * 2**20)


def sds(shape, dtype=BF16):
    return jax.ShapeDtypeStruct(shape, dtype)


def cost(flops, nbytes):
    return pl.CostEstimate(flops=int(flops), bytes_accessed=int(nbytes), transcendentals=0)


def rms_factor(v):
    return lax.rsqrt(jnp.mean(v * v, axis=-1, keepdims=True) + EPS)


def norm_back(v, factor, gain, incoming):
    united = v * factor
    scaled = incoming * gain
    back = factor * (scaled - united * jnp.mean(scaled * united, axis=-1, keepdims=True))
    return back, jnp.sum(incoming * united, axis=0, keepdims=True)


def offsets(me, rows):
    return (
        me * rows,
        (me + 1 - 2 * (me % 2)) * rows,
        ((me + 2) % 4) * rows,
        (3 - me) * rows,
    )


def place_copies(me, pieces, src_of, buf, rows, sems, first):
    copies = []
    for k, off in enumerate(offsets(me, rows)):
        copies.append(
            pltpu.make_async_copy(
                src_of(pieces[k]),
                buf.at[pl.ds(pl.multiple_of(off, 32), rows)],
                sems.at[first + k],
            )
        )
    return copies


def pre_kernel(me_ref, tok, gains, cos_ref, sin_ref, w0, w1, w2, w3, nin_o, qraw_o, qs_o, kraw_o, kv_o, wbuf, sems):
    rows = D // 4
    copies = place_copies(
        me_ref[0], (w0, w1, w2, w3), lambda w: w.at[pl.ds(0, rows)], wbuf, rows, sems, 0
    )
    for c in copies:
        c.start()
    x = tok[...].astype(F32)
    nin = (x * rms_factor(x) * gains[0:1, :]).astype(BF16)
    nin_o[...] = nin
    cos = cos_ref[...]
    sin = sin_ref[...]
    hd = HEAD_DIM // 2
    for c in copies:
        c.wait()
    for h in range(HEADS):
        q = dot(nin, wbuf[:, HEAD_DIM * h : HEAD_DIM * (h + 1)])
        qraw_o[h] = q.astype(BF16)
        u = q * (rms_factor(q) * (SCALE * LOG2E)) * gains[4:5, :HEAD_DIM]
        u1 = u[:, :hd]
        u2 = u[:, hd:]
        qs_o[h, :, :hd] = (u1 * cos - u2 * sin).astype(BF16)
        qs_o[h, :, hd:] = (u2 * cos + u1 * sin).astype(BF16)
    base = HEADS * HEAD_DIM
    k = dot(nin, wbuf[:, base : base + HEAD_DIM])
    kraw_o[...] = k.astype(BF16)
    u = k * rms_factor(k) * gains[5:6, :HEAD_DIM]
    u1 = u[:, :hd]
    u2 = u[:, hd:]
    kv_o[:, :hd] = (u1 * cos - u2 * sin).astype(BF16)
    kv_o[:, hd:HEAD_DIM] = (u2 * cos + u1 * sin).astype(BF16)
    kv_o[:, HEAD_DIM:] = dot(nin, wbuf[:, base + HEAD_DIM :]).astype(BF16)


def pre(me, tok, gains, cos, sin, pieces, half):
    part = pl.BlockSpec((HALF, D), lambda i: (half, 0))
    tab = pl.BlockSpec((HALF, HEAD_DIM // 2), lambda i: (half, 0))
    return pl.pallas_call(
        pre_kernel,
        grid=(1,),
        out_shape=(
            sds((HALF, D)),
            sds((HEADS, HALF, HEAD_DIM)),
            sds((HEADS, HALF, HEAD_DIM)),
            sds((HALF, HEAD_DIM)),
            sds((HALF, 2 * HEAD_DIM)),
        ),
        in_specs=[SM, part, VM, tab, tab, HB, HB, HB, HB],
        out_specs=(VM,) * 5,
        scratch_shapes=[pltpu.VMEM((D, 6 * HEAD_DIM), BF16), pltpu.SemaphoreType.DMA((4,))],
        compiler_params=params(),
        cost_estimate=cost(2 * HALF * D * 1536, 5e6),
        name="pre",
    )(me, tok, gains, cos, sin, *pieces)


def key_blocks(j, kvp, kvs, lo, hi):
    blocks = (kvp[0:QB, lo:hi], kvp[QB : 2 * QB, lo:hi], kvs[0:QB, lo:hi], kvs[QB : 2 * QB, lo:hi])
    return blocks[j : j + 3]


def upper_mask():
    row = lax.broadcasted_iota(jnp.int32, (HEADS, QB, QB), 1).reshape(ROWS, QB)
    col = lax.broadcasted_iota(jnp.int32, (ROWS, QB), 1)
    return col > row


def att_kernel(masked, flag_ref, qs, kvp, kvs, o_o, pm_o, p1_o):
    upper = upper_mask()
    for j in range(2):
        sl = slice(QB * j, QB * (j + 1))
        q = qs[:, sl, :].reshape(ROWS, HEAD_DIM)
        k0, k1, k2 = key_blocks(j, kvp, kvs, 0, HEAD_DIM)
        v0, v1, v2 = key_blocks(j, kvp, kvs, HEAD_DIM, 2 * HEAD_DIM)
        em = jnp.exp2(jnp.where(upper, dot(q, k0, NT), dot(q, k2, NT)))
        e1 = jnp.exp2(dot(q, k1, NT))
        if masked:
            keep = flag_ref[0].astype(F32)
            em = em * jnp.where(upper, keep, 1.0)
            if j == 0:
                e1 = e1 * keep
        inv = 1.0 / jnp.sum(em + e1, axis=-1, keepdims=True)
        pm = (em * inv).astype(BF16)
        p1 = (e1 * inv).astype(BF16)
        zero = jnp.zeros_like(pm)
        out = dot(p1, v1) + dot(jnp.where(upper, pm, zero), v0) + dot(jnp.where(upper, zero, pm), v2)
        pm_o[:, sl, :] = pm.reshape(HEADS, QB, QB)
        p1_o[:, sl, :] = p1.reshape(HEADS, QB, QB)
        o_o[:, sl, :] = out.astype(BF16).reshape(HEADS, QB, HEAD_DIM)


def att(flag, qs, kvp, kvs, masked):
    shp = sds((HEADS, HALF, HEAD_DIM))

    def body(*refs):
        att_kernel(masked, *refs)

    return pl.pallas_call(
        body,
        out_shape=(shp, shp, shp),
        in_specs=[SM, VM, VM, VM],
        out_specs=(VM,) * 3,
        compiler_params=params(),
        cost_estimate=cost(12e9 / 4, 5e6),
        name="att",
    )(flag, qs, kvp, kvs)


def att_back_kernel(qs, qraw, kvp, kvs, pm_i, p1_i, do_i, gains, cos_ref, sin_ref, dq_o, dkvp_o, dkvs_o, gain_o, acc):
    upper = upper_mask()
    hd = HEAD_DIM // 2
    acc[...] = jnp.zeros_like(acc)
    gsum = jnp.zeros((1, HEAD_DIM), F32)
    for j in range(2):
        sl = slice(QB * j, QB * (j + 1))
        q = qs[:, sl, :].reshape(ROWS, HEAD_DIM)
        do = do_i[:, sl, :].reshape(ROWS, HEAD_DIM)
        k0, k1, k2 = key_blocks(j, kvp, kvs, 0, HEAD_DIM)
        v0, v1, v2 = key_blocks(j, kvp, kvs, HEAD_DIM, 2 * HEAD_DIM)
        pmb = pm_i[:, sl, :].reshape(ROWS, QB)
        p1b = p1_i[:, sl, :].reshape(ROWS, QB)
        dpm = jnp.where(upper, dot(do, v0, NT), dot(do, v2, NT))
        dp1 = dot(do, v1, NT)
        pm = pmb.astype(F32)
        p1 = p1b.astype(F32)
        total = jnp.sum(pm * dpm + p1 * dp1, axis=-1, keepdims=True)
        dsm = (pm * (dpm - total)).astype(BF16)
        ds1 = (p1 * (dp1 - total)).astype(BF16)
        zero = jnp.zeros_like(dsm)
        ds0 = jnp.where(upper, dsm, zero)
        ds2 = jnp.where(upper, zero, dsm)
        p0 = jnp.where(upper, pmb, zero)
        p2 = jnp.where(upper, zero, pmb)
        for t, (ds, p) in enumerate(((ds0, p0), (ds1, p1b), (ds2, p2))):
            at = slice(QB * (j + t), QB * (j + t + 1))
            acc[at, :HEAD_DIM] += dot(ds, q, TN) * LN2
            acc[at, HEAD_DIM:] += dot(p, do, TN)
        dq = (dot(ds0, k0) + dot(ds1, k1) + dot(ds2, k2)) * SCALE
        cos = cos_ref[sl, :]
        sin = sin_ref[sl, :]
        gain = gains[4:5, :HEAD_DIM]
        for h in range(HEADS):
            d1 = dq[QB * h : QB * (h + 1), :hd]
            d2 = dq[QB * h : QB * (h + 1), hd:]
            inc = jnp.concatenate([d1 * cos + d2 * sin, d2 * cos - d1 * sin], axis=-1)
            raw = qraw[h, sl, :].astype(F32)
            back, terms = norm_back(raw, rms_factor(raw), gain, inc)
            gsum = gsum + terms
            dq_o[sl, HEAD_DIM * h : HEAD_DIM * (h + 1)] = back.astype(BF16)
    dkvp_o[...] = acc[:HALF, :].astype(BF16)
    dkvs_o[...] = acc[HALF:, :]
    gain_o[...] = jnp.broadcast_to(gsum, (8, HEAD_DIM))


def att_back(qs, qraw, kvp, kvs, pm, p1, do, gains, cos, sin, half):
    dospec = pl.BlockSpec((HEADS, HALF, HEAD_DIM), lambda i: (0, half, 0))
    tab = pl.BlockSpec((HALF, HEAD_DIM // 2), lambda i: (half, 0))
    return pl.pallas_call(
        att_back_kernel,
        grid=(1,),
        out_shape=(
            sds((HALF, HEADS * HEAD_DIM)),
            sds((HALF, 2 * HEAD_DIM)),
            sds((HALF, 2 * HEAD_DIM), F32),
            sds((8, HEAD_DIM), F32),
        ),
        in_specs=[VM, VM, VM, VM, VM, VM, dospec, VM, tab, tab],
        out_specs=(VM,) * 4,
        scratch_shapes=[pltpu.VMEM((2 * HALF, 2 * HEAD_DIM), F32)],
        compiler_params=params(),
        cost_estimate=cost(24e9 / 4, 9e6),
        name="att_back",
    )(qs, qraw, kvp, kvs, pm, p1, do, gains, cos, sin)


def ffn_kernel(
    me_ref, o_lo, o_hi, tok, cot, gains,
    od0, od1, od2, od3, gu0, gu1, gu2, gu3,
    out_o, ap_o, nm_o, dd_o, a_o, b_o, gd_o, gain_o,
    wo, wg, wu, wd, hid, down, sems,
):
    me = me_ref[0]
    ods = (od0, od1, od2, od3)
    gus = (gu0, gu1, gu2, gu3)
    ro = HEADS * HEAD_DIM // 4
    rf = FF // 4
    rd = D // 4
    c_o = place_copies(me, ods, lambda w: w.at[pl.ds(0, ro)], wo, ro, sems, 0)
    c_g = place_copies(me, gus, lambda w: w.at[:, pl.ds(0, FF)], wg, rd, sems, 4)
    c_u = place_copies(me, gus, lambda w: w.at[:, pl.ds(FF, FF)], wu, rd, sems, 8)
    c_d = place_copies(me, ods, lambda w: w.at[pl.ds(ro, rf)], wd, rf, sems, 12)
    for c in c_o + c_g + c_u + c_d:
        c.start()
    for c in c_o:
        c.wait()
    for half, o in enumerate((o_lo, o_hi)):
        sl = slice(HALF * half, HALF * (half + 1))
        proj = dot(o[0], wo[0:HEAD_DIM, :])
        for h in range(1, HEADS):
            proj = proj + dot(o[h], wo[HEAD_DIM * h : HEAD_DIM * (h + 1), :])
        ap_o[sl, :] = proj.astype(BF16)
        mid = tok[sl, :].astype(F32) + proj * rms_factor(proj) * gains[1:2, :]
        nm_o[sl, :] = (mid * rms_factor(mid) * gains[2:3, :]).astype(BF16)
    for c in c_g + c_u:
        c.wait()
    down[...] = jnp.zeros_like(down)
    for c in c_d:
        c.wait()

    def chunk(i, _):
        cs = pl.ds(pl.multiple_of(i * CHUNK, CHUNK), CHUNK)
        g = dot(nm_o[...], wg[:, cs])
        u = dot(nm_o[...], wu[:, cs])
        c0 = 0.7978845608028654
        c1 = 0.044715 * c0
        g2 = g * g
        t = jnp.tanh(g * (c0 + c1 * g2))
        h = 0.5 + 0.5 * t
        a = g * h
        slope = h + a * (1.0 - h) * (2.0 * c0 + (6.0 * c1) * g2)
        hc = (a * u).astype(BF16)
        hid[:, cs] = hc
        a_o[:, cs] = a.astype(BF16)
        b_o[:, cs] = (u * slope).astype(BF16)
        down[...] += dot(hc, wd[cs, :])
        return 0

    lax.fori_loop(0, FF // CHUNK, chunk, 0)
    gsum = jnp.zeros((1, D), F32)
    for half in range(2):
        sl = slice(HALF * half, HALF * (half + 1))
        dn = down[sl, :]
        proj = ap_o[sl, :].astype(F32)
        mid = tok[sl, :].astype(F32) + proj * rms_factor(proj) * gains[1:2, :]
        fac = rms_factor(dn)
        out_o[sl, :] = (mid + dn * fac * gains[3:4, :]).astype(BF16)
        back, terms = norm_back(dn, fac, gains[3:4, :], cot[sl, :].astype(F32))
        dd_o[sl, :] = back.astype(BF16)
        gsum = gsum + terms
    gain_o[...] = jnp.broadcast_to(gsum, (8, D))

    def grad(i, _):
        cs = pl.ds(pl.multiple_of(i * CHUNK, CHUNK), CHUNK)
        gd_o[cs, :] = dot(hid[:, cs], dd_o[...], TN).astype(BF16)
        return 0

    lax.fori_loop(0, FF // CHUNK, grad, 0)


def ffn(me, o_lo, o_hi, tok, cot, gains, ods, gus):
    t = tok.shape[0]
    return pl.pallas_call(
        ffn_kernel,
        out_shape=(
            sds((t, D)),
            sds((t, D)),
            sds((t, D)),
            sds((t, D)),
            sds((t, FF)),
            sds((t, FF)),
            sds((FF, D)),
            sds((8, D), F32),
        ),
        in_specs=[SM] + [VM] * 5 + [HB] * 8,
        out_specs=(VM,) * 8,
        scratch_shapes=[
            pltpu.VMEM((HEADS * HEAD_DIM, D), BF16),
            pltpu.VMEM((D, FF), BF16),
            pltpu.VMEM((D, FF), BF16),
            pltpu.VMEM((FF, D), BF16),
            pltpu.VMEM((t, FF), BF16),
            pltpu.VMEM((t, D), F32),
            pltpu.SemaphoreType.DMA((16,)),
        ],
        compiler_params=params(),
        cost_estimate=cost(12e9, 30e6),
        name="ffn",
    )(me, o_lo, o_hi, tok, cot, gains, *ods, *gus)


def ffn_back_kernel(
    me_ref, o_lo, o_hi, tok, cot, gains, ap, nm, dd, a_i, b_i,
    od0, od1, od2, od3, gu0, gu1, gu2, gu3,
    ggu_o, go_o, do_o, dmid_o, gain_o,
    wo, wg, wu, wd, dnm, datt, sems,
):
    me = me_ref[0]
    ods = (od0, od1, od2, od3)
    gus = (gu0, gu1, gu2, gu3)
    ro = HEADS * HEAD_DIM // 4
    rf = FF // 4
    rd = D // 4
    c_d = place_copies(me, ods, lambda w: w.at[pl.ds(ro, rf)], wd, rf, sems, 12)
    c_g = place_copies(me, gus, lambda w: w.at[:, pl.ds(0, FF)], wg, rd, sems, 4)
    c_u = place_copies(me, gus, lambda w: w.at[:, pl.ds(FF, FF)], wu, rd, sems, 8)
    c_o = place_copies(me, ods, lambda w: w.at[pl.ds(0, ro)], wo, ro, sems, 0)
    for c in c_d + c_g + c_u + c_o:
        c.start()
    dnm[...] = jnp.zeros_like(dnm)
    for c in c_d + c_g + c_u:
        c.wait()

    def chunk(i, _):
        at = pl.multiple_of(i * CHUNK, CHUNK)
        cs = pl.ds(at, CHUNK)
        dh = dot(dd[...], wd[cs, :], NT)
        dg = (dh * b_i[:, cs].astype(F32)).astype(BF16)
        du = (dh * a_i[:, cs].astype(F32)).astype(BF16)
        dnm[...] += dot(dg, wg[:, cs], NT) + dot(du, wu[:, cs], NT)
        ggu_o[:, cs] = dot(nm[...], dg, TN).astype(BF16)
        ggu_o[:, pl.ds(FF + at, CHUNK)] = dot(nm[...], du, TN).astype(BF16)
        return 0

    lax.fori_loop(0, FF // CHUNK, chunk, 0)
    for c in c_o:
        c.wait()
    gm = jnp.zeros((1, D), F32)
    ga = jnp.zeros((1, D), F32)
    for half in range(2):
        sl = slice(HALF * half, HALF * (half + 1))
        proj = ap[sl, :].astype(F32)
        pfac = rms_factor(proj)
        mid = tok[sl, :].astype(F32) + proj * pfac * gains[1:2, :]
        back, terms = norm_back(mid, rms_factor(mid), gains[2:3, :], dnm[sl, :])
        dmid = cot[sl, :].astype(F32) + back
        gm = gm + terms
        dmid_o[sl, :] = dmid.astype(BF16)
        back, terms = norm_back(proj, pfac, gains[1:2, :], dmid)
        ga = ga + terms
        datt[sl, :] = back.astype(BF16)
    gain_o[0:8, :] = jnp.broadcast_to(gm, (8, D))
    gain_o[8:16, :] = jnp.broadcast_to(ga, (8, D))
    for h in range(HEADS):
        at = slice(HEAD_DIM * h, HEAD_DIM * (h + 1))
        do_o[h] = dot(datt[...], wo[at, :], NT).astype(BF16)
        go_o[at, :] = (dot(o_lo[h], datt[:HALF, :], TN) + dot(o_hi[h], datt[HALF:, :], TN)).astype(BF16)


def ffn_back(me, o_lo, o_hi, tok, cot, gains, ap, nm, dd, a, b, ods, gus):
    t = tok.shape[0]
    return pl.pallas_call(
        ffn_back_kernel,
        out_shape=(
            sds((D, 2 * FF)),
            sds((HEADS * HEAD_DIM, D)),
            sds((HEADS, t, HEAD_DIM)),
            sds((t, D)),
            sds((16, D), F32),
        ),
        in_specs=[SM] + [VM] * 10 + [HB] * 8,
        out_specs=(VM,) * 5,
        scratch_shapes=[
            pltpu.VMEM((HEADS * HEAD_DIM, D), BF16),
            pltpu.VMEM((D, FF), BF16),
            pltpu.VMEM((D, FF), BF16),
            pltpu.VMEM((FF, D), BF16),
            pltpu.VMEM((t, D), F32),
            pltpu.VMEM((t, D), BF16),
            pltpu.SemaphoreType.DMA((16,)),
        ],
        compiler_params=params(),
        cost_estimate=cost(16e9, 30e6),
        name="ffn_back",
    )(me, o_lo, o_hi, tok, cot, gains, ap, nm, dd, a, b, *ods, *gus)


def post_kernel(
    me_ref, tok, dmid, nin_lo, nin_hi, dq_lo, dq_hi, kv_a, kv_b, kv_c, kv_d, kraw_lo, kraw_hi,
    gains, cos_ref, sin_ref, w0, w1, w2, w3,
    gt_o, gw_o, gin_o, gk_o,
    wbuf, dkv, sems,
):
    rows = D // 4
    copies = place_copies(
        me_ref[0], (w0, w1, w2, w3), lambda w: w.at[pl.ds(0, rows)], wbuf, rows, sems, 0
    )
    for c in copies:
        c.start()
    hd = HEAD_DIM // 2
    base = HEADS * HEAD_DIM
    gk = jnp.zeros((1, HEAD_DIM), F32)
    for half, (first, second, kraw) in enumerate(((kv_a, kv_b, kraw_lo), (kv_c, kv_d, kraw_hi))):
        sl = slice(HALF * half, HALF * (half + 1))
        both = first[...].astype(F32) + second[...].astype(F32)
        cos = cos_ref[sl, :]
        sin = sin_ref[sl, :]
        d1 = both[:, :hd]
        d2 = both[:, hd:HEAD_DIM]
        inc = jnp.concatenate([d1 * cos + d2 * sin, d2 * cos - d1 * sin], axis=-1)
        raw = kraw[...].astype(F32)
        back, terms = norm_back(raw, rms_factor(raw), gains[5:6, :HEAD_DIM], inc)
        gk = gk + terms
        dkv[sl, :HEAD_DIM] = back.astype(BF16)
        dkv[sl, HEAD_DIM:] = both[:, HEAD_DIM:].astype(BF16)
    gk_o[...] = jnp.broadcast_to(gk, (8, HEAD_DIM))
    gw_o[:, :base] = (dot(nin_lo[...], dq_lo[...], TN) + dot(nin_hi[...], dq_hi[...], TN)).astype(BF16)
    gw_o[:, base:] = (
        dot(nin_lo[...], dkv[:HALF, :], TN) + dot(nin_hi[...], dkv[HALF:, :], TN)
    ).astype(BF16)
    for c in copies:
        c.wait()
    gi = jnp.zeros((1, D), F32)
    for half, dq in enumerate((dq_lo, dq_hi)):
        sl = slice(HALF * half, HALF * (half + 1))
        dnin = dot(dq[...], wbuf[:, :base], NT) + dot(dkv[sl, :], wbuf[:, base:], NT)
        x = tok[sl, :].astype(F32)
        back, terms = norm_back(x, rms_factor(x), gains[0:1, :], dnin)
        gi = gi + terms
        gt_o[sl, :] = (dmid[sl, :].astype(F32) + back).astype(BF16)
    gin_o[...] = jnp.broadcast_to(gi, (8, D))


def post(me, tok, dmid, nins, dqs, kvs, kraws, gains, cos, sin, pieces):
    t = tok.shape[0]
    return pl.pallas_call(
        post_kernel,
        out_shape=(
            sds((t, D)),
            sds((D, 6 * HEAD_DIM)),
            sds((8, D), F32),
            sds((8, HEAD_DIM), F32),
        ),
        in_specs=[SM] + [VM] * 15 + [HB] * 4,
        out_specs=(VM,) * 4,
        scratch_shapes=[
            pltpu.VMEM((D, 6 * HEAD_DIM), BF16),
            pltpu.VMEM((t, 2 * HEAD_DIM), BF16),
            pltpu.SemaphoreType.DMA((4,)),
        ],
        compiler_params=params(),
        cost_estimate=cost(4e9, 15e6),
        name="post",
    )(me, tok, dmid, *nins, *dqs, *kvs, *kraws, gains, cos, sin, *pieces)


def flip(x, axis, bit):
    n = lax.axis_size(axis)
    return lax.ppermute(x, axis, [(i, i ^ bit) for i in range(n)])


def gather_pieces(x):
    near = flip(x, "shard", 1)
    far = flip(x, "shard", 2)
    return (x, near, far, flip(far, "shard", 1))


def pick(x, index, axis):
    return lax.dynamic_index_in_dim(x, index, axis, keepdims=False)


def joined(a, b):
    return (a.astype(F32) + b.astype(F32)).astype(BF16)


def reduce_grad(x):
    rows, cols = x.shape[1:]
    shard = lax.axis_index("shard")
    core = shard % 2
    y = shard // 2
    x = x.reshape(2, 2, rows, cols)
    acc = joined(pick(x, core, 1), flip(pick(x, 1 - core, 1), "shard", 1))
    acc = joined(pick(acc, y, 0), flip(pick(acc, 1 - y, 0), "shard", 2))
    seq = lax.axis_index("seq")
    bits = []
    bit = 1
    while bit < lax.axis_size("seq"):
        bits.append(bit)
        bit *= 2
    for bit in bits[:-1]:
        here = (seq // bit) % 2
        acc = acc.reshape(2, acc.shape[0] // 2, cols)
        acc = joined(pick(acc, here, 0), flip(pick(acc, 1 - here, 0), "seq", bit))
    acc = joined(acc, flip(acc, "seq", bits[-1]))
    for bit in reversed(bits[:-1]):
        here = (seq // bit) % 2
        other = flip(acc, "seq", bit)
        acc = jnp.concatenate(
            [jnp.where(here == 0, acc, other), jnp.where(here == 0, other, acc)], axis=0
        )
    return acc.astype(F32)


def shards(
    tokens,
    query_weight,
    key_weight,
    value_weight,
    out_weight,
    gate_weight,
    up_weight,
    down_weight,
    input_gain,
    query_gain,
    key_gain,
    attended_gain,
    middle_gain,
    output_gain,
    cotangent,
):
    n_seq = lax.axis_size("seq")
    n_shard = lax.axis_size("shard")
    shard = lax.axis_index("shard")
    me = shard.reshape(1).astype(jnp.int32)
    count = tokens.shape[0]
    total = count * n_seq * n_shard
    length = min(SEQ_CAP, total)
    rank = lax.axis_index("seq") * n_shard + shard
    first_pos = rank * count % length
    flag = (first_pos > 0).reshape(1).astype(jnp.int32)

    gain_row = jnp.concatenate(
        [input_gain, attended_gain, middle_gain, output_gain, query_gain, key_gain]
    )
    wide = 6 * HEAD_DIM
    qkv_own = jnp.concatenate(
        [
            jnp.concatenate([query_weight, key_weight, value_weight], axis=1),
            jnp.pad(gain_row[None], ((0, 15), (0, wide - gain_row.shape[0]))),
        ],
        axis=0,
    )
    qkv = gather_pieces(qkv_own)
    gd = D // 4
    gh = HEAD_DIM // 4
    rows = jnp.stack([p[gd, : gain_row.shape[0]] for p in qkv])
    order = jnp.stack([shard, shard ^ 1, shard ^ 2, shard ^ 3])
    rows = jnp.zeros_like(rows).at[order].set(rows).astype(F32)
    gain_list = [rows[:, gd * i : gd * (i + 1)].reshape(1, D) for i in range(4)]
    gain_list += [
        jnp.pad(
            rows[:, 4 * gd + gh * i : 4 * gd + gh * (i + 1)].reshape(1, HEAD_DIM),
            ((0, 0), (0, D - HEAD_DIM)),
        )
        for i in range(2)
    ]
    gains = jnp.concatenate(gain_list + [jnp.zeros((2, D), F32)], axis=0)

    positions = first_pos + jnp.arange(count, dtype=jnp.int32)
    hd = HEAD_DIM // 2
    freq = ROPE_BASE ** (-(jnp.arange(hd, dtype=F32) * 2.0 / HEAD_DIM))
    angles = positions.astype(F32)[:, None] * freq[None, :]
    cos = jnp.cos(angles)
    sin = jnp.sin(angles)

    gus = gather_pieces(jnp.concatenate([gate_weight, up_weight], axis=1))
    ods = gather_pieces(jnp.concatenate([out_weight, down_weight], axis=0))

    nin_hi, qraw_hi, qs_hi, kraw_hi, kv_hi = pre(me, tokens, gains, cos, sin, qkv, 1)
    ranks = n_seq * n_shard
    per_seq = length // count
    pairs = [(i, i + 1) for i in range(ranks - 1) if (i + 1) % per_seq]
    halo = lax.ppermute(kv_hi, ("seq", "shard"), pairs)
    nin_lo, qraw_lo, qs_lo, kraw_lo, kv_lo = pre(me, tokens, gains, cos, sin, qkv, 0)
    o_hi, pm_hi, p1_hi = att(flag, qs_hi, kv_lo, kv_hi, False)
    o_lo, pm_lo, p1_lo = att(flag, qs_lo, halo, kv_lo, True)

    block_out, ap, nm, dd, a, b, g_down, gain_out = ffn(
        me, o_lo, o_hi, tokens, cotangent, gains, ods, gus
    )
    r_down = reduce_grad(g_down.reshape(4, FF // 4, D))
    g_gu, g_out, d_o, d_mid, gain_mid = ffn_back(
        me, o_lo, o_hi, tokens, cotangent, gains, ap, nm, dd, a, b, ods, gus
    )
    r_gu = reduce_grad(g_gu.reshape(4, D // 4, 2 * FF))
    r_out = reduce_grad(g_out.reshape(4, HEADS * HEAD_DIM // 4, D))

    dq_lo, kv_back, kv_a, gq_lo = att_back(
        qs_lo, qraw_lo, halo, kv_lo, pm_lo, p1_lo, d_o, gains, cos, sin, 0
    )
    returned = lax.ppermute(kv_back, ("seq", "shard"), [(j, i) for i, j in pairs])
    dq_hi, kv_b, kv_c, gq_hi = att_back(
        qs_hi, qraw_hi, kv_lo, kv_hi, pm_hi, p1_hi, d_o, gains, cos, sin, 1
    )
    grad_tokens, g_qkv, gain_in, gain_k = post(
        me,
        tokens,
        d_mid,
        (nin_lo, nin_hi),
        (dq_lo, dq_hi),
        (kv_a, kv_b, kv_c, returned),
        (kraw_lo, kraw_hi),
        gains,
        cos,
        sin,
        qkv,
    )
    gain_q = gq_lo[0] + gq_hi[0]
    parts = [gain_in[0], gain_mid[8], gain_mid[0], gain_out[0], gain_q, gain_k[0]]
    packed = jnp.concatenate([p.reshape(4, -1) for p in parts], axis=1).astype(BF16)
    packed = jnp.pad(packed[:, None], ((0, 0), (0, 15), (0, wide - packed.shape[1])))
    last = reduce_grad(jnp.concatenate([g_qkv.reshape(4, D // 4, wide), packed], axis=1))
    tail = last[gd]
    qd = HEADS * HEAD_DIM
    return (
        block_out,
        grad_tokens,
        last[:gd, :qd],
        last[:gd, qd : qd + HEAD_DIM],
        last[:gd, qd + HEAD_DIM :],
        r_out,
        r_gu[:, :FF],
        r_gu[:, FF:],
        r_down,
        tail[:gd],
        tail[4 * gd : 4 * gd + gh],
        tail[4 * gd + gh : 4 * gd + 2 * gh],
        tail[gd : 2 * gd],
        tail[2 * gd : 3 * gd],
        tail[3 * gd : 4 * gd],
    )


def solution(mesh):
    token = P(("seq", "shard"), None)
    matrix = P("shard", None)
    vector = P("shard")
    in_specs = (token,) + (matrix,) * 7 + (vector,) * 6 + (token,)
    out_specs = (token, token) + (matrix,) * 7 + (vector,) * 6
    return jax.shard_map(shards, mesh=mesh, in_specs=in_specs, out_specs=out_specs, check_vma=False)
```

```python
import jax
import jax.numpy as jnp
from jax import lax
from jax.experimental import pallas as pl
from jax.experimental.pallas import tpu as pltpu
from jax.sharding import PartitionSpec as P

D = 640
HEADS = 4
HEAD_DIM = 256
FF = 2048
WINDOW = 512
SEQ_CAP = 8192
HALF = 512
QB = 256
ROWS = HEADS * QB
CHUNK = 512

EPS = 1e-06
ROPE_BASE = 10000.0
LOG2E = 1.4426950408889634
LN2 = 0.6931471805599453
SCALE = HEAD_DIM**-0.5

F32 = jnp.float32
BF16 = jnp.bfloat16
VM = pl.BlockSpec(memory_space=pltpu.VMEM)
SM = pl.BlockSpec(memory_space=pltpu.SMEM)
HB = pl.BlockSpec(memory_space=pl.ANY)
NN = (((1,), (0,)), ((), ()))
NT = (((1,), (1,)), ((), ()))
TN = (((0,), (0,)), ((), ()))


def dot(a, b, dims=NN):
    return lax.dot_general(a, b, dims, preferred_element_type=F32)


def params():
    return pltpu.CompilerParams(vmem_limit_bytes=16 * 2**20)


def sds(shape, dtype=BF16):
    return jax.ShapeDtypeStruct(shape, dtype)


def cost(flops, nbytes):
    return pl.CostEstimate(flops=int(flops), bytes_accessed=int(nbytes), transcendentals=0)


def rms_factor(v):
    return lax.rsqrt(jnp.mean(v * v, axis=-1, keepdims=True) + EPS)


def norm_back(v, factor, gain, incoming):
    united = v * factor
    scaled = incoming * gain
    back = factor * (scaled - united * jnp.mean(scaled * united, axis=-1, keepdims=True))
    return back, jnp.sum(incoming * united, axis=0, keepdims=True)


def offsets(me, rows):
    return (
        me * rows,
        (me + 1 - 2 * (me % 2)) * rows,
        ((me + 2) % 4) * rows,
        (3 - me) * rows,
    )


def hbm(shape, dtype=BF16):
    return pltpu.HBM(shape, dtype)


ME, XBIT, FLAG, EVEN, YBIT, SECOND, HERE = range(7)


def whole(piece):
    return piece


def place_copies(me_ref, pieces, src_of, buf, rows, sems, first):
    me, b = me_ref[ME], me_ref[XBIT]
    spots = [(p, o, rows) for p, o in zip(pieces, offsets(me, rows))]
    if len(pieces) == 6:
        part = rows // 2
        far, last = spots[2][1], spots[3][1]
        spots = spots[:2]
        for base, p in ((far, pieces[2:4]), (last, pieces[4:6])):
            spots.append((p[0], base + b * part, part))
            spots.append((p[1], base + (1 - b) * part, part))
    copies = []
    for k, (piece, off, n) in enumerate(spots):
        copies.append(
            pltpu.make_async_copy(
                src_of(piece), buf.at[pl.ds(pl.multiple_of(off, 16), n)], sems.at[first + k]
            )
        )
    return copies


def pack_kernel(info, k, v, g0, g1, g2, g3, g4, g5, out):
    rows = D // 4
    out[:rows, :HEAD_DIM] = k[...]
    out[:rows, HEAD_DIM:] = v[...]
    out[rows:, :] = jnp.zeros((16, 2 * HEAD_DIM), BF16)
    for i, g in enumerate((g0, g1, g2, g3, g4, g5)):
        out[rows + i : rows + i + 1, : g.shape[0]] = g[...].reshape(1, -1)


def pack(info, k, v, *gains):
    return pl.pallas_call(
        pack_kernel,
        out_shape=sds((D // 4 + 16, 2 * HEAD_DIM)),
        in_specs=[SM] + [VM] * 8,
        out_specs=VM,
        compiler_params=params(),
        cost_estimate=cost(1e6, 4e5),
        name="pack",
    )(info, k, v, *gains)


def gains_kernel(me_ref, g0, g1, g2, g3, out):
    gd = D // 4
    gh = HEAD_DIM // 4
    wide = jnp.zeros((16, D), F32)
    small = jnp.zeros((16, HEAD_DIM), F32)
    spots = offsets(me_ref[ME], 1)
    for spot, g in zip(spots, (g0, g1, g2, g3)):
        piece = g[...]
        row = lax.broadcasted_iota(jnp.int32, (HEAD_DIM, D), 0)
        col = lax.broadcasted_iota(jnp.int32, (HEAD_DIM, D), 1)
        place = ((col == row + spot * gd) & (row < gd)).astype(BF16)
        wide = wide + dot(piece, place)
        row = lax.broadcasted_iota(jnp.int32, (HEAD_DIM, HEAD_DIM), 0)
        col = lax.broadcasted_iota(jnp.int32, (HEAD_DIM, HEAD_DIM), 1)
        place = ((col == row + spot * gh) & (row < gh)).astype(BF16)
        small = small + dot(piece, place)
    out[0:4, :] = wide[0:4, :]
    out[4:8, :] = jnp.zeros((4, D), F32)
    out[4:8, :HEAD_DIM] = small[4:8, :]


def gains_of(me, pieces):
    part = pl.BlockSpec((16, HEAD_DIM), lambda i: (D // 4 // 16, 0))
    return pl.pallas_call(
        gains_kernel,
        grid=(1,),
        out_shape=sds((8, D), F32),
        in_specs=[SM] + [part] * 4,
        out_specs=VM,
        compiler_params=params(),
        cost_estimate=cost(1e8, 1e5),
        name="gains",
    )(me, *pieces)


def rotated(u, cos, sin):
    hd = HEAD_DIM // 2
    u1 = u[:, :hd]
    u2 = u[:, hd:]
    return (u1 * cos - u2 * sin).astype(BF16), (u2 * cos + u1 * sin).astype(BF16)


def pre_kv_kernel(me_ref, tok, gains, cos_ref, sin_ref, w0, w1, w2, w3, nin_o, kraw_o, lo_o, hi_o, wbuf, sems):
    rows = D // 4
    copies = place_copies(
        me_ref, (w0, w1, w2, w3), lambda w: w.at[pl.ds(0, rows)], wbuf, rows, sems, 0
    )
    for c in copies:
        c.start()
    hd = HEAD_DIM // 2
    x = tok[...].astype(F32)
    nin = (x * rms_factor(x) * gains[0:1, :]).astype(BF16)
    nin_o[...] = nin
    for c in copies:
        c.wait()
    k = dot(nin, wbuf[:, :HEAD_DIM])
    kraw_o[...] = k.astype(BF16)
    r1, r2 = rotated(k * rms_factor(k) * gains[5:6, :HEAD_DIM], cos_ref[...], sin_ref[...])
    v = dot(nin, wbuf[:, HEAD_DIM:]).astype(BF16)
    for half, o in enumerate((lo_o, hi_o)):
        sl = slice(HALF * half, HALF * (half + 1))
        o[:, :hd] = r1[sl]
        o[:, hd:HEAD_DIM] = r2[sl]
        o[:, HEAD_DIM:] = v[sl]


def pre_kv(me, tok, gains, cos, sin, pieces):
    t = tok.shape[0]
    return pl.pallas_call(
        pre_kv_kernel,
        out_shape=(
            sds((t, D)),
            sds((t, HEAD_DIM)),
            sds((HALF, 2 * HEAD_DIM)),
            sds((HALF, 2 * HEAD_DIM)),
        ),
        in_specs=[SM, VM, VM, VM, VM, HB, HB, HB, HB],
        out_specs=(VM,) * 4,
        scratch_shapes=[pltpu.VMEM((D, 2 * HEAD_DIM), BF16), pltpu.SemaphoreType.DMA((4,))],
        compiler_params=params(),
        cost_estimate=cost(2 * t * D * 512, 5e6),
        name="pre_kv",
    )(me, tok, gains, cos, sin, *pieces)


def pre_q_kernel(me_ref, nin_i, gains, cos_ref, sin_ref, w0, w1, w2, w3, qraw_o, qs_o, wbuf, sems):
    rows = D // 4
    hd = HEAD_DIM // 2

    @pl.when(pl.program_id(0) == 0)
    def _():
        copies = place_copies(
            me_ref, (w0, w1, w2, w3), lambda w: w.at[pl.ds(0, rows)], wbuf, rows, sems, 0
        )
        for c in copies:
            c.start()
        for c in copies:
            c.wait()

    q = dot(nin_i[...], wbuf[:, pl.ds(pl.multiple_of(pl.program_id(0) * HEAD_DIM, HEAD_DIM), HEAD_DIM)])
    qraw_o[0] = q.astype(BF16)
    u = q * (rms_factor(q) * (SCALE * LOG2E)) * gains[4:5, :HEAD_DIM]
    r1, r2 = rotated(u, cos_ref[...], sin_ref[...])
    qs_o[0, :, :hd] = r1
    qs_o[0, :, hd:] = r2


def pre_q(me, nin, gains, cos, sin, pieces):
    t = nin.shape[0]
    head = pl.BlockSpec((1, t, HEAD_DIM), lambda h: (h, 0, 0))
    return pl.pallas_call(
        pre_q_kernel,
        grid=(HEADS,),
        out_shape=(hbm((HEADS, t, HEAD_DIM)), sds((HEADS, t, HEAD_DIM))),
        in_specs=[SM, VM, VM, VM, VM, HB, HB, HB, HB],
        out_specs=(head, head),
        scratch_shapes=[pltpu.VMEM((D, HEADS * HEAD_DIM), BF16), pltpu.SemaphoreType.DMA((4,))],
        compiler_params=params(),
        cost_estimate=cost(2 * t * D * 1024, 5e6),
        name="pre_q",
    )(me, nin, gains, cos, sin, *pieces)


def key_blocks(j, kvp, kvs, lo, hi):
    blocks = (kvp[0:QB, lo:hi], kvp[QB : 2 * QB, lo:hi], kvs[0:QB, lo:hi], kvs[QB : 2 * QB, lo:hi])
    return blocks[j : j + 3]


def upper_mask():
    row = lax.broadcasted_iota(jnp.int32, (HEADS, QB, QB), 1).reshape(ROWS, QB)
    col = lax.broadcasted_iota(jnp.int32, (ROWS, QB), 1)
    return col > row


def att_kernel(masked, flag_ref, qs, kvp, kvs, o_o, pm_o, p1_o):
    upper = upper_mask()
    for j in range(2):
        sl = slice(QB * j, QB * (j + 1))
        q = qs[:, sl, :].reshape(ROWS, HEAD_DIM)
        k0, k1, k2 = key_blocks(j, kvp, kvs, 0, HEAD_DIM)
        v0, v1, v2 = key_blocks(j, kvp, kvs, HEAD_DIM, 2 * HEAD_DIM)
        em = jnp.exp2(jnp.where(upper, dot(q, k0, NT), dot(q, k2, NT)))
        e1 = jnp.exp2(dot(q, k1, NT))
        if masked:
            keep = flag_ref[FLAG].astype(F32)
            em = em * jnp.where(upper, keep, 1.0)
            if j == 0:
                e1 = e1 * keep
        inv = 1.0 / jnp.sum(em + e1, axis=-1, keepdims=True)
        pm = (em * inv).astype(BF16)
        p1 = (e1 * inv).astype(BF16)
        zero = jnp.zeros_like(pm)
        out = dot(p1, v1) + dot(jnp.where(upper, pm, zero), v0) + dot(jnp.where(upper, zero, pm), v2)
        pm_o[:, sl, :] = pm.reshape(HEADS, QB, QB)
        p1_o[:, sl, :] = p1.reshape(HEADS, QB, QB)
        o_o[:, sl, :] = out.astype(BF16).reshape(HEADS, QB, HEAD_DIM)


def half_spec(half):
    return pl.BlockSpec((HEADS, HALF, HEAD_DIM), lambda i: (0, half, 0))


def att(flag, qs, kvp, kvs, masked, half):
    shp = sds((HEADS, HALF, HEAD_DIM))

    def body(*refs):
        att_kernel(masked, *refs)

    return pl.pallas_call(
        body,
        grid=(1,),
        out_shape=(shp, shp, shp),
        in_specs=[SM, half_spec(half), VM, VM],
        out_specs=(VM,) * 3,
        compiler_params=params(),
        cost_estimate=cost(12e9 / 4, 5e6),
        name="att",
    )(flag, qs, kvp, kvs)


def att_back_kernel(qs, qraw, kvp, kvs, pm_i, p1_i, do_i, gains, cos_ref, sin_ref, dq_o, dkvp_o, dkvs_o, gain_o, acc):
    upper = upper_mask()
    hd = HEAD_DIM // 2
    acc[...] = jnp.zeros_like(acc)
    gsum = jnp.zeros((1, HEAD_DIM), F32)
    for j in range(2):
        sl = slice(QB * j, QB * (j + 1))
        q = qs[:, sl, :].reshape(ROWS, HEAD_DIM)
        do = do_i[:, sl, :].reshape(ROWS, HEAD_DIM)
        k0, k1, k2 = key_blocks(j, kvp, kvs, 0, HEAD_DIM)
        v0, v1, v2 = key_blocks(j, kvp, kvs, HEAD_DIM, 2 * HEAD_DIM)
        pmb = pm_i[:, sl, :].reshape(ROWS, QB)
        p1b = p1_i[:, sl, :].reshape(ROWS, QB)
        dpm = jnp.where(upper, dot(do, v0, NT), dot(do, v2, NT))
        dp1 = dot(do, v1, NT)
        pm = pmb.astype(F32)
        p1 = p1b.astype(F32)
        total = jnp.sum(pm * dpm + p1 * dp1, axis=-1, keepdims=True)
        dsm = (pm * (dpm - total)).astype(BF16)
        ds1 = (p1 * (dp1 - total)).astype(BF16)
        zero = jnp.zeros_like(dsm)
        ds0 = jnp.where(upper, dsm, zero)
        ds2 = jnp.where(upper, zero, dsm)
        p0 = jnp.where(upper, pmb, zero)
        p2 = jnp.where(upper, zero, pmb)
        for t, (ds, p) in enumerate(((ds0, p0), (ds1, p1b), (ds2, p2))):
            at = slice(QB * (j + t), QB * (j + t + 1))
            acc[at, :HEAD_DIM] += dot(ds, q, TN) * LN2
            acc[at, HEAD_DIM:] += dot(p, do, TN)
        dq = (dot(ds0, k0) + dot(ds1, k1) + dot(ds2, k2)) * SCALE
        cos = cos_ref[sl, :]
        sin = sin_ref[sl, :]
        gain = gains[4:5, :HEAD_DIM]
        for h in range(HEADS):
            d1 = dq[QB * h : QB * (h + 1), :hd]
            d2 = dq[QB * h : QB * (h + 1), hd:]
            inc = jnp.concatenate([d1 * cos + d2 * sin, d2 * cos - d1 * sin], axis=-1)
            raw = qraw[h, sl, :].astype(F32)
            back, terms = norm_back(raw, rms_factor(raw), gain, inc)
            gsum = gsum + terms
            dq_o[sl, HEAD_DIM * h : HEAD_DIM * (h + 1)] = back.astype(BF16)
    dkvp_o[...] = acc[:HALF, :].astype(BF16)
    dkvs_o[...] = acc[HALF:, :]
    gain_o[...] = jnp.broadcast_to(gsum, (8, HEAD_DIM))


def att_back(qs, qraw, kvp, kvs, pm, p1, do, gains, cos, sin, half):
    dospec = half_spec(half)
    tab = pl.BlockSpec((HALF, HEAD_DIM // 2), lambda i: (half, 0))
    return pl.pallas_call(
        att_back_kernel,
        grid=(1,),
        out_shape=(
            sds((HALF, HEADS * HEAD_DIM)),
            sds((HALF, 2 * HEAD_DIM)),
            sds((HALF, 2 * HEAD_DIM), F32),
            sds((8, HEAD_DIM), F32),
        ),
        in_specs=[dospec, dospec, VM, VM, VM, VM, dospec, VM, tab, tab],
        out_specs=(VM,) * 4,
        scratch_shapes=[pltpu.VMEM((2 * HALF, 2 * HEAD_DIM), F32)],
        compiler_params=params(),
        cost_estimate=cost(24e9 / 4, 9e6),
        name="att_back",
    )(qs, qraw, kvp, kvs, pm, p1, do, gains, cos, sin)


def mid_kernel(me_ref, o_lo, o_hi, tok, gains, w0, w1, w2, w3, ap_o, nm_o, wo, sems):
    ro = HEADS * HEAD_DIM // 4
    copies = place_copies(me_ref, (w0, w1, w2, w3), lambda w: w, wo, ro, sems, 0)
    for c in copies:
        c.start()
    for c in copies:
        c.wait()
    for half, o in enumerate((o_lo, o_hi)):
        sl = slice(HALF * half, HALF * (half + 1))
        proj = dot(o[0], wo[0:HEAD_DIM, :])
        for h in range(1, HEADS):
            proj = proj + dot(o[h], wo[HEAD_DIM * h : HEAD_DIM * (h + 1), :])
        ap_o[sl, :] = proj.astype(BF16)
        mid = tok[sl, :].astype(F32) + proj * rms_factor(proj) * gains[1:2, :]
        nm_o[sl, :] = (mid * rms_factor(mid) * gains[2:3, :]).astype(BF16)


def mid_part(me, o_lo, o_hi, tok, gains, outs):
    t = tok.shape[0]
    return pl.pallas_call(
        mid_kernel,
        out_shape=(sds((t, D)), sds((t, D))),
        in_specs=[SM] + [VM] * 4 + [HB] * 4,
        out_specs=(VM, VM),
        scratch_shapes=[
            pltpu.VMEM((HEADS * HEAD_DIM, D), BF16),
            pltpu.SemaphoreType.DMA((4,)),
        ],
        compiler_params=params(),
        cost_estimate=cost(2 * t * D * 1024, 8e6),
        name="mid",
    )(me, o_lo, o_hi, tok, gains, *outs)


FH = FF // 2
STEP = 256


def gate_kernel(me_ref, nm, *rest):
    pieces, (a_o, s_o, wg, sems) = rest[:6], rest[6:]

    @pl.when(pl.program_id(0) == 0)
    def _():
        copies = place_copies(me_ref, pieces, whole, wg, D // 4, sems, 0)
        for c in copies:
            c.start()
        for c in copies:
            c.wait()

    cs = pl.ds(pl.multiple_of(pl.program_id(0) * STEP, STEP), STEP)
    g = dot(nm[...], wg[:, cs])
    c0 = 0.7978845608028654
    c1 = 0.044715 * c0
    g2 = g * g
    t = jnp.tanh(g * (c0 + c1 * g2))
    h = 0.5 + 0.5 * t
    a = g * h
    slope = h + a * (1.0 - h) * (2.0 * c0 + (6.0 * c1) * g2)
    a_o[...] = a.astype(BF16)
    s_o[...] = slope.astype(BF16)


def up_kernel(me_ref, nm, a_i, s_i, *rest):
    pieces, (hid_o, b_o, wu, sems) = rest[:6], rest[6:]

    @pl.when(pl.program_id(0) == 0)
    def _():
        copies = place_copies(me_ref, pieces, whole, wu, D // 4, sems, 0)
        for c in copies:
            c.start()
        for c in copies:
            c.wait()

    cs = pl.ds(pl.multiple_of(pl.program_id(0) * STEP, STEP), STEP)
    u = dot(nm[...], wu[:, cs])
    hid_o[...] = (a_i[...].astype(F32) * u).astype(BF16)
    b_o[...] = (u * s_i[...].astype(F32)).astype(BF16)


def ff(me, nm, pieces, before=()):
    t = nm.shape[0]
    col = pl.BlockSpec((t, STEP), lambda i: (0, i))
    return pl.pallas_call(
        up_kernel if before else gate_kernel,
        grid=(FF // STEP,),
        out_shape=(sds((t, FF)),) * 2,
        in_specs=[SM, VM] + [col] * len(before) + [HB] * 6,
        out_specs=(col,) * 2,
        scratch_shapes=[pltpu.VMEM((D, FF), BF16), pltpu.SemaphoreType.DMA((6,))],
        compiler_params=params(),
        cost_estimate=cost(2 * t * D * FF, 12e6),
        name="up" if before else "gate",
    )(me, nm, *before, *pieces)


def down_kernel(me_ref, hid, tok, cot, ap, gains, *rest):
    pieces, (out_o, dd_o, wd_o, keep_o, send_o, gain_o, sems) = rest[:6], rest[6:]
    rf = FF // 4
    core = me_ref[ME] % 2
    copies = place_copies(me_ref, pieces, whole, wd_o, rf, sems, 0)
    for c in copies:
        c.start()
    for c in copies:
        c.wait()
    gsum = jnp.zeros((1, D), F32)
    for half in range(2):
        sl = slice(HALF * half, HALF * (half + 1))
        dn = dot(hid[sl, :], wd_o[...])
        proj = ap[sl, :].astype(F32)
        mid = tok[sl, :].astype(F32) + proj * rms_factor(proj) * gains[1:2, :]
        fac = rms_factor(dn)
        out_o[sl, :] = (mid + dn * fac * gains[3:4, :]).astype(BF16)
        back, terms = norm_back(dn, fac, gains[3:4, :], cot[sl, :].astype(F32))
        dd_o[sl, :] = back.astype(BF16)
        gsum = gsum + terms
    gain_o[...] = jnp.broadcast_to(gsum, (8, D))
    for y in range(2):
        for part, o in ((core, keep_o), (1 - core, send_o)):
            at = pl.ds(pl.multiple_of((2 * y + part) * rf, rf), rf)
            g = dot(hid[:, at], dd_o[...], TN).astype(BF16)
            for j in range(D // 128):
                o[y, j] = g[:, 128 * j : 128 * (j + 1)]


def down_part(me, hid, tok, cot, ap, gains, pieces):
    t = tok.shape[0]
    return pl.pallas_call(
        down_kernel,
        out_shape=(
            sds((t, D)),
            sds((t, D)),
            sds((FF, D)),
            sds((2, D // 128, FF // 4, 128)),
            sds((2, D // 128, FF // 4, 128)),
            sds((8, D), F32),
        ),
        in_specs=[SM] + [VM] * 5 + [HB] * 6,
        out_specs=(VM,) * 6,
        scratch_shapes=[pltpu.SemaphoreType.DMA((6,))],
        compiler_params=params(),
        cost_estimate=cost(4 * t * D * FF, 20e6),
        name="down",
    )(me, hid, tok, cot, ap, gains, *pieces)


def fb_kernel(half, me_ref, nm, dd, a_i, b_i, wd, *rest):
    gates, ups, rest = rest[:6], rest[6:12], rest[12:]
    first = half == 0
    if first:
        keep_o, send_o, dnm_o, wg, wu, gs, sems = rest
    else:
        dnm_i, keep_o, send_o, dnm_o, wg, wu, gs, sems = rest
    core = me_ref[ME] % 2

    @pl.when(pl.program_id(0) == 0)
    def _():
        copies = []
        for k, (pieces, buf) in enumerate(((gates, wg), (ups, wu))):
            copies += place_copies(
                me_ref, pieces, lambda w: w.at[:, pl.ds(FH * half, FH)], buf, D // 4, sems, 6 * k
            )
        for c in copies:
            c.start()
        for c in copies:
            c.wait()
        if first:
            dnm_o[...] = jnp.zeros_like(dnm_o)
        else:
            dnm_o[...] = dnm_i[...]

    cs = pl.ds(pl.multiple_of(pl.program_id(0) * STEP, STEP), STEP)
    dh = dot(dd[...], wd[...], NT)
    dg = (dh * b_i[...].astype(F32)).astype(BF16)
    du = (dh * a_i[...].astype(F32)).astype(BF16)
    dnm_o[...] += dot(dg, wg[:, cs], NT) + dot(du, wu[:, cs], NT)
    gr = D // 4
    for k, d in enumerate((dg, du)):
        gs[k] = dot(nm[...], d, TN).astype(BF16)
        for y in range(2):
            for part, o in ((core, keep_o), (1 - core, send_o)):
                at = pl.ds(pl.multiple_of((2 * y + part) * gr, gr), gr)
                for j in range(STEP // 128):
                    o[y, k, j] = gs[k, at, 128 * j : 128 * (j + 1)]


def fb(me, nm, dd, a, b, wd, gates, ups, part, dnm):
    t = nm.shape[0]
    steps = FH // STEP
    col = pl.BlockSpec((t, STEP), lambda i: (0, i + steps * part))
    extra = () if dnm is None else (dnm,)

    def body(*refs):
        fb_kernel(part, *refs)

    return pl.pallas_call(
        body,
        grid=(steps,),
        out_shape=(sds((2, 2, FH // 128, D // 4, 128)),) * 2 + (sds((t, D), F32),),
        in_specs=[SM, VM, VM, col, col, pl.BlockSpec((STEP, D), lambda i: (i + steps * part, 0))]
        + [HB] * 12
        + [VM] * len(extra),
        out_specs=(pl.BlockSpec((2, 2, STEP // 128, D // 4, 128), lambda i: (0, 0, i, 0, 0)),) * 2
        + (VM,),
        scratch_shapes=[
            pltpu.VMEM((D, FH), BF16),
            pltpu.VMEM((D, FH), BF16),
            pltpu.VMEM((2, D, STEP), BF16),
            pltpu.SemaphoreType.DMA((12,)),
        ],
        compiler_params=params(),
        cost_estimate=cost(10 * t * D * FH, 16e6),
        name="fb",
    )(me, nm, dd, a, b, wd, *gates, *ups, *extra)


def fe_kernel(me_ref, o_lo, o_hi, tok, cot, gains, ap, dnm, w0, w1, w2, w3, keep_o, send_o, do_o, dmid_o, gain_o, wo, datt, sems):
    ro = HEADS * HEAD_DIM // 4
    copies = place_copies(me_ref, (w0, w1, w2, w3), lambda w: w, wo, ro, sems, 0)
    for c in copies:
        c.start()
    gm = jnp.zeros((1, D), F32)
    ga = jnp.zeros((1, D), F32)
    for half in range(2):
        sl = slice(HALF * half, HALF * (half + 1))
        proj = ap[sl, :].astype(F32)
        pfac = rms_factor(proj)
        mid = tok[sl, :].astype(F32) + proj * pfac * gains[1:2, :]
        back, terms = norm_back(mid, rms_factor(mid), gains[2:3, :], dnm[sl, :])
        dmid = cot[sl, :].astype(F32) + back
        gm = gm + terms
        dmid_o[sl, :] = dmid.astype(BF16)
        back, terms = norm_back(proj, pfac, gains[1:2, :], dmid)
        ga = ga + terms
        datt[sl, :] = back.astype(BF16)
    gain_o[0:8, :] = jnp.broadcast_to(gm, (8, D))
    gain_o[8:16, :] = jnp.broadcast_to(ga, (8, D))
    for c in copies:
        c.wait()
    for h in range(HEADS):
        at = slice(HEAD_DIM * h, HEAD_DIM * (h + 1))
        do_o[h] = dot(datt[...], wo[at, :], NT).astype(BF16)
    core = me_ref[ME] % 2
    for y in range(2):
        for part, o in ((core, keep_o), (1 - core, send_o)):
            h = 2 * y + part
            g = (dot(o_lo[h], datt[:HALF, :], TN) + dot(o_hi[h], datt[HALF:, :], TN)).astype(BF16)
            for j in range(D // 128):
                o[y, j] = g[:, 128 * j : 128 * (j + 1)]


def fe(me, o_lo, o_hi, tok, cot, gains, ap, dnm, outs):
    t = tok.shape[0]
    return pl.pallas_call(
        fe_kernel,
        out_shape=(
            sds((2, D // 128, HEAD_DIM, 128)),
            sds((2, D // 128, HEAD_DIM, 128)),
            sds((HEADS, t, HEAD_DIM)),
            sds((t, D)),
            sds((16, D), F32),
        ),
        in_specs=[SM] + [VM] * 7 + [HB] * 4,
        out_specs=(VM,) * 5,
        scratch_shapes=[
            pltpu.VMEM((HEADS * HEAD_DIM, D), BF16),
            pltpu.VMEM((t, D), BF16),
            pltpu.SemaphoreType.DMA((4,)),
        ],
        compiler_params=params(),
        cost_estimate=cost(4 * t * D * 1024, 14e6),
        name="fe",
    )(me, o_lo, o_hi, tok, cot, gains, ap, dnm, *outs)


LAST = 2048


def post_kernel(
    me_ref, tok, dmid, nin, dq_lo, dq_hi, kv_a, kv_b, kv_c, kv_d, kraw,
    gains, cos_ref, sin_ref, gq_lo, gq_hi, gmid, gdown,
    q0, q1, q2, q3, k0, k1, k2, k3,
    gt_o, keep_o, send_o,
    wq, wkv, dkv, gs, sums, small, sems,
):
    rows = D // 4
    copies = place_copies(me_ref, (q0, q1, q2, q3), lambda w: w, wq, rows, sems, 0)
    copies += place_copies(
        me_ref, (k0, k1, k2, k3), lambda w: w.at[pl.ds(0, rows)], wkv, rows, sems, 4
    )
    for c in copies:
        c.start()
    hd = HEAD_DIM // 2
    gk = jnp.zeros((1, HEAD_DIM), F32)
    for half, (first, second) in enumerate(((kv_a, kv_b), (kv_c, kv_d))):
        sl = slice(HALF * half, HALF * (half + 1))
        both = first[...].astype(F32) + second[...].astype(F32)
        cos = cos_ref[sl, :]
        sin = sin_ref[sl, :]
        d1 = both[:, :hd]
        d2 = both[:, hd:HEAD_DIM]
        inc = jnp.concatenate([d1 * cos + d2 * sin, d2 * cos - d1 * sin], axis=-1)
        raw = kraw[sl, :].astype(F32)
        back, terms = norm_back(raw, rms_factor(raw), gains[5:6, :HEAD_DIM], inc)
        gk = gk + terms
        dkv[sl, :HEAD_DIM] = back.astype(BF16)
        dkv[sl, HEAD_DIM:] = both[:, HEAD_DIM:].astype(BF16)

    core = me_ref[ME] % 2

    def put(slot, g):
        gs[slot] = g.astype(BF16)
        for y in range(2):
            for part, o in ((core, keep_o), (1 - core, send_o)):
                at = pl.ds(pl.multiple_of((2 * y + part) * rows, rows), rows)
                for j in range(2):
                    to = (2 * slot + j) * rows
                    o[y, to : to + rows, :] = gs[slot, at, 128 * j : 128 * (j + 1)]

    for h in range(HEADS):
        cs = slice(HEAD_DIM * h, HEAD_DIM * (h + 1))
        put(h, dot(nin[:HALF, :], dq_lo[:, cs], TN) + dot(nin[HALF:, :], dq_hi[:, cs], TN))
    put(HEADS, dot(nin[...], dkv[:, :HEAD_DIM], TN))
    put(HEADS + 1, dot(nin[...], dkv[:, HEAD_DIM:], TN))
    for c in copies:
        c.wait()
    gi = jnp.zeros((1, D), F32)
    for half, dq in enumerate((dq_lo, dq_hi)):
        sl = slice(HALF * half, HALF * (half + 1))
        dnin = dot(dq[...], wq[...], NT) + dot(dkv[sl, :], wkv[...], NT)
        x = tok[sl, :].astype(F32)
        back, terms = norm_back(x, rms_factor(x), gains[0:1, :], dnin)
        gi = gi + terms
        gt_o[sl, :] = (dmid[sl, :].astype(F32) + back).astype(BF16)
    sums[...] = jnp.zeros_like(sums)
    small[...] = jnp.zeros_like(small)
    sums[0:1, :] = gi
    sums[1:2, :] = gmid[8:9, :]
    sums[2:3, :] = gmid[0:1, :]
    sums[3:4, :] = gdown[0:1, :]
    small[4:5, :] = gq_lo[0:1, :] + gq_hi[0:1, :]
    small[5:6, :] = gk
    gd = D // 4
    gh = HEAD_DIM // 4
    base = 12 * rows
    for y in range(2):
        for part, o in ((core, keep_o), (1 - core, send_o)):
            s = 2 * y + part
            row = lax.broadcasted_iota(jnp.int32, (D, HEAD_DIM), 0)
            col = lax.broadcasted_iota(jnp.int32, (D, HEAD_DIM), 1)
            place = ((row == col + s * gd) & (col < gd)).astype(BF16)
            g = dot(sums[...].astype(BF16), place)
            row = lax.broadcasted_iota(jnp.int32, (HEAD_DIM, HEAD_DIM), 0)
            col = lax.broadcasted_iota(jnp.int32, (HEAD_DIM, HEAD_DIM), 1)
            place = ((row == col + s * gh) & (col < gh)).astype(BF16)
            g = (g + dot(small[...].astype(BF16), place)).astype(BF16)
            o[y, base : base + 16, :] = g[:, :128]
            o[y, base + 16 : base + 32, :] = g[:, 128:]
            o[y, base + 32 :, :] = jnp.zeros((LAST - base - 32, 128), BF16)


def post(me, tok, dmid, nin, dqs, kvs, kraw, gains, cos, sin, sums, qs, kvgs):
    t = tok.shape[0]
    return pl.pallas_call(
        post_kernel,
        out_shape=(
            sds((t, D)),
            sds((2, LAST, 128)),
            sds((2, LAST, 128)),
        ),
        in_specs=[SM] + [VM] * 17 + [HB] * 8,
        out_specs=(VM,) * 3,
        scratch_shapes=[
            pltpu.VMEM((D, HEADS * HEAD_DIM), BF16),
            pltpu.VMEM((D, 2 * HEAD_DIM), BF16),
            pltpu.VMEM((t, 2 * HEAD_DIM), BF16),
            pltpu.VMEM((HEADS + 2, D, HEAD_DIM), BF16),
            pltpu.VMEM((16, D), F32),
            pltpu.VMEM((16, HEAD_DIM), F32),
            pltpu.SemaphoreType.DMA((8,)),
        ],
        compiler_params=params(),
        cost_estimate=cost(4e9, 15e6),
        name="post",
    )(me, tok, dmid, nin, *dqs, *kvs, kraw, gains, cos, sin, *sums, *qs, *kvgs)


def flip(x, axis, bit):
    n = lax.axis_size(axis)
    return lax.ppermute(x, axis, [(i, i ^ bit) for i in range(n)])


def pick(x, index, axis=0):
    return lax.dynamic_index_in_dim(x, index, axis, keepdims=False)


def after(x, *first):
    return lax.optimization_barrier((x,) + first)[0]


def joined(a, b):
    return (a.astype(F32) + b.astype(F32)).astype(BF16)


def small_call(body, name, out_rows, scalars, *arrays, scratch=()):
    size = sum(a.size for a in arrays)
    return pl.pallas_call(
        body,
        out_shape=tuple(sds(r + (128,)) for r in out_rows),
        in_specs=[SM] + [VM] * len(arrays),
        out_specs=(VM,) * len(out_rows),
        scratch_shapes=scratch,
        compiler_params=params(),
        cost_estimate=cost(size, 4 * size),
        name=name,
    )(scalars, *arrays)


def mix_first(scalars, keeps, gots):
    n = len(keeps)
    sizes = [k.shape[1] for k in keeps]
    rows = sum(sizes)

    def body(s, *refs):
        ks, gs = refs[:n], refs[n : 2 * n]
        send, keep, total = refs[2 * n :]
        at = 0
        for k, g, size in zip(ks, gs, sizes):
            for y in range(2):
                total[y, at : at + size, :] = joined(k[y], g[y])
            at += size
        even, y, x = s[EVEN], s[YBIT], s[XBIT]
        for t in range(2):
            for o, flip_it in ((send, 1), (keep, 0)):
                own_y = flip_it + y - 2 * flip_it * y
                own_x = flip_it + x - 2 * flip_it * x
                row = even * own_y + (1 - even) * t
                half = even * t + (1 - even) * own_x
                o[t] = total[row, pl.ds(pl.multiple_of(half * (rows // 2), 16), rows // 2), :]

    shape = (2, rows // 2)
    return small_call(
        body, "mix_first", (shape, shape), scalars, *keeps, *gots,
        scratch=[pltpu.VMEM((2, rows, 128), BF16)],
    )


def mix_half(info, index, keep, got):
    keep = keep.reshape(2, -1, 128)
    got = got.reshape(2, -1, 128)

    def body(i, k, g, send, kept):
        own = i[index]
        send[...] = joined(k[1 - own], g[1 - own])
        kept[...] = joined(k[own], g[own])

    shape = (keep.shape[1],)
    return small_call(body, "mix_half", (shape, shape), info, keep, got)


def mix_sum(info, keep, got):
    def body(i, k, g, o):
        o[...] = joined(k[...], g[...])

    return small_call(body, "mix_sum", (keep.shape[:1],), info, keep, got)[0]


def mix_both(info, index, own, other):
    rows = own.shape[0]

    def body(i, a, b, o):
        o[i[index]] = a[...]
        o[1 - i[index]] = b[...]

    return small_call(body, "mix_both", ((2, rows),), info, own, other)[0].reshape(2 * rows, 128)


class Place:
    def __init__(self, first_pos):
        shard = lax.axis_index("shard")
        seq = lax.axis_index("seq")
        self.n_shard = lax.axis_size("shard")
        self.n = lax.axis_size("seq") * self.n_shard
        core = shard & 1
        y = shard >> 1
        x = seq & 1
        bits = []
        bit = 1
        while bit < lax.axis_size("seq"):
            bits.append(bit)
            bit *= 2
        self.far = [self.n_shard * b for b in bits]
        here = [(seq >> i) & 1 for i in range(len(bits))]
        flag = (first_pos > 0).astype(jnp.int32)
        second = jnp.where(core == 0, x, y)
        self.token = None
        self.info = jnp.stack([shard, x, flag, 1 - core, y, second] + here).astype(jnp.int32)

    def send(self, x, even, odd):
        pairs = [(i, i ^ (even if i % 2 == 0 else odd)) for i in range(self.n)]
        return lax.ppermute(x, ("seq", "shard"), pairs)


ORDER = ("d", "da", "da", "dab", "da", "dabcabcbcbcbc")


class Chain:
    def __init__(self, place):
        self.place = place
        self.keeps = []
        self.gots = []
        self.keep = None
        n = len(place.far)
        self.steps = [self.start, self.second]
        self.steps += [lambda i=i: self.halve(i) for i in range(1, n - 1)]
        self.steps += [self.exchange]
        self.steps += [lambda i=i: self.double(i) for i in range(n - 2, -1, -1)]
        self.count = len(self.steps)

    def add(self, keep, send):
        self.keeps.append(keep.reshape(2, -1, 128))
        self.gots.append(self.place.send(send.reshape(2, -1, 128), 1, 1))

    def wait(self, *first):
        if not first:
            return
        if len(self.steps) == self.count:
            self.gots = [after(g, *first) for g in self.gots]
        else:
            self.got = after(self.got, *first)

    def step(self):
        if self.keep is None:
            self.keeps[0] = self.turn(self.keeps[0])
        else:
            self.keep = self.turn(self.keep)
        return self.steps.pop(0)()

    def go(self, out, even, odd):
        self.got = self.place.send(out, even, odd)
        self.place.token = out

    def turn(self, x):
        return x if self.place.token is None else after(x, self.place.token)

    def start(self):
        out, self.keep = mix_first(self.place.info, self.keeps, self.gots)
        self.go(out, 2, self.place.far[0])
        return out

    def second(self):
        out, self.keep = mix_half(self.place.info, SECOND, self.keep, self.got)
        self.go(out, self.place.far[0], 2)
        return out

    def halve(self, i):
        keep, got = self.keep, self.got
        out, self.keep = mix_half(self.place.info, HERE + i, keep, got)
        self.go(out, self.place.far[i], self.place.far[i])
        return out

    def exchange(self):
        self.keep = mix_sum(self.place.info, self.keep, self.got)
        self.go(self.keep, self.place.far[-1], self.place.far[-1])
        return self.keep

    def double(self, i):
        if i == len(self.place.far) - 2:
            self.keep = mix_sum(self.place.info, self.keep, self.got)
        else:
            self.keep = mix_both(self.place.info, HERE + i + 1, self.keep, self.got)
        self.go(self.keep, self.place.far[i], self.place.far[i])
        return self.keep


def gather_halves(info, own, other, total):
    total[info[HERE]] = own[...]
    total[1 - info[HERE]] = other[...]


def spread(o, total, at, rows, blocks):
    half = total.shape[1]
    for j in range(blocks):
        done = 0
        while done < rows:
            part, row = divmod(at + j * rows + done, half)
            n = min(rows - done, half - row)
            o[done : done + n, 128 * j : 128 * (j + 1)] = total[part, row : row + n, :].astype(o.dtype)
            done += n


def finish_one(info, own, other):
    def body(i, a, b, down, total):
        gather_halves(i, a, b, total)
        spread(down, total, 0, FF // 4, D // 128)

    return pl.pallas_call(
        body,
        out_shape=hbm((FF // 4, D), F32),
        in_specs=[SM, VM, VM],
        out_specs=VM,
        scratch_shapes=[pltpu.VMEM((2,) + own.shape, BF16)],
        compiler_params=params(),
        cost_estimate=cost(1e7, 1e7),
        name="finish_one",
    )(info, own, other)


def finish_two(info, own_a, other_a, own_b, other_b):
    gr = D // 4
    blocks = FH // 128

    def body(i, a, oa, b, ob, gate, up, out, total_a, total_b):
        gather_halves(i, a, oa, total_a)
        gather_halves(i, b, ob, total_b)
        for k, total in enumerate((total_a, total_b)):
            spread(gate.at[:, pl.ds(FH * k, FH)], total, 0, gr, blocks)
            spread(up.at[:, pl.ds(FH * k, FH)], total, gr * blocks, gr, blocks)
        spread(out, total_b, 2 * gr * blocks, HEAD_DIM, D // 128)

    return pl.pallas_call(
        body,
        out_shape=(hbm((gr, FF), F32), hbm((gr, FF), F32), hbm((HEAD_DIM, D), F32)),
        in_specs=[SM] + [VM] * 4,
        out_specs=(VM,) * 3,
        scratch_shapes=[
            pltpu.VMEM((2,) + own_a.shape, BF16),
            pltpu.VMEM((2,) + own_b.shape, BF16),
        ],
        compiler_params=params(),
        cost_estimate=cost(1e7, 1e7),
        name="finish_two",
    )(info, own_a, other_a, own_b, other_b)


def finish_three(info, own, other):
    gr = D // 4

    def body(i, a, b, query, key, value, gains, total):
        gather_halves(i, a, b, total)
        spread(query, total, 0, gr, 8)
        spread(key, total, 8 * gr, gr, 2)
        spread(value, total, 10 * gr, gr, 2)
        spread(gains, total, 12 * gr, 16, 2)

    return pl.pallas_call(
        body,
        out_shape=(
            hbm((gr, HEADS * HEAD_DIM), F32),
            hbm((gr, HEAD_DIM), F32),
            hbm((gr, HEAD_DIM), F32),
            sds((16, HEAD_DIM), F32),
        ),
        in_specs=[SM, VM, VM],
        out_specs=(VM,) * 4,
        scratch_shapes=[pltpu.VMEM((2,) + own.shape, BF16)],
        compiler_params=params(),
        cost_estimate=cost(1e7, 1e7),
        name="finish_three",
    )(info, own, other)


def shards(
    tokens,
    query_weight,
    key_weight,
    value_weight,
    out_weight,
    gate_weight,
    up_weight,
    down_weight,
    input_gain,
    query_gain,
    key_gain,
    attended_gain,
    middle_gain,
    output_gain,
    cotangent,
):
    n_seq = lax.axis_size("seq")
    n_shard = lax.axis_size("shard")
    shard = lax.axis_index("shard")
    x_bit = lax.axis_index("seq") & 1
    count = tokens.shape[0]
    total = count * n_seq * n_shard
    length = min(SEQ_CAP, total)
    rank = lax.axis_index("seq") * n_shard + shard
    first_pos = rank * count % length
    place = Place(first_pos)
    me = flag = place.info
    gd = D // 4
    gh = HEAD_DIM // 4

    kvg = pack(
        me,
        key_weight,
        value_weight,
        input_gain,
        attended_gain,
        middle_gain,
        output_gain,
        query_gain,
        key_gain,
    )
    def near(x):
        return flip(x, "shard", 1)

    def far(x):
        return flip(x, "shard", 2)

    q_far = far(query_weight)
    kvg_far = far(kvg)
    kvgs = (kvg, near(kvg), kvg_far, near(kvg_far))
    q_near = near(query_weight)
    out_near, gate_near, up_near, down_near = (
        near(out_weight), near(gate_weight), near(up_weight), near(down_weight)
    )

    def half(w):
        return pick(w.reshape(2, w.shape[0] // 2, w.shape[1]), x_bit)

    def relay(x):
        return flip(x, "seq", 1)

    gate_half, up_half, down_half = half(gate_weight), half(up_weight), half(down_weight)

    positions = first_pos + jnp.arange(count, dtype=jnp.int32)
    hd = HEAD_DIM // 2
    freq = ROPE_BASE ** (-(jnp.arange(hd, dtype=F32) * 2.0 / HEAD_DIM))
    angles = positions.astype(F32)[:, None] * freq[None, :]
    cos = jnp.cos(angles)
    sin = jnp.sin(angles)

    gains = gains_of(me, kvgs)
    nin, kraw, kv_lo, kv_hi = pre_kv(me, tokens, gains, cos, sin, kvgs)
    ranks = n_seq * n_shard
    per_seq = length // count
    pairs = [(i, i + 1) for i in range(ranks - 1) if (i + 1) % per_seq]
    halo = lax.ppermute(kv_hi, ("seq", "shard"), pairs)
    out_far = far(out_weight)
    q_far = after(q_far, nin)
    qs_w = (query_weight, q_near, q_far, near(q_far))
    gate_a = far(gate_half)
    qraw, qs = pre_q(me, nin, gains, cos, sin, qs_w)
    o_hi, pm_hi, p1_hi = att(flag, qs, kv_lo, kv_hi, False, 1)
    o_lo, pm_lo, p1_lo = att(flag, after(qs, o_hi), halo, kv_lo, True, 0)
    out_far = after(out_far, o_lo)
    gate_a = after(gate_a, o_lo)
    up_a = far(after(up_half, gate_a))
    gate_b = relay(gate_a)
    outs = (out_weight, out_near, out_far, near(out_far))
    ap, nm = mid_part(me, o_lo, o_hi, tokens, gains, outs)
    gate_b = after(gate_b, nm)
    up_a = after(up_a, nm)
    down_a = far(after(down_half, up_a))
    up_b = relay(up_a)
    gates = (gate_weight, gate_near, gate_a, gate_b, near(gate_a), near(gate_b))
    act, slope = ff(me, nm, gates)
    up_b = after(up_b, act)
    down_a = after(down_a, act)
    down_b = relay(down_a)
    ups = (up_weight, up_near, up_a, up_b, near(up_a), near(up_b))
    hid, bact = ff(me, nm, ups, (act, slope))
    down_b = after(down_b, hid)
    downs = (down_weight, down_near, down_a, down_b, near(down_a), near(down_b))
    block_out, dd, wd, keep, send, gain_down = down_part(
        me, hid, tokens, cotangent, ap, gains, downs
    )
    chains = {name: Chain(place) for name in "abcd"}

    def advance(order, *first):
        for name in order:
            chain = chains[name]
            if chain.steps:
                chain.wait(*first)
                chain.step()

    chains["d"].add(keep, send)
    keep, send, dnm = fb(me, nm, dd, act, bact, wd, gates, ups, 0, None)
    chains["a"].add(keep, send)
    advance(ORDER[0], dnm)
    dnm = after(dnm, place.token)
    keep, send, dnm = fb(me, nm, dd, act, bact, wd, gates, ups, 1, dnm)
    chains["b"].add(keep, send)
    advance(ORDER[1], dnm)
    keep, send, d_o, d_mid, gain_mid = fe(
        me, o_lo, o_hi, tokens, cotangent, gains, ap, after(dnm, place.token), outs
    )
    chains["b"].add(keep, send)
    advance(ORDER[2], d_o)
    dq_lo, kv_back, kv_a, gq_lo = att_back(
        qs, qraw, halo, kv_lo, pm_lo, p1_lo, after(d_o, place.token), gains, cos, sin, 0
    )
    returned = lax.ppermute(kv_back, ("seq", "shard"), [(j, i) for i, j in pairs])
    advance(ORDER[3], dq_lo)
    dq_hi, kv_b, kv_c, gq_hi = att_back(
        qs, qraw, kv_lo, kv_hi, pm_hi, p1_hi, after(d_o, dq_lo, place.token), gains, cos, sin, 1
    )
    advance(ORDER[4], dq_hi)
    grad_tokens, keep, send = post(
        me,
        tokens,
        d_mid,
        nin,
        (dq_lo, after(dq_hi, place.token)),
        (kv_a, kv_b, kv_c, returned),
        kraw,
        gains,
        cos,
        sin,
        (gq_lo, gq_hi, gain_mid, gain_down),
        qs_w,
        kvgs,
    )
    chains["c"].add(keep, send)
    advance(ORDER[5], keep)
    for name in "dacb":
        advance(name * len(chains[name].steps))
    r_down = finish_one(me, chains["d"].keep, chains["d"].got)
    r_query, r_key, r_value, tail = finish_three(me, chains["c"].keep, chains["c"].got)
    r_gate, r_up, r_out = finish_two(
        me, chains["a"].keep, chains["a"].got, chains["b"].keep, chains["b"].got
    )
    return (
        block_out,
        grad_tokens,
        r_query,
        r_key,
        r_value,
        r_out,
        r_gate,
        r_up,
        r_down,
        tail[0, :gd],
        tail[4, :gh],
        tail[5, :gh],
        tail[1, :gd],
        tail[2, :gd],
        tail[3, :gd],
    )


def solution(mesh):
    token = P(("seq", "shard"), None)
    matrix = P("shard", None)
    vector = P("shard")
    in_specs = (token,) + (matrix,) * 7 + (vector,) * 6 + (token,)
    out_specs = (token, token) + (matrix,) * 7 + (vector,) * 6
    return jax.shard_map(shards, mesh=mesh, in_specs=in_specs, out_specs=out_specs, check_vma=False)
```

```python
import jax
import jax.numpy as jnp
from jax import lax
from jax.experimental import pallas as pl
from jax.experimental.pallas import tpu as pltpu
from jax.sharding import PartitionSpec as P

D = 640
HEADS = 4
HEAD_DIM = 256
FF = 2048
WINDOW = 512
SEQ_CAP = 8192
HALF = 512
QB = 256
ROWS = HEADS * QB
CHUNK = 512

EPS = 1e-06
ROPE_BASE = 10000.0
LOG2E = 1.4426950408889634
LN2 = 0.6931471805599453
SCALE = HEAD_DIM**-0.5

F32 = jnp.float32
BF16 = jnp.bfloat16
VM = pl.BlockSpec(memory_space=pltpu.VMEM)
SM = pl.BlockSpec(memory_space=pltpu.SMEM)
HM = pl.BlockSpec(memory_space=pltpu.HBM)
NN = (((1,), (0,)), ((), ()))
NT = (((1,), (1,)), ((), ()))
TN = (((0,), (0,)), ((), ()))


def dot(a, b, dims=NN):
    return lax.dot_general(a, b, dims, preferred_element_type=F32)


def params(mib=14):
    return pltpu.CompilerParams(vmem_limit_bytes=mib * 2**20)


def sds(shape, dtype=BF16):
    return jax.ShapeDtypeStruct(shape, dtype)


def cost(flops, nbytes):
    return pl.CostEstimate(flops=int(flops), bytes_accessed=int(nbytes), transcendentals=0)


def rms_factor(v):
    return lax.rsqrt(jnp.mean(v * v, axis=-1, keepdims=True) + EPS)


def norm_back(v, factor, gain, incoming):
    united = v * factor
    scaled = incoming * gain
    back = factor * (scaled - united * jnp.mean(scaled * united, axis=-1, keepdims=True))
    return back, jnp.sum(incoming * united, axis=0, keepdims=True)


def offsets(me, rows):
    return (
        me * rows,
        (me + 1 - 2 * (me % 2)) * rows,
        ((me + 2) % 4) * rows,
        (3 - me) * rows,
    )


def hbm(shape, dtype=BF16):
    return pltpu.HBM(shape, dtype)


ME, XBIT, FLAG, EVEN, YBIT, SECOND, HERE = range(7)


def pin(x):
    return pltpu.with_memory_space_constraint(x, pltpu.HBM)


def pinned(*arrays):
    return tuple(pin(x) for x in arrays)


def whole(piece):
    return piece


def place_copies(me_ref, pieces, src_of, buf, rows, sems, first):
    me, b = me_ref[ME], me_ref[XBIT]
    spots = [(p, o, rows) for p, o in zip(pieces, offsets(me, rows))]
    if len(pieces) == 6:
        part = rows // 2
        far, last = spots[2][1], spots[3][1]
        spots = spots[:2]
        for base, p in ((far, pieces[2:4]), (last, pieces[4:6])):
            spots.append((p[0], base + b * part, part))
            spots.append((p[1], base + (1 - b) * part, part))
    copies = []
    for k, (piece, off, n) in enumerate(spots):
        copies.append(
            pltpu.make_async_copy(
                src_of(piece), buf.at[pl.ds(pl.multiple_of(off, 16), n)], sems.at[first + k]
            )
        )
    return copies


def pack_kernel(info, k, v, g0, g1, g2, g3, g4, g5, out, r0, r1, r2, r3, r4, r5, sems):
    rows = D // 4
    gains = (g0, g1, g2, g3, g4, g5)
    places = (r0, r1, r2, r3, r4, r5)
    copies = [
        pltpu.make_async_copy(k, out.at[pl.ds(0, rows), pl.ds(0, HEAD_DIM)], sems.at[0]),
        pltpu.make_async_copy(v, out.at[pl.ds(0, rows), pl.ds(HEAD_DIM, HEAD_DIM)], sems.at[1]),
    ]
    for i in range(6):
        copies.append(pltpu.make_async_copy(gains[i], places[i], sems.at[2 + i]))
    for c in copies:
        c.start()
    out[rows:, :] = jnp.zeros((16, 2 * HEAD_DIM), BF16)
    for c in copies:
        c.wait()
    for i, r in enumerate(places):
        out[rows + i : rows + i + 1, : r.shape[0]] = r[...].reshape(1, -1)


def pack(info, k, v, *gains):
    return pl.pallas_call(
        pack_kernel,
        out_shape=sds((D // 4 + 16, 2 * HEAD_DIM)),
        in_specs=[SM] + [HM] * 8,
        out_specs=VM,
        scratch_shapes=[pltpu.VMEM(g.shape, BF16) for g in gains] + [pltpu.SemaphoreType.DMA((8,))],
        compiler_params=params(),
        cost_estimate=cost(1e6, 4e5),
        name="pack",
    )(info, *(pin(w) for w in (k, v) + gains))


def halves_kernel(info, *refs):
    n = len(refs) // 2
    ins, outs, sems = refs[:n], refs[n : 2 * n], refs[2 * n]
    copies = []
    for i, (w, o) in enumerate(zip(ins, outs)):
        rows = w.shape[0] // 2
        at = pl.multiple_of(info[XBIT] * rows, 16)
        copies.append(pltpu.make_async_copy(w.at[pl.ds(at, rows)], o, sems.at[i]))
    for c in copies:
        c.start()
    for c in copies:
        c.wait()


def halves(info, *weights):
    return pl.pallas_call(
        halves_kernel,
        out_shape=tuple(sds((w.shape[0] // 2, w.shape[1])) for w in weights),
        in_specs=[SM] + [HM] * len(weights),
        out_specs=(VM,) * len(weights),
        scratch_shapes=[pltpu.SemaphoreType.DMA((len(weights),))],
        compiler_params=params(),
        cost_estimate=cost(1e6, 2e6),
        name="halves",
    )(info, *(pin(w) for w in weights))


def gains_kernel(me_ref, g0, g1, g2, g3, out):
    gd = D // 4
    gh = HEAD_DIM // 4
    wide = jnp.zeros((16, D), F32)
    small = jnp.zeros((16, HEAD_DIM), F32)
    spots = offsets(me_ref[ME], 1)
    for spot, g in zip(spots, (g0, g1, g2, g3)):
        piece = g[...]
        row = lax.broadcasted_iota(jnp.int32, (HEAD_DIM, D), 0)
        col = lax.broadcasted_iota(jnp.int32, (HEAD_DIM, D), 1)
        place = ((col == row + spot * gd) & (row < gd)).astype(BF16)
        wide = wide + dot(piece, place)
        row = lax.broadcasted_iota(jnp.int32, (HEAD_DIM, HEAD_DIM), 0)
        col = lax.broadcasted_iota(jnp.int32, (HEAD_DIM, HEAD_DIM), 1)
        place = ((col == row + spot * gh) & (row < gh)).astype(BF16)
        small = small + dot(piece, place)
    out[0:4, :] = wide[0:4, :]
    out[4:8, :] = jnp.zeros((4, D), F32)
    out[4:8, :HEAD_DIM] = small[4:8, :]


def gains_of(me, pieces):
    part = pl.BlockSpec((16, HEAD_DIM), lambda i: (D // 4 // 16, 0))
    return pl.pallas_call(
        gains_kernel,
        grid=(1,),
        out_shape=sds((8, D), F32),
        in_specs=[SM] + [part] * 4,
        out_specs=VM,
        compiler_params=params(),
        cost_estimate=cost(1e8, 1e5),
        name="gains",
    )(me, *pieces)


def rotated(u, cos, sin):
    hd = HEAD_DIM // 2
    u1 = u[:, :hd]
    u2 = u[:, hd:]
    return (u1 * cos - u2 * sin).astype(BF16), (u2 * cos + u1 * sin).astype(BF16)


def pre_kv_kernel(me_ref, tok, gains, cos_ref, sin_ref, w0, w1, w2, w3, nin_o, kraw_o, lo_o, hi_o, wbuf, sems):
    rows = D // 4
    copies = place_copies(
        me_ref, (w0, w1, w2, w3), lambda w: w.at[pl.ds(0, rows)], wbuf, rows, sems, 0
    )
    for c in copies:
        c.start()
    hd = HEAD_DIM // 2
    x = tok[...].astype(F32)
    nin = (x * rms_factor(x) * gains[0:1, :]).astype(BF16)
    nin_o[...] = nin
    for c in copies:
        c.wait()
    k = dot(nin, wbuf[:, :HEAD_DIM])
    kraw_o[...] = k.astype(BF16)
    r1, r2 = rotated(k * rms_factor(k) * gains[5:6, :HEAD_DIM], cos_ref[...], sin_ref[...])
    v = dot(nin, wbuf[:, HEAD_DIM:]).astype(BF16)
    for half, o in enumerate((lo_o, hi_o)):
        sl = slice(HALF * half, HALF * (half + 1))
        o[:, :hd] = r1[sl]
        o[:, hd:HEAD_DIM] = r2[sl]
        o[:, HEAD_DIM:] = v[sl]


def pre_kv(me, tok, gains, cos, sin, pieces):
    t = tok.shape[0]
    return pl.pallas_call(
        pre_kv_kernel,
        out_shape=(
            sds((t, D)),
            sds((t, HEAD_DIM)),
            sds((HALF, 2 * HEAD_DIM)),
            sds((HALF, 2 * HEAD_DIM)),
        ),
        in_specs=[SM, VM, VM, VM, VM, HM, HM, HM, HM],
        out_specs=(VM,) * 4,
        scratch_shapes=[pltpu.VMEM((D, 2 * HEAD_DIM), BF16), pltpu.SemaphoreType.DMA((4,))],
        compiler_params=params(),
        cost_estimate=cost(2 * t * D * 512, 5e6),
        name="pre_kv",
    )(me, tok, gains, cos, sin, *pieces)


def pre_q_kernel(me_ref, nin_i, gains, cos_ref, sin_ref, w0, w1, w2, w3, qraw_o, qs_o, wbuf, sems):
    rows = D // 4
    hd = HEAD_DIM // 2

    @pl.when(pl.program_id(0) == 0)
    def _():
        copies = place_copies(
            me_ref, (w0, w1, w2, w3), lambda w: w.at[pl.ds(0, rows)], wbuf, rows, sems, 0
        )
        for c in copies:
            c.start()
        for c in copies:
            c.wait()

    q = dot(nin_i[...], wbuf[:, pl.ds(pl.multiple_of(pl.program_id(0) * HEAD_DIM, HEAD_DIM), HEAD_DIM)])
    qraw_o[0] = q.astype(BF16)
    u = q * (rms_factor(q) * (SCALE * LOG2E)) * gains[4:5, :HEAD_DIM]
    r1, r2 = rotated(u, cos_ref[...], sin_ref[...])
    qs_o[0, :, :hd] = r1
    qs_o[0, :, hd:] = r2


def pre_q(me, nin, gains, cos, sin, pieces):
    t = nin.shape[0]
    head = pl.BlockSpec((1, t, HEAD_DIM), lambda h: (h, 0, 0))
    return pl.pallas_call(
        pre_q_kernel,
        grid=(HEADS,),
        out_shape=(hbm((HEADS, t, HEAD_DIM)), sds((HEADS, t, HEAD_DIM))),
        in_specs=[SM, VM, VM, VM, VM, HM, HM, HM, HM],
        out_specs=(head, head),
        scratch_shapes=[pltpu.VMEM((D, HEADS * HEAD_DIM), BF16), pltpu.SemaphoreType.DMA((4,))],
        compiler_params=params(),
        cost_estimate=cost(2 * t * D * 1024, 5e6),
        name="pre_q",
    )(me, nin, gains, cos, sin, *pieces)


def key_blocks(j, kvp, kvs, lo, hi):
    blocks = (kvp[0:QB, lo:hi], kvp[QB : 2 * QB, lo:hi], kvs[0:QB, lo:hi], kvs[QB : 2 * QB, lo:hi])
    return blocks[j : j + 3]


def upper_mask():
    row = lax.broadcasted_iota(jnp.int32, (HEADS, QB, QB), 1).reshape(ROWS, QB)
    col = lax.broadcasted_iota(jnp.int32, (ROWS, QB), 1)
    return col > row


def att_kernel(masked, flag_ref, qs, kvp, kvs, o_o, pm_o, p1_o):
    upper = upper_mask()
    for j in range(2):
        sl = slice(QB * j, QB * (j + 1))
        q = qs[:, sl, :].reshape(ROWS, HEAD_DIM)
        k0, k1, k2 = key_blocks(j, kvp, kvs, 0, HEAD_DIM)
        v0, v1, v2 = key_blocks(j, kvp, kvs, HEAD_DIM, 2 * HEAD_DIM)
        em = jnp.exp2(jnp.where(upper, dot(q, k0, NT), dot(q, k2, NT)))
        e1 = jnp.exp2(dot(q, k1, NT))
        if masked:
            keep = flag_ref[FLAG].astype(F32)
            em = em * jnp.where(upper, keep, 1.0)
            if j == 0:
                e1 = e1 * keep
        inv = 1.0 / jnp.sum(em + e1, axis=-1, keepdims=True)
        pm = (em * inv).astype(BF16)
        p1 = (e1 * inv).astype(BF16)
        zero = jnp.zeros_like(pm)
        out = dot(p1, v1) + dot(jnp.where(upper, pm, zero), v0) + dot(jnp.where(upper, zero, pm), v2)
        pm_o[:, sl, :] = pm.reshape(HEADS, QB, QB)
        p1_o[:, sl, :] = p1.reshape(HEADS, QB, QB)
        for h in range(HEADS):
            o_o[sl, HEAD_DIM * h : HEAD_DIM * (h + 1)] = out[QB * h : QB * (h + 1), :].astype(BF16)


def half_spec(half):
    return pl.BlockSpec((HEADS, HALF, HEAD_DIM), lambda i: (0, half, 0))


def att(flag, qs, kvp, kvs, masked, half):
    shp = sds((HEADS, HALF, HEAD_DIM))

    def body(*refs):
        att_kernel(masked, *refs)

    return pl.pallas_call(
        body,
        grid=(1,),
        out_shape=(sds((HALF, HEADS * HEAD_DIM)), shp, shp),
        in_specs=[SM, half_spec(half), VM, VM],
        out_specs=(VM,) * 3,
        compiler_params=params(),
        cost_estimate=cost(12e9 / 4, 5e6),
        name="att",
    )(flag, qs, kvp, kvs)


def att_back_kernel(qs, qraw, kvp, kvs, pm_i, p1_i, do_i, gains, cos_ref, sin_ref, dq_o, dkvp_o, dkvs_o, gain_o, acc):
    upper = upper_mask()
    hd = HEAD_DIM // 2
    acc[...] = jnp.zeros_like(acc)
    gsum = jnp.zeros((1, HEAD_DIM), F32)
    for j in range(2):
        sl = slice(QB * j, QB * (j + 1))
        q = qs[:, sl, :].reshape(ROWS, HEAD_DIM)
        do = do_i[:, sl, :].reshape(ROWS, HEAD_DIM)
        k0, k1, k2 = key_blocks(j, kvp, kvs, 0, HEAD_DIM)
        v0, v1, v2 = key_blocks(j, kvp, kvs, HEAD_DIM, 2 * HEAD_DIM)
        pmb = pm_i[:, sl, :].reshape(ROWS, QB)
        p1b = p1_i[:, sl, :].reshape(ROWS, QB)
        dpm = jnp.where(upper, dot(do, v0, NT), dot(do, v2, NT))
        dp1 = dot(do, v1, NT)
        pm = pmb.astype(F32)
        p1 = p1b.astype(F32)
        total = jnp.sum(pm * dpm + p1 * dp1, axis=-1, keepdims=True)
        dsm = (pm * (dpm - total)).astype(BF16)
        ds1 = (p1 * (dp1 - total)).astype(BF16)
        zero = jnp.zeros_like(dsm)
        ds0 = jnp.where(upper, dsm, zero)
        ds2 = jnp.where(upper, zero, dsm)
        p0 = jnp.where(upper, pmb, zero)
        p2 = jnp.where(upper, zero, pmb)
        for t, (ds, p) in enumerate(((ds0, p0), (ds1, p1b), (ds2, p2))):
            at = slice(QB * (j + t), QB * (j + t + 1))
            acc[at, :HEAD_DIM] += dot(ds, q, TN) * LN2
            acc[at, HEAD_DIM:] += dot(p, do, TN)
        dq = (dot(ds0, k0) + dot(ds1, k1) + dot(ds2, k2)) * SCALE
        cos = cos_ref[sl, :]
        sin = sin_ref[sl, :]
        gain = gains[4:5, :HEAD_DIM]
        for h in range(HEADS):
            d1 = dq[QB * h : QB * (h + 1), :hd]
            d2 = dq[QB * h : QB * (h + 1), hd:]
            inc = jnp.concatenate([d1 * cos + d2 * sin, d2 * cos - d1 * sin], axis=-1)
            raw = qraw[h, sl, :].astype(F32)
            back, terms = norm_back(raw, rms_factor(raw), gain, inc)
            gsum = gsum + terms
            dq_o[sl, HEAD_DIM * h : HEAD_DIM * (h + 1)] = back.astype(BF16)
    dkvp_o[...] = acc[:HALF, :].astype(BF16)
    dkvs_o[...] = acc[HALF:, :]
    gain_o[...] = jnp.broadcast_to(gsum, (8, HEAD_DIM))


def att_back(qs, qraw, kvp, kvs, pm, p1, do, gains, cos, sin, half):
    dospec = half_spec(half)
    tab = pl.BlockSpec((HALF, HEAD_DIM // 2), lambda i: (half, 0))
    return pl.pallas_call(
        att_back_kernel,
        grid=(1,),
        out_shape=(
            sds((HALF, HEADS * HEAD_DIM)),
            sds((HALF, 2 * HEAD_DIM)),
            sds((HALF, 2 * HEAD_DIM), F32),
            sds((8, HEAD_DIM), F32),
        ),
        in_specs=[dospec, dospec, VM, VM, VM, VM, dospec, VM, tab, tab],
        out_specs=(VM,) * 4,
        scratch_shapes=[pltpu.VMEM((2 * HALF, 2 * HEAD_DIM), F32)],
        compiler_params=params(),
        cost_estimate=cost(24e9 / 4, 9e6),
        name="att_back",
    )(qs, qraw, kvp, kvs, pm, p1, do, gains, cos, sin)


def mid_kernel(me_ref, o_lo, o_hi, tok, gains, w0, w1, w2, w3, ap_o, nm_o, wo, sems):
    ro = HEADS * HEAD_DIM // 4
    copies = place_copies(me_ref, (w0, w1, w2, w3), lambda w: w, wo, ro, sems, 0)
    for c in copies:
        c.start()
    for c in copies:
        c.wait()
    for half, o in enumerate((o_lo, o_hi)):
        sl = slice(HALF * half, HALF * (half + 1))
        proj = dot(o[...], wo[...])
        ap_o[sl, :] = proj.astype(BF16)
        mid = tok[sl, :].astype(F32) + proj * rms_factor(proj) * gains[1:2, :]
        nm_o[sl, :] = (mid * rms_factor(mid) * gains[2:3, :]).astype(BF16)


def mid_part(me, o_lo, o_hi, tok, gains, outs):
    t = tok.shape[0]
    return pl.pallas_call(
        mid_kernel,
        out_shape=(sds((t, D)), sds((t, D))),
        in_specs=[SM] + [VM] * 4 + [HM] * 4,
        out_specs=(VM, VM),
        scratch_shapes=[
            pltpu.VMEM((HEADS * HEAD_DIM, D), BF16),
            pltpu.SemaphoreType.DMA((4,)),
        ],
        compiler_params=params(),
        cost_estimate=cost(2 * t * D * 1024, 8e6),
        name="mid",
    )(me, o_lo, o_hi, tok, gains, *outs)


FH = FF // 2
STEP = 512
WIDE = 512
RB = 512


def by_columns(me_ref, pieces, buf, sems):
    step = pl.program_id(0)

    def copies(i):
        at = pl.ds(pl.multiple_of(i * STEP, STEP), STEP)
        return place_copies(
            me_ref, pieces, lambda w: w.at[:, at], buf.at[:, at], D // 4, sems, 6 * i
        )

    @pl.when(step == 0)
    def _():
        for i in range(FF // STEP):
            for c in copies(i):
                c.start()

    for c in copies(step):
        c.wait()
    return pl.ds(pl.multiple_of(step * STEP, STEP), STEP)


def gate_kernel(me_ref, nm, *rest):
    pieces, (a_o, s_o, wg, sems) = rest[:6], rest[6:]

    cs = by_columns(me_ref, pieces, wg, sems)
    c0 = 0.7978845608028654
    c1 = 0.044715 * c0
    for r in range(0, nm.shape[0], RB):
        g = dot(nm[r : r + RB, :], wg[:, cs])
        g2 = g * g
        t = jnp.tanh(g * (c0 + c1 * g2))
        h = 0.5 + 0.5 * t
        a = g * h
        slope = h + a * (1.0 - h) * (2.0 * c0 + (6.0 * c1) * g2)
        a_o[r : r + RB, :] = a.astype(BF16)
        s_o[r : r + RB, :] = slope.astype(BF16)


def up_kernel(me_ref, nm, a_i, s_i, *rest):
    pieces, (hid_o, b_o, wu, sems) = rest[:6], rest[6:]

    cs = by_columns(me_ref, pieces, wu, sems)
    for r in range(0, nm.shape[0], RB):
        rs = slice(r, r + RB)
        u = dot(nm[rs, :], wu[:, cs])
        hid_o[rs, :] = (a_i[rs, :].astype(F32) * u).astype(BF16)
        b_o[rs, :] = (u * s_i[rs, :].astype(F32)).astype(BF16)


def ff(me, nm, pieces, before=()):
    t = nm.shape[0]
    col = pl.BlockSpec((t, STEP), lambda i: (0, i))
    return pl.pallas_call(
        up_kernel if before else gate_kernel,
        grid=(FF // STEP,),
        out_shape=(sds((t, FF)),) * 2,
        in_specs=[SM, VM] + [col] * len(before) + [HM] * 6,
        out_specs=(col,) * 2,
        scratch_shapes=[pltpu.VMEM((D, FF), BF16), pltpu.SemaphoreType.DMA((6 * FF // STEP,))],
        compiler_params=params(),
        cost_estimate=cost(2 * t * D * FF, 12e6),
        name="up" if before else "gate",
    )(me, nm, *before, *pieces)


def down_kernel(me_ref, hid, tok, cot, ap, gains, *rest):
    pieces, (out_o, dd_o, wd_o, keep_o, send_o, gain_o, sems) = rest[:6], rest[6:]
    rf = FF // 4
    core = me_ref[ME] % 2
    copies = place_copies(me_ref, pieces, whole, wd_o, rf, sems, 0)
    for c in copies:
        c.start()
    for c in copies:
        c.wait()
    gsum = jnp.zeros((1, D), F32)
    for half in range(2):
        sl = slice(HALF * half, HALF * (half + 1))
        dn = dot(hid[sl, :], wd_o[...])
        proj = ap[sl, :].astype(F32)
        mid = tok[sl, :].astype(F32) + proj * rms_factor(proj) * gains[1:2, :]
        fac = rms_factor(dn)
        out_o[sl, :] = (mid + dn * fac * gains[3:4, :]).astype(BF16)
        back, terms = norm_back(dn, fac, gains[3:4, :], cot[sl, :].astype(F32))
        dd_o[sl, :] = back.astype(BF16)
        gsum = gsum + terms
    gain_o[...] = jnp.broadcast_to(gsum, (8, D))
    for y in range(2):
        for part, o in ((core, keep_o), (1 - core, send_o)):
            at = pl.ds(pl.multiple_of((2 * y + part) * rf, rf), rf)
            g = dot(hid[:, at], dd_o[...], TN).astype(BF16)
            for j in range(D // 128):
                o[y, j] = g[:, 128 * j : 128 * (j + 1)]


def down_part(me, hid, tok, cot, ap, gains, pieces):
    t = tok.shape[0]
    return pl.pallas_call(
        down_kernel,
        out_shape=(
            sds((t, D)),
            sds((t, D)),
            sds((FF, D)),
            sds((2, D // 128, FF // 4, 128)),
            sds((2, D // 128, FF // 4, 128)),
            sds((8, D), F32),
        ),
        in_specs=[SM] + [VM] * 5 + [HM] * 6,
        out_specs=(VM,) * 6,
        scratch_shapes=[pltpu.SemaphoreType.DMA((6,))],
        compiler_params=params(),
        cost_estimate=cost(4 * t * D * FF, 20e6),
        name="down",
    )(me, hid, tok, cot, ap, gains, *pieces)


def fb_kernel(half, me_ref, nm, dd, a_i, b_i, wd, *rest):
    gates, ups, rest = rest[:6], rest[6:12], rest[12:]
    first = half == 0
    if first:
        keep_o, send_o, dnm_o, wg, wu, gs, sems = rest
    else:
        dnm_i, keep_o, send_o, dnm_o, wg, wu, gs, sems = rest
    core = me_ref[ME] % 2

    copies = []
    for k, (pieces, buf) in enumerate(((gates, wg), (ups, wu))):
        copies += place_copies(
            me_ref, pieces, lambda w: w.at[:, pl.ds(FH * half, FH)], buf, D // 4, sems, 6 * k
        )

    @pl.when(pl.program_id(0) == 0)
    def _():
        for c in copies:
            c.start()

    cs = pl.ds(pl.multiple_of(pl.program_id(0) * WIDE, WIDE), WIDE)
    dh = dot(dd[...], wd[...], NT)
    dg = (dh * b_i[...].astype(F32)).astype(BF16)
    du = (dh * a_i[...].astype(F32)).astype(BF16)
    gr = D // 4
    for k, d in enumerate((dg, du)):
        gs[k] = dot(nm[...], d, TN).astype(BF16)
        for y in range(2):
            for part, o in ((core, keep_o), (1 - core, send_o)):
                at = pl.ds(pl.multiple_of((2 * y + part) * gr, gr), gr)
                for j in range(WIDE // 128):
                    o[y, k, j] = gs[k, at, 128 * j : 128 * (j + 1)]

    @pl.when(pl.program_id(0) == 0)
    def _():
        for c in copies:
            c.wait()
        if first:
            dnm_o[...] = jnp.zeros_like(dnm_o)
        else:
            dnm_o[...] = dnm_i[...]

    dnm_o[...] += dot(dg, wg[:, cs], NT) + dot(du, wu[:, cs], NT)


def fb(me, nm, dd, a, b, wd, gates, ups, part, dnm):
    t = nm.shape[0]
    steps = FH // WIDE
    col = pl.BlockSpec((t, WIDE), lambda i: (0, i + steps * part))
    extra = () if dnm is None else (dnm,)

    def body(*refs):
        fb_kernel(part, *refs)

    return pl.pallas_call(
        body,
        grid=(steps,),
        out_shape=(sds((2, 2, FH // 128, D // 4, 128)),) * 2 + (sds((t, D), F32),),
        in_specs=[SM, VM, VM, col, col, pl.BlockSpec((WIDE, D), lambda i: (i + steps * part, 0))]
        + [HM] * 12
        + [VM] * len(extra),
        out_specs=(pl.BlockSpec((2, 2, WIDE // 128, D // 4, 128), lambda i: (0, 0, i, 0, 0)),) * 2
        + (VM,),
        scratch_shapes=[
            pltpu.VMEM((D, FH), BF16),
            pltpu.VMEM((D, FH), BF16),
            pltpu.VMEM((2, D, WIDE), BF16),
            pltpu.SemaphoreType.DMA((12,)),
        ],
        compiler_params=params(20),
        cost_estimate=cost(10 * t * D * FH, 16e6),
        name="fb",
    )(me, nm, dd, a, b, wd, *gates, *ups, *extra)


def fe_kernel(me_ref, o_lo, o_hi, tok, cot, gains, ap, dnm, w0, w1, w2, w3, keep_o, send_o, do_o, dmid_o, gain_o, wo, datt, sems):
    ro = HEADS * HEAD_DIM // 4
    copies = place_copies(me_ref, (w0, w1, w2, w3), lambda w: w, wo, ro, sems, 0)
    for c in copies:
        c.start()
    gm = jnp.zeros((1, D), F32)
    ga = jnp.zeros((1, D), F32)
    for half in range(2):
        sl = slice(HALF * half, HALF * (half + 1))
        proj = ap[sl, :].astype(F32)
        pfac = rms_factor(proj)
        mid = tok[sl, :].astype(F32) + proj * pfac * gains[1:2, :]
        back, terms = norm_back(mid, rms_factor(mid), gains[2:3, :], dnm[sl, :])
        dmid = cot[sl, :].astype(F32) + back
        gm = gm + terms
        dmid_o[sl, :] = dmid.astype(BF16)
        back, terms = norm_back(proj, pfac, gains[1:2, :], dmid)
        ga = ga + terms
        datt[sl, :] = back.astype(BF16)
    gain_o[0:8, :] = jnp.broadcast_to(gm, (8, D))
    gain_o[8:16, :] = jnp.broadcast_to(ga, (8, D))
    for c in copies:
        c.wait()
    for h in range(HEADS):
        at = slice(HEAD_DIM * h, HEAD_DIM * (h + 1))
        do_o[h] = dot(datt[...], wo[at, :], NT).astype(BF16)
    core = me_ref[ME] % 2
    for y in range(2):
        for part, o in ((core, keep_o), (1 - core, send_o)):
            cs = pl.ds(pl.multiple_of((2 * y + part) * HEAD_DIM, HEAD_DIM), HEAD_DIM)
            g = dot(o_lo[:, cs], datt[:HALF, :], TN) + dot(o_hi[:, cs], datt[HALF:, :], TN)
            g = g.astype(BF16)
            for j in range(D // 128):
                o[y, j] = g[:, 128 * j : 128 * (j + 1)]


def fe(me, o_lo, o_hi, tok, cot, gains, ap, dnm, outs):
    t = tok.shape[0]
    return pl.pallas_call(
        fe_kernel,
        out_shape=(
            sds((2, D // 128, HEAD_DIM, 128)),
            sds((2, D // 128, HEAD_DIM, 128)),
            sds((HEADS, t, HEAD_DIM)),
            sds((t, D)),
            sds((16, D), F32),
        ),
        in_specs=[SM] + [VM] * 7 + [HM] * 4,
        out_specs=(VM,) * 5,
        scratch_shapes=[
            pltpu.VMEM((HEADS * HEAD_DIM, D), BF16),
            pltpu.VMEM((t, D), BF16),
            pltpu.SemaphoreType.DMA((4,)),
        ],
        compiler_params=params(),
        cost_estimate=cost(4 * t * D * 1024, 14e6),
        name="fe",
    )(me, o_lo, o_hi, tok, cot, gains, ap, dnm, *outs)


LAST = 2048


def post_kernel(
    me_ref, nin, dq_lo, dq_hi, kv_a, kv_b, kv_c, kv_d, kraw,
    gains, cos_ref, sin_ref, gq_lo, gq_hi, gmid, gdown,
    dkv, keep_o, send_o,
    gs, sums, small,
):
    rows = D // 4
    hd = HEAD_DIM // 2
    gk = jnp.zeros((1, HEAD_DIM), F32)
    for half, (first, second) in enumerate(((kv_a, kv_b), (kv_c, kv_d))):
        sl = slice(HALF * half, HALF * (half + 1))
        both = first[...].astype(F32) + second[...].astype(F32)
        cos = cos_ref[sl, :]
        sin = sin_ref[sl, :]
        d1 = both[:, :hd]
        d2 = both[:, hd:HEAD_DIM]
        inc = jnp.concatenate([d1 * cos + d2 * sin, d2 * cos - d1 * sin], axis=-1)
        raw = kraw[sl, :].astype(F32)
        back, terms = norm_back(raw, rms_factor(raw), gains[5:6, :HEAD_DIM], inc)
        gk = gk + terms
        dkv[sl, :HEAD_DIM] = back.astype(BF16)
        dkv[sl, HEAD_DIM:] = both[:, HEAD_DIM:].astype(BF16)

    core = me_ref[ME] % 2

    def put(slot, g):
        gs[slot] = g.astype(BF16)
        for y in range(2):
            for part, o in ((core, keep_o), (1 - core, send_o)):
                at = pl.ds(pl.multiple_of((2 * y + part) * rows, rows), rows)
                for j in range(2):
                    to = (2 * slot + j) * rows
                    o[y, to : to + rows, :] = gs[slot, at, 128 * j : 128 * (j + 1)]

    for h in range(HEADS):
        cs = slice(HEAD_DIM * h, HEAD_DIM * (h + 1))
        put(h, dot(nin[:HALF, :], dq_lo[:, cs], TN) + dot(nin[HALF:, :], dq_hi[:, cs], TN))
    put(HEADS, dot(nin[...], dkv[:, :HEAD_DIM], TN))
    put(HEADS + 1, dot(nin[...], dkv[:, HEAD_DIM:], TN))
    sums[...] = jnp.zeros_like(sums)
    small[...] = jnp.zeros_like(small)
    sums[1:2, :] = gmid[8:9, :]
    sums[2:3, :] = gmid[0:1, :]
    sums[3:4, :] = gdown[0:1, :]
    small[4:5, :] = gq_lo[0:1, :] + gq_hi[0:1, :]
    small[5:6, :] = gk
    gd = D // 4
    gh = HEAD_DIM // 4
    base = 12 * rows
    for y in range(2):
        for part, o in ((core, keep_o), (1 - core, send_o)):
            s = 2 * y + part
            row = lax.broadcasted_iota(jnp.int32, (D, HEAD_DIM), 0)
            col = lax.broadcasted_iota(jnp.int32, (D, HEAD_DIM), 1)
            place = ((row == col + s * gd) & (col < gd)).astype(BF16)
            g = dot(sums[...].astype(BF16), place)
            row = lax.broadcasted_iota(jnp.int32, (HEAD_DIM, HEAD_DIM), 0)
            col = lax.broadcasted_iota(jnp.int32, (HEAD_DIM, HEAD_DIM), 1)
            place = ((row == col + s * gh) & (col < gh)).astype(BF16)
            g = (g + dot(small[...].astype(BF16), place)).astype(BF16)
            o[y, base : base + 16, :] = g[:, :128]
            o[y, base + 16 : base + 32, :] = g[:, 128:]
            o[y, base + 32 :, :] = jnp.zeros((LAST - base - 32, 128), BF16)


def post(me, nin, dqs, kvs, kraw, gains, cos, sin, sums):
    t = nin.shape[0]
    return pl.pallas_call(
        post_kernel,
        out_shape=(
            sds((t, 2 * HEAD_DIM)),
            sds((2, LAST, 128)),
            sds((2, LAST, 128)),
        ),
        in_specs=[SM] + [VM] * 15,
        out_specs=(VM,) * 3,
        scratch_shapes=[
            pltpu.VMEM((HEADS + 2, D, HEAD_DIM), BF16),
            pltpu.VMEM((16, D), F32),
            pltpu.VMEM((16, HEAD_DIM), F32),
        ],
        compiler_params=params(),
        cost_estimate=cost(2e9, 10e6),
        name="post",
    )(me, nin, *dqs, *kvs, kraw, gains, cos, sin, *sums)


def last_kernel(me_ref, tok, dmid, dq_lo, dq_hi, dkv, gains, q0, q1, q2, q3, k0, k1, k2, k3, gt_o, wq, wkv, sems):
    rows = D // 4
    copies = place_copies(me_ref, (q0, q1, q2, q3), whole, wq, rows, sems, 0)
    copies += place_copies(
        me_ref, (k0, k1, k2, k3), lambda w: w.at[pl.ds(0, rows)], wkv, rows, sems, 4
    )
    for c in copies:
        c.start()
    for c in copies:
        c.wait()
    for half, dq in enumerate((dq_lo, dq_hi)):
        for r in range(0, HALF, RB):
            rs = slice(HALF * half + r, HALF * half + r + RB)
            dnin = dot(dq[r : r + RB, :], wq[...], NT) + dot(dkv[rs, :], wkv[...], NT)
            x = tok[rs, :].astype(F32)
            back, _ = norm_back(x, rms_factor(x), gains[0:1, :], dnin)
            gt_o[rs, :] = (dmid[rs, :].astype(F32) + back).astype(BF16)


def last(me, tok, dmid, dqs, dkv, gains, qs, kvgs):
    t = tok.shape[0]
    return pl.pallas_call(
        last_kernel,
        out_shape=hbm((t, D)),
        in_specs=[SM] + [VM] * 6 + [HM] * 8,
        out_specs=VM,
        scratch_shapes=[
            pltpu.VMEM((D, HEADS * HEAD_DIM), BF16),
            pltpu.VMEM((D, 2 * HEAD_DIM), BF16),
            pltpu.SemaphoreType.DMA((8,)),
        ],
        compiler_params=params(),
        cost_estimate=cost(2e9, 8e6),
        name="last",
    )(me, tok, dmid, *dqs, dkv, gains, *qs, *kvgs)


def flip(x, axis, bit):
    n = lax.axis_size(axis)
    return lax.ppermute(x, axis, [(i, i ^ bit) for i in range(n)])


def pick(x, index, axis=0):
    return lax.dynamic_index_in_dim(x, index, axis, keepdims=False)


def after(x, *first):
    return lax.optimization_barrier((x,) + first)[0]


def joined(a, b):
    return (a.astype(F32) + b.astype(F32)).astype(BF16)


def small_call(body, name, out_rows, scalars, *arrays, scratch=()):
    size = sum(a.size for a in arrays)
    return pl.pallas_call(
        body,
        out_shape=tuple(sds(r + (128,)) for r in out_rows),
        in_specs=[SM] + [VM] * len(arrays),
        out_specs=(VM,) * len(out_rows),
        scratch_shapes=scratch,
        compiler_params=params(),
        cost_estimate=cost(size, 4 * size),
        name=name,
    )(scalars, *arrays)


def mix_first(scalars, keeps, gots):
    n = len(keeps)
    sizes = [k.shape[1] for k in keeps]
    rows = sum(sizes)

    def body(s, *refs):
        ks, gs = refs[:n], refs[n : 2 * n]
        send, keep, total = refs[2 * n :]
        at = 0
        for k, g, size in zip(ks, gs, sizes):
            for y in range(2):
                total[y, at : at + size, :] = joined(k[y], g[y])
            at += size
        even, y, x = s[EVEN], s[YBIT], s[XBIT]
        for t in range(2):
            for o, flip_it in ((send, 1), (keep, 0)):
                own_y = flip_it + y - 2 * flip_it * y
                own_x = flip_it + x - 2 * flip_it * x
                row = even * own_y + (1 - even) * t
                half = even * t + (1 - even) * own_x
                o[t] = total[row, pl.ds(pl.multiple_of(half * (rows // 2), 16), rows // 2), :]

    shape = (2, rows // 2)
    return small_call(
        body, "mix_first", (shape, shape), scalars, *keeps, *gots,
        scratch=[pltpu.VMEM((2, rows, 128), BF16)],
    )


def mix_half(info, index, keep, got):
    keep = keep.reshape(2, -1, 128)
    got = got.reshape(2, -1, 128)

    def body(i, k, g, send, kept):
        own = i[index]
        send[...] = joined(k[1 - own], g[1 - own])
        kept[...] = joined(k[own], g[own])

    shape = (keep.shape[1],)
    return small_call(body, "mix_half", (shape, shape), info, keep, got)


def mix_sum(info, keep, got):
    def body(i, k, g, o):
        o[...] = joined(k[...], g[...])

    return small_call(body, "mix_sum", (keep.shape[:1],), info, keep, got)[0]


def mix_both(info, index, own, other):
    rows = own.shape[0]

    def body(i, a, b, o):
        o[i[index]] = a[...]
        o[1 - i[index]] = b[...]

    return small_call(body, "mix_both", ((2, rows),), info, own, other)[0].reshape(2 * rows, 128)


class Place:
    def __init__(self, first_pos):
        shard = lax.axis_index("shard")
        seq = lax.axis_index("seq")
        self.n_shard = lax.axis_size("shard")
        self.n = lax.axis_size("seq") * self.n_shard
        core = shard & 1
        y = shard >> 1
        x = seq & 1
        bits = []
        bit = 1
        while bit < lax.axis_size("seq"):
            bits.append(bit)
            bit *= 2
        self.far = [self.n_shard * b for b in bits]
        here = [(seq >> i) & 1 for i in range(len(bits))]
        flag = (first_pos > 0).astype(jnp.int32)
        second = jnp.where(core == 0, x, y)
        self.token = ()
        self.info = jnp.stack([shard, x, flag, 1 - core, y, second] + here).astype(jnp.int32)

    def send(self, x, even, odd):
        pairs = [(i, i ^ (even if i % 2 == 0 else odd)) for i in range(self.n)]
        return lax.ppermute(x, ("seq", "shard"), pairs)


ORDER = ("d", "da", "da", "dab", "da", "b", "acbcbcbccb")


class Chain:
    def __init__(self, place):
        self.place = place
        self.keeps = []
        self.gots = []
        self.keep = None
        n = len(place.far)
        self.steps = [self.start, self.second]
        self.steps += [lambda i=i: self.halve(i) for i in range(1, n - 1)]
        self.steps += [self.exchange]
        self.steps += [lambda i=i: self.double(i) for i in range(n - 2, 1, -1)]
        self.steps += [self.spread]
        self.count = len(self.steps)

    def add(self, keep, send):
        self.keeps.append(keep.reshape(2, -1, 128))
        self.gots.append(self.place.send(send.reshape(2, -1, 128), 1, 1))

    def wait(self, *first):
        if not first:
            return
        if len(self.steps) == self.count:
            self.gots = [after(g, *first) for g in self.gots]
        else:
            self.got = after(self.got, *first)

    def step(self):
        if self.keep is None:
            self.keeps[0] = self.turn(self.keeps[0])
        else:
            self.keep = self.turn(self.keep)
        return self.steps.pop(0)()

    def go(self, out, even, odd):
        self.got = self.place.send(out, even, odd)
        self.place.token = (out,)

    def turn(self, x):
        return after(x, *self.place.token) if self.place.token else x

    def collect(self):
        self.place.token = tuple(self.parts)

    def start(self):
        out, self.keep = mix_first(self.place.info, self.keeps, self.gots)
        self.go(out, 2, self.place.far[0])
        return out

    def second(self):
        out, self.keep = mix_half(self.place.info, SECOND, self.keep, self.got)
        self.go(out, self.place.far[0], 2)
        return out

    def halve(self, i):
        keep, got = self.keep, self.got
        out, self.keep = mix_half(self.place.info, HERE + i, keep, got)
        self.go(out, self.place.far[i], self.place.far[i])
        return out

    def exchange(self):
        self.keep = mix_sum(self.place.info, self.keep, self.got)
        self.go(self.keep, self.place.far[-1], self.place.far[-1])
        return self.keep

    def settle(self, i):
        if i == len(self.place.far) - 2:
            self.keep = mix_sum(self.place.info, self.keep, self.got)
        else:
            self.keep = mix_both(self.place.info, HERE + i + 1, self.keep, self.got)

    def spread(self):
        self.settle(1)
        x, z = self.place.far[:2]
        self.place.token = (self.keep,)
        self.parts = [self.keep] + [self.place.send(self.keep, f, f) for f in (x, z, x + z)]

    def double(self, i):
        self.settle(i)
        self.go(self.keep, self.place.far[i], self.place.far[i])
        return self.keep


def gather_parts(info, parts, total):
    x, z = info[HERE], info[HERE + 1]
    for part, (i, j) in zip(parts, ((x, z), (1 - x, z), (x, 1 - z), (1 - x, 1 - z))):
        total[2 * i + j] = part[...]


def spread(o, total, at, rows, blocks):
    half = total.shape[1]
    for j in range(blocks):
        done = 0
        while done < rows:
            part, row = divmod(at + j * rows + done, half)
            n = min(rows - done, half - row)
            o[done : done + n, 128 * j : 128 * (j + 1)] = total[part, row : row + n, :].astype(o.dtype)
            done += n


def finish_one(info, parts):
    def body(i, *refs):
        down, total = refs[4:]
        gather_parts(i, refs[:4], total)
        spread(down, total, 0, FF // 4, D // 128)

    return pl.pallas_call(
        body,
        out_shape=hbm((FF // 4, D), F32),
        in_specs=[SM] + [VM] * 4,
        out_specs=VM,
        scratch_shapes=[pltpu.VMEM((4,) + parts[0].shape, BF16)],
        compiler_params=params(),
        cost_estimate=cost(1e7, 1e7),
        name="finish_one",
    )(info, *parts)


def finish_two(info, parts_a, parts_b):
    gr = D // 4
    blocks = FH // 128

    def body(i, *refs):
        gate, up, out, total_a, total_b = refs[8:]
        gather_parts(i, refs[:4], total_a)
        gather_parts(i, refs[4:8], total_b)
        for k, total in enumerate((total_a, total_b)):
            spread(gate.at[:, pl.ds(FH * k, FH)], total, 0, gr, blocks)
            spread(up.at[:, pl.ds(FH * k, FH)], total, gr * blocks, gr, blocks)
        spread(out, total_b, 2 * gr * blocks, HEAD_DIM, D // 128)

    return pl.pallas_call(
        body,
        out_shape=(hbm((gr, FF), F32), hbm((gr, FF), F32), hbm((HEAD_DIM, D), F32)),
        in_specs=[SM] + [VM] * 8,
        out_specs=(VM,) * 3,
        scratch_shapes=[
            pltpu.VMEM((4,) + parts_a[0].shape, BF16),
            pltpu.VMEM((4,) + parts_b[0].shape, BF16),
        ],
        compiler_params=params(),
        cost_estimate=cost(1e7, 1e7),
        name="finish_two",
    )(info, *parts_a, *parts_b)


def finish_three(info, parts, query_w, key_w, value_w, gain):
    gr = D // 4

    def body(i, *refs):
        wq, wk, wv, g, query, key, value, gains, first, total, prod = refs[4:]
        gather_parts(i, refs[:4], total)
        spread(query, total, 0, gr, 8)
        spread(key, total, 8 * gr, gr, 2)
        spread(value, total, 10 * gr, gr, 2)
        spread(gains, total, 12 * gr, 16, 2)
        base = HEADS * HEAD_DIM
        prod[:, :base] = query[...] * wq[...].astype(F32)
        prod[:, base : base + HEAD_DIM] = key[...] * wk[...].astype(F32)
        prod[:, base + HEAD_DIM :] = value[...] * wv[...].astype(F32)
        p = prod[...]
        high = p.astype(BF16)
        low = (p - high.astype(F32)).astype(BF16)
        ones = jnp.ones((16, 6 * HEAD_DIM), BF16)
        first[...] = (dot(ones, high, NT) + dot(ones, low, NT)) / g[...].astype(F32).reshape(1, -1)

    return pl.pallas_call(
        body,
        out_shape=(
            hbm((gr, HEADS * HEAD_DIM), F32),
            hbm((gr, HEAD_DIM), F32),
            hbm((gr, HEAD_DIM), F32),
            sds((16, HEAD_DIM), F32),
            sds((16, gr), F32),
        ),
        in_specs=[SM] + [VM] * 8,
        out_specs=(VM,) * 5,
        scratch_shapes=[
            pltpu.VMEM((4,) + parts[0].shape, BF16),
            pltpu.VMEM((gr, 6 * HEAD_DIM), F32),
        ],
        compiler_params=params(),
        cost_estimate=cost(1e7, 1e7),
        name="finish_three",
    )(info, *parts, query_w, key_w, value_w, gain)


def shards(
    tokens,
    query_weight,
    key_weight,
    value_weight,
    out_weight,
    gate_weight,
    up_weight,
    down_weight,
    input_gain,
    query_gain,
    key_gain,
    attended_gain,
    middle_gain,
    output_gain,
    cotangent,
):
    n_seq = lax.axis_size("seq")
    n_shard = lax.axis_size("shard")
    shard = lax.axis_index("shard")
    count = tokens.shape[0]
    total = count * n_seq * n_shard
    length = min(SEQ_CAP, total)
    rank = lax.axis_index("seq") * n_shard + shard
    first_pos = rank * count % length
    place = Place(first_pos)
    me = flag = place.info
    gd = D // 4
    gh = HEAD_DIM // 4

    kvg = pack(
        me,
        key_weight,
        value_weight,
        input_gain,
        attended_gain,
        middle_gain,
        output_gain,
        query_gain,
        key_gain,
    )
    def near(x):
        return flip(x, "shard", 1)

    def far(x):
        return flip(x, "shard", 2)

    q_far = far(query_weight)
    kvg_far = far(kvg)
    kvgs = (kvg, near(kvg), kvg_far, near(kvg_far))
    q_near = near(query_weight)
    out_near, gate_near, up_near, down_near = (
        near(out_weight), near(gate_weight), near(up_weight), near(down_weight)
    )

    def relay(x):
        return flip(x, "seq", 1)

    gate_half, up_half, down_half = halves(me, gate_weight, up_weight, down_weight)

    positions = first_pos + jnp.arange(count, dtype=jnp.int32)
    hd = HEAD_DIM // 2
    freq = ROPE_BASE ** (-(jnp.arange(hd, dtype=F32) * 2.0 / HEAD_DIM))
    angles = positions.astype(F32)[:, None] * freq[None, :]
    cos = jnp.cos(angles)
    sin = jnp.sin(angles)

    gains = gains_of(me, kvgs)
    kvgs = pinned(*kvgs)
    nin, kraw, kv_lo, kv_hi = pre_kv(me, tokens, gains, cos, sin, kvgs)
    ranks = n_seq * n_shard
    per_seq = length // count
    pairs = [(i, i + 1) for i in range(ranks - 1) if (i + 1) % per_seq]
    halo = lax.ppermute(kv_hi, ("seq", "shard"), pairs)
    out_far = far(out_weight)
    gate_a = far(gate_half)
    q_far = after(q_far, nin)
    qs_w = pinned(query_weight, q_near, q_far, near(q_far))
    up_a = far(after(up_half, gate_a))
    gate_b = relay(gate_a)
    qraw, qs = pre_q(me, nin, gains, cos, sin, qs_w)
    qs = after(qs, out_far, gate_a)
    o_hi, pm_hi, p1_hi = att(flag, qs, kv_lo, kv_hi, False, 1)
    o_lo, pm_lo, p1_lo = att(flag, after(qs, o_hi), halo, kv_lo, True, 0)
    gate_b = after(gate_b, o_lo)
    up_a = after(up_a, o_lo)
    down_a = far(after(down_half, up_a))
    up_b = relay(up_a)
    outs = pinned(out_weight, out_near, out_far, near(out_far))
    ap, nm = mid_part(me, o_lo, o_hi, tokens, gains, outs)
    gates = pinned(gate_weight, gate_near, gate_a, gate_b, near(gate_a), near(gate_b))
    act, slope = ff(me, nm, gates)
    up_b = after(up_b, act)
    down_a = after(down_a, act)
    down_b = relay(down_a)
    ups = pinned(up_weight, up_near, up_a, up_b, near(up_a), near(up_b))
    hid, bact = ff(me, nm, ups, (act, slope))
    down_b = after(down_b, hid)
    downs = pinned(down_weight, down_near, down_a, down_b, near(down_a), near(down_b))
    block_out, dd, wd, keep, send, gain_down = down_part(
        me, hid, tokens, cotangent, ap, gains, downs
    )
    chains = {name: Chain(place) for name in "abcd"}

    def advance(order, *first):
        for name in order:
            chain = chains[name.lower()]
            if name.isupper():
                chain.parts = [after(x, *first) for x in chain.parts]
                chain.collect()
            elif chain.steps:
                chain.wait(*first)
                chain.step()

    chains["d"].add(keep, send)
    keep, send, dnm = fb(me, nm, dd, act, bact, wd, gates, ups, 0, None)
    chains["a"].add(keep, send)
    advance(ORDER[0], dnm)
    dnm = after(dnm, *place.token)
    keep, send, dnm = fb(me, nm, dd, act, bact, wd, gates, ups, 1, dnm)
    chains["b"].add(keep, send)
    advance(ORDER[1], dnm)
    keep, send, d_o, d_mid, gain_mid = fe(
        me, o_lo, o_hi, tokens, cotangent, gains, ap, after(dnm, *place.token), outs
    )
    chains["b"].add(keep, send)
    advance(ORDER[2], d_o)
    dq_lo, kv_back, kv_a, gq_lo = att_back(
        qs, qraw, halo, kv_lo, pm_lo, p1_lo, after(d_o, *place.token), gains, cos, sin, 0
    )
    returned = lax.ppermute(kv_back, ("seq", "shard"), [(j, i) for i, j in pairs])
    advance(ORDER[3], dq_lo)
    dq_hi, kv_b, kv_c, gq_hi = att_back(
        qs, qraw, kv_lo, kv_hi, pm_hi, p1_hi, after(d_o, dq_lo, *place.token), gains, cos, sin, 1
    )
    advance(ORDER[4], dq_hi)
    dkv, keep, send = post(
        me,
        nin,
        (dq_lo, after(dq_hi, *place.token)),
        (kv_a, kv_b, kv_c, returned),
        kraw,
        gains,
        cos,
        sin,
        (gq_lo, gq_hi, gain_mid, gain_down),
    )
    chains["c"].add(keep, send)
    advance(ORDER[5], keep)
    grad_tokens = last(
        me, tokens, d_mid, (dq_lo, dq_hi), after(dkv, *place.token), gains, qs_w, kvgs
    )
    advance(ORDER[6], grad_tokens)
    for name in "dacb":
        advance(name * len(chains[name].steps))
    r_down = finish_one(me, chains["d"].parts)
    r_query, r_key, r_value, tail, first = finish_three(
        me,
        chains["c"].parts,
        query_weight,
        key_weight,
        value_weight,
        input_gain,
    )
    r_gate, r_up, r_out = finish_two(me, chains["a"].parts, chains["b"].parts)
    return (
        block_out,
        grad_tokens,
        r_query,
        r_key,
        r_value,
        r_out,
        r_gate,
        r_up,
        r_down,
        first[0],
        tail[4, :gh],
        tail[5, :gh],
        tail[1, :gd],
        tail[2, :gd],
        tail[3, :gd],
    )


def solution(mesh):
    token = P(("seq", "shard"), None)
    matrix = P("shard", None)
    vector = P("shard")
    in_specs = (token,) + (matrix,) * 7 + (vector,) * 6 + (token,)
    out_specs = (token, token) + (matrix,) * 7 + (vector,) * 6
    return jax.shard_map(shards, mesh=mesh, in_specs=in_specs, out_specs=out_specs, check_vma=False)
```

```python
import jax
import jax.numpy as jnp
from jax import lax
from jax.experimental import pallas as pl
from jax.experimental.pallas import tpu as pltpu
from jax.sharding import PartitionSpec as P

D = 640
HEADS = 4
HEAD_DIM = 256
FF = 2048
WINDOW = 512
SEQ_CAP = 8192
HALF = 512
QB = 256
ROWS = HEADS * QB
CHUNK = 512

EPS = 1e-06
ROPE_BASE = 10000.0
LOG2E = 1.4426950408889634
LN2 = 0.6931471805599453
SCALE = HEAD_DIM**-0.5

F32 = jnp.float32
BF16 = jnp.bfloat16
VM = pl.BlockSpec(memory_space=pltpu.VMEM)
SM = pl.BlockSpec(memory_space=pltpu.SMEM)
HM = pl.BlockSpec(memory_space=pltpu.HBM)
NN = (((1,), (0,)), ((), ()))
NT = (((1,), (1,)), ((), ()))
TN = (((0,), (0,)), ((), ()))


def dot(a, b, dims=NN):
    return lax.dot_general(a, b, dims, preferred_element_type=F32)


def params(mib=14):
    return pltpu.CompilerParams(vmem_limit_bytes=mib * 2**20)


def sds(shape, dtype=BF16):
    return jax.ShapeDtypeStruct(shape, dtype)


def cost(flops, nbytes):
    return pl.CostEstimate(flops=int(flops), bytes_accessed=int(nbytes), transcendentals=0)


def rms_factor(v):
    return lax.rsqrt(jnp.mean(v * v, axis=-1, keepdims=True) + EPS)


def norm_back(v, factor, gain, incoming):
    united = v * factor
    scaled = incoming * gain
    back = factor * (scaled - united * jnp.mean(scaled * united, axis=-1, keepdims=True))
    return back, jnp.sum(incoming * united, axis=0, keepdims=True)


def offsets(me, rows):
    return (
        me * rows,
        (me + 1 - 2 * (me % 2)) * rows,
        ((me + 2) % 4) * rows,
        (3 - me) * rows,
    )


def hbm(shape, dtype=BF16):
    return pltpu.HBM(shape, dtype)


ME, XBIT, FLAG, EVEN, YBIT, SECOND, HERE = range(7)


def pin(x):
    return pltpu.with_memory_space_constraint(x, pltpu.HBM)


def pinned(*arrays):
    return tuple(pin(x) for x in arrays)


def whole(piece):
    return piece


def place_copies(me_ref, pieces, src_of, buf, rows, sems, first):
    me, b = me_ref[ME], me_ref[XBIT]
    spots = [(p, o, rows) for p, o in zip(pieces, offsets(me, rows))]
    if len(pieces) == 6:
        part = rows // 2
        far, last = spots[2][1], spots[3][1]
        spots = spots[:2]
        for base, p in ((far, pieces[2:4]), (last, pieces[4:6])):
            spots.append((p[0], base + b * part, part))
            spots.append((p[1], base + (1 - b) * part, part))
    copies = []
    for k, (piece, off, n) in enumerate(spots):
        copies.append(
            pltpu.make_async_copy(
                src_of(piece), buf.at[pl.ds(pl.multiple_of(off, 16), n)], sems.at[first + k]
            )
        )
    return copies


def pack_kernel(info, k, v, g0, g1, g2, g3, g4, g5, out, r0, r1, r2, r3, r4, r5, sems):
    rows = D // 4
    gains = (g0, g1, g2, g3, g4, g5)
    places = (r0, r1, r2, r3, r4, r5)
    copies = [
        pltpu.make_async_copy(k, out.at[pl.ds(0, rows), pl.ds(0, HEAD_DIM)], sems.at[0]),
        pltpu.make_async_copy(v, out.at[pl.ds(0, rows), pl.ds(HEAD_DIM, HEAD_DIM)], sems.at[1]),
    ]
    for i in range(6):
        copies.append(pltpu.make_async_copy(gains[i], places[i], sems.at[2 + i]))
    for c in copies:
        c.start()
    out[rows:, :] = jnp.zeros((16, 2 * HEAD_DIM), BF16)
    for c in copies:
        c.wait()
    for i, r in enumerate(places):
        out[rows + i : rows + i + 1, : r.shape[0]] = r[...].reshape(1, -1)


def pack(info, k, v, *gains):
    return pl.pallas_call(
        pack_kernel,
        out_shape=sds((D // 4 + 16, 2 * HEAD_DIM)),
        in_specs=[SM] + [HM] * 8,
        out_specs=VM,
        scratch_shapes=[pltpu.VMEM(g.shape, BF16) for g in gains] + [pltpu.SemaphoreType.DMA((8,))],
        compiler_params=params(),
        cost_estimate=cost(1e6, 4e5),
        name="pack",
    )(info, *(pin(w) for w in (k, v) + gains))


def halves_kernel(info, *refs):
    n = len(refs) // 2
    ins, outs, sems = refs[:n], refs[n : 2 * n], refs[2 * n]
    copies = []
    for i, (w, o) in enumerate(zip(ins, outs)):
        rows = w.shape[0] // 2
        at = pl.multiple_of(info[XBIT] * rows, 16)
        copies.append(pltpu.make_async_copy(w.at[pl.ds(at, rows)], o, sems.at[i]))
    for c in copies:
        c.start()
    for c in copies:
        c.wait()


def halves(info, *weights):
    return pl.pallas_call(
        halves_kernel,
        out_shape=tuple(sds((w.shape[0] // 2, w.shape[1])) for w in weights),
        in_specs=[SM] + [HM] * len(weights),
        out_specs=(VM,) * len(weights),
        scratch_shapes=[pltpu.SemaphoreType.DMA((len(weights),))],
        compiler_params=params(),
        cost_estimate=cost(1e6, 2e6),
        name="halves",
    )(info, *(pin(w) for w in weights))


def gains_kernel(me_ref, g0, g1, g2, g3, out):
    gd = D // 4
    gh = HEAD_DIM // 4
    wide = jnp.zeros((16, D), F32)
    small = jnp.zeros((16, HEAD_DIM), F32)
    spots = offsets(me_ref[ME], 1)
    for spot, g in zip(spots, (g0, g1, g2, g3)):
        piece = g[...]
        row = lax.broadcasted_iota(jnp.int32, (HEAD_DIM, D), 0)
        col = lax.broadcasted_iota(jnp.int32, (HEAD_DIM, D), 1)
        place = ((col == row + spot * gd) & (row < gd)).astype(BF16)
        wide = wide + dot(piece, place)
        row = lax.broadcasted_iota(jnp.int32, (HEAD_DIM, HEAD_DIM), 0)
        col = lax.broadcasted_iota(jnp.int32, (HEAD_DIM, HEAD_DIM), 1)
        place = ((col == row + spot * gh) & (row < gh)).astype(BF16)
        small = small + dot(piece, place)
    out[0:4, :] = wide[0:4, :]
    out[4:8, :] = jnp.zeros((4, D), F32)
    out[4:8, :HEAD_DIM] = small[4:8, :]


def gains_of(me, pieces):
    part = pl.BlockSpec((16, HEAD_DIM), lambda i: (D // 4 // 16, 0))
    return pl.pallas_call(
        gains_kernel,
        grid=(1,),
        out_shape=sds((8, D), F32),
        in_specs=[SM] + [part] * 4,
        out_specs=VM,
        compiler_params=params(),
        cost_estimate=cost(1e8, 1e5),
        name="gains",
    )(me, *pieces)


def rotated(u, cos, sin):
    hd = HEAD_DIM // 2
    u1 = u[:, :hd]
    u2 = u[:, hd:]
    return (u1 * cos - u2 * sin).astype(BF16), (u2 * cos + u1 * sin).astype(BF16)


def pre_kv_kernel(me_ref, tok, gains, cos_ref, sin_ref, w0, w1, w2, w3, nin_o, kraw_o, lo_o, hi_o, wbuf, sems):
    rows = D // 4
    copies = place_copies(
        me_ref, (w0, w1, w2, w3), lambda w: w.at[pl.ds(0, rows)], wbuf, rows, sems, 0
    )
    for c in copies:
        c.start()
    hd = HEAD_DIM // 2
    x = tok[...].astype(F32)
    nin = (x * rms_factor(x) * gains[0:1, :]).astype(BF16)
    nin_o[...] = nin
    for c in copies:
        c.wait()
    k = dot(nin, wbuf[:, :HEAD_DIM])
    kraw_o[...] = k.astype(BF16)
    r1, r2 = rotated(k * rms_factor(k) * gains[5:6, :HEAD_DIM], cos_ref[...], sin_ref[...])
    v = dot(nin, wbuf[:, HEAD_DIM:]).astype(BF16)
    for half, o in enumerate((lo_o, hi_o)):
        sl = slice(HALF * half, HALF * (half + 1))
        o[:, :hd] = r1[sl]
        o[:, hd:HEAD_DIM] = r2[sl]
        o[:, HEAD_DIM:] = v[sl]


def pre_kv(me, tok, gains, cos, sin, pieces):
    t = tok.shape[0]
    return pl.pallas_call(
        pre_kv_kernel,
        out_shape=(
            sds((t, D)),
            sds((t, HEAD_DIM)),
            sds((HALF, 2 * HEAD_DIM)),
            sds((HALF, 2 * HEAD_DIM)),
        ),
        in_specs=[SM, VM, VM, VM, VM, HM, HM, HM, HM],
        out_specs=(VM,) * 4,
        scratch_shapes=[pltpu.VMEM((D, 2 * HEAD_DIM), BF16), pltpu.SemaphoreType.DMA((4,))],
        compiler_params=params(),
        cost_estimate=cost(2 * t * D * 512, 5e6),
        name="pre_kv",
    )(me, tok, gains, cos, sin, *pieces)


def pre_q_kernel(me_ref, nin_i, gains, cos_ref, sin_ref, w0, w1, w2, w3, qraw_o, qs_o, wbuf, sems):
    rows = D // 4
    hd = HEAD_DIM // 2

    @pl.when(pl.program_id(0) == 0)
    def _():
        copies = place_copies(
            me_ref, (w0, w1, w2, w3), lambda w: w.at[pl.ds(0, rows)], wbuf, rows, sems, 0
        )
        for c in copies:
            c.start()
        for c in copies:
            c.wait()

    q = dot(nin_i[...], wbuf[:, pl.ds(pl.multiple_of(pl.program_id(0) * HEAD_DIM, HEAD_DIM), HEAD_DIM)])
    qraw_o[0] = q.astype(BF16)
    u = q * (rms_factor(q) * (SCALE * LOG2E)) * gains[4:5, :HEAD_DIM]
    r1, r2 = rotated(u, cos_ref[...], sin_ref[...])
    qs_o[0, :, :hd] = r1
    qs_o[0, :, hd:] = r2


def pre_q(me, nin, gains, cos, sin, pieces):
    t = nin.shape[0]
    head = pl.BlockSpec((1, t, HEAD_DIM), lambda h: (h, 0, 0))
    return pl.pallas_call(
        pre_q_kernel,
        grid=(HEADS,),
        out_shape=(hbm((HEADS, t, HEAD_DIM)), sds((HEADS, t, HEAD_DIM))),
        in_specs=[SM, VM, VM, VM, VM, HM, HM, HM, HM],
        out_specs=(head, head),
        scratch_shapes=[pltpu.VMEM((D, HEADS * HEAD_DIM), BF16), pltpu.SemaphoreType.DMA((4,))],
        compiler_params=params(),
        cost_estimate=cost(2 * t * D * 1024, 5e6),
        name="pre_q",
    )(me, nin, gains, cos, sin, *pieces)


def key_blocks(j, kvp, kvs, lo, hi):
    blocks = (kvp[0:QB, lo:hi], kvp[QB : 2 * QB, lo:hi], kvs[0:QB, lo:hi], kvs[QB : 2 * QB, lo:hi])
    return blocks[j : j + 3]


def upper_mask():
    row = lax.broadcasted_iota(jnp.int32, (HEADS, QB, QB), 1).reshape(ROWS, QB)
    col = lax.broadcasted_iota(jnp.int32, (ROWS, QB), 1)
    return col > row


def att_kernel(masked, flag_ref, qs, kvp, kvs, o_o, pm_o, p1_o):
    upper = upper_mask()
    for j in range(2):
        sl = slice(QB * j, QB * (j + 1))
        q = qs[:, sl, :].reshape(ROWS, HEAD_DIM)
        k0, k1, k2 = key_blocks(j, kvp, kvs, 0, HEAD_DIM)
        v0, v1, v2 = key_blocks(j, kvp, kvs, HEAD_DIM, 2 * HEAD_DIM)
        em = jnp.exp2(jnp.where(upper, dot(q, k0, NT), dot(q, k2, NT)))
        e1 = jnp.exp2(dot(q, k1, NT))
        if masked:
            keep = flag_ref[FLAG].astype(F32)
            em = em * jnp.where(upper, keep, 1.0)
            if j == 0:
                e1 = e1 * keep
        inv = 1.0 / jnp.sum(em + e1, axis=-1, keepdims=True)
        pm = (em * inv).astype(BF16)
        p1 = (e1 * inv).astype(BF16)
        zero = jnp.zeros_like(pm)
        out = dot(p1, v1) + dot(jnp.where(upper, pm, zero), v0) + dot(jnp.where(upper, zero, pm), v2)
        pm_o[:, sl, :] = pm.reshape(HEADS, QB, QB)
        p1_o[:, sl, :] = p1.reshape(HEADS, QB, QB)
        for h in range(HEADS):
            o_o[sl, HEAD_DIM * h : HEAD_DIM * (h + 1)] = out[QB * h : QB * (h + 1), :].astype(BF16)


def half_spec(half):
    return pl.BlockSpec((HEADS, HALF, HEAD_DIM), lambda i: (0, half, 0))


def att(flag, qs, kvp, kvs, masked, half):
    shp = sds((HEADS, HALF, HEAD_DIM))

    def body(*refs):
        att_kernel(masked, *refs)

    return pl.pallas_call(
        body,
        grid=(1,),
        out_shape=(sds((HALF, HEADS * HEAD_DIM)), shp, shp),
        in_specs=[SM, half_spec(half), VM, VM],
        out_specs=(VM,) * 3,
        compiler_params=params(),
        cost_estimate=cost(12e9 / 4, 5e6),
        name="att",
    )(flag, qs, kvp, kvs)


def att_back_kernel(qs, qraw, kvp, kvs, pm_i, p1_i, do_i, gains, cos_ref, sin_ref, dq_o, dkvp_o, dkvs_o, gain_o, acc):
    upper = upper_mask()
    hd = HEAD_DIM // 2
    acc[...] = jnp.zeros_like(acc)
    gsum = jnp.zeros((1, HEAD_DIM), F32)
    for j in range(2):
        sl = slice(QB * j, QB * (j + 1))
        q = qs[:, sl, :].reshape(ROWS, HEAD_DIM)
        do = do_i[:, sl, :].reshape(ROWS, HEAD_DIM)
        k0, k1, k2 = key_blocks(j, kvp, kvs, 0, HEAD_DIM)
        v0, v1, v2 = key_blocks(j, kvp, kvs, HEAD_DIM, 2 * HEAD_DIM)
        pmb = pm_i[:, sl, :].reshape(ROWS, QB)
        p1b = p1_i[:, sl, :].reshape(ROWS, QB)
        dpm = jnp.where(upper, dot(do, v0, NT), dot(do, v2, NT))
        dp1 = dot(do, v1, NT)
        pm = pmb.astype(F32)
        p1 = p1b.astype(F32)
        total = jnp.sum(pm * dpm + p1 * dp1, axis=-1, keepdims=True)
        dsm = (pm * (dpm - total)).astype(BF16)
        ds1 = (p1 * (dp1 - total)).astype(BF16)
        zero = jnp.zeros_like(dsm)
        ds0 = jnp.where(upper, dsm, zero)
        ds2 = jnp.where(upper, zero, dsm)
        p0 = jnp.where(upper, pmb, zero)
        p2 = jnp.where(upper, zero, pmb)
        for t, (ds, p) in enumerate(((ds0, p0), (ds1, p1b), (ds2, p2))):
            at = slice(QB * (j + t), QB * (j + t + 1))
            acc[at, :HEAD_DIM] += dot(ds, q, TN) * LN2
            acc[at, HEAD_DIM:] += dot(p, do, TN)
        dq = (dot(ds0, k0) + dot(ds1, k1) + dot(ds2, k2)) * SCALE
        cos = cos_ref[sl, :]
        sin = sin_ref[sl, :]
        gain = gains[4:5, :HEAD_DIM]
        for h in range(HEADS):
            d1 = dq[QB * h : QB * (h + 1), :hd]
            d2 = dq[QB * h : QB * (h + 1), hd:]
            inc = jnp.concatenate([d1 * cos + d2 * sin, d2 * cos - d1 * sin], axis=-1)
            raw = qraw[h, sl, :].astype(F32)
            back, terms = norm_back(raw, rms_factor(raw), gain, inc)
            gsum = gsum + terms
            dq_o[sl, HEAD_DIM * h : HEAD_DIM * (h + 1)] = back.astype(BF16)
    dkvp_o[...] = acc[:HALF, :].astype(BF16)
    dkvs_o[...] = acc[HALF:, :]
    gain_o[...] = jnp.broadcast_to(gsum, (8, HEAD_DIM))


def att_back(qs, qraw, kvp, kvs, pm, p1, do, gains, cos, sin, half):
    dospec = half_spec(half)
    tab = pl.BlockSpec((HALF, HEAD_DIM // 2), lambda i: (half, 0))
    return pl.pallas_call(
        att_back_kernel,
        grid=(1,),
        out_shape=(
            sds((HALF, HEADS * HEAD_DIM)),
            sds((HALF, 2 * HEAD_DIM)),
            sds((HALF, 2 * HEAD_DIM), F32),
            sds((8, HEAD_DIM), F32),
        ),
        in_specs=[dospec, dospec, VM, VM, VM, VM, dospec, VM, tab, tab],
        out_specs=(VM,) * 4,
        scratch_shapes=[pltpu.VMEM((2 * HALF, 2 * HEAD_DIM), F32)],
        compiler_params=params(),
        cost_estimate=cost(24e9 / 4, 9e6),
        name="att_back",
    )(qs, qraw, kvp, kvs, pm, p1, do, gains, cos, sin)


def mid_kernel(me_ref, o_lo, o_hi, tok, gains, w0, w1, w2, w3, ap_o, nm_o, wo, sems):
    ro = HEADS * HEAD_DIM // 4
    copies = place_copies(me_ref, (w0, w1, w2, w3), lambda w: w, wo, ro, sems, 0)
    for c in copies:
        c.start()
    for c in copies:
        c.wait()
    for half, o in enumerate((o_lo, o_hi)):
        sl = slice(HALF * half, HALF * (half + 1))
        proj = dot(o[...], wo[...])
        ap_o[sl, :] = proj.astype(BF16)
        mid = tok[sl, :].astype(F32) + proj * rms_factor(proj) * gains[1:2, :]
        nm_o[sl, :] = (mid * rms_factor(mid) * gains[2:3, :]).astype(BF16)


def mid_part(me, o_lo, o_hi, tok, gains, outs):
    t = tok.shape[0]
    return pl.pallas_call(
        mid_kernel,
        out_shape=(sds((t, D)), sds((t, D))),
        in_specs=[SM] + [VM] * 4 + [HM] * 4,
        out_specs=(VM, VM),
        scratch_shapes=[
            pltpu.VMEM((HEADS * HEAD_DIM, D), BF16),
            pltpu.SemaphoreType.DMA((4,)),
        ],
        compiler_params=params(),
        cost_estimate=cost(2 * t * D * 1024, 8e6),
        name="mid",
    )(me, o_lo, o_hi, tok, gains, *outs)


FH = FF // 2
STEP = 512
WIDE = 512
RB = 512


def by_columns(me_ref, pieces, buf, sems, body):
    def copies(i):
        at = pl.ds(pl.multiple_of(i * STEP, STEP), STEP)
        return place_copies(
            me_ref, pieces, lambda w: w.at[:, at], buf.at[:, at], D // 4, sems, 6 * i
        )

    for i in range(FF // STEP):
        for c in copies(i):
            c.start()

    def step(i, carry):
        for c in copies(i):
            c.wait()
        body(pl.ds(pl.multiple_of(i * STEP, STEP), STEP))
        return carry

    lax.fori_loop(0, FF // STEP, step, 0)


def gate_kernel(me_ref, nm, *rest):
    pieces, (a_o, s_o, wg, sems) = rest[:6], rest[6:]
    c0 = 0.7978845608028654
    c1 = 0.044715 * c0

    def body(cs):
        for r in range(0, nm.shape[0], RB):
            rs = slice(r, r + RB)
            g = dot(nm[rs, :], wg[:, cs]).astype(BF16)
            g2 = g * g
            t = jnp.tanh(g * (c0 + c1 * g2))
            h = 0.5 + 0.5 * t
            a = g * h
            a_o[rs, cs] = a
            s_o[rs, cs] = h + a * (1.0 - h) * (2.0 * c0 + (6.0 * c1) * g2)

    by_columns(me_ref, pieces, wg, sems, body)


def up_kernel(me_ref, nm, a_i, s_i, *rest):
    pieces, (hid_o, b_o, wu, sems) = rest[:6], rest[6:]

    def body(cs):
        for r in range(0, nm.shape[0], RB):
            rs = slice(r, r + RB)
            u = dot(nm[rs, :], wu[:, cs]).astype(BF16)
            hid_o[rs, cs] = a_i[rs, cs] * u
            b_o[rs, cs] = u * s_i[rs, cs]

    by_columns(me_ref, pieces, wu, sems, body)


def ff(me, nm, pieces, before=()):
    t = nm.shape[0]
    return pl.pallas_call(
        up_kernel if before else gate_kernel,
        out_shape=(sds((t, FF)),) * 2,
        in_specs=[SM, VM] + [VM] * len(before) + [HM] * 6,
        out_specs=(VM,) * 2,
        scratch_shapes=[pltpu.VMEM((D, FF), BF16), pltpu.SemaphoreType.DMA((6 * FF // STEP,))],
        compiler_params=params(),
        cost_estimate=cost(2 * t * D * FF, 12e6),
        name="up" if before else "gate",
    )(me, nm, *before, *pieces)


def down_kernel(me_ref, hid, tok, cot, ap, gains, *rest):
    pieces, (out_o, dd_o, wd_o, keep_o, send_o, gain_o, sems) = rest[:6], rest[6:]
    rf = FF // 4
    core = me_ref[ME] % 2
    copies = place_copies(me_ref, pieces, whole, wd_o, rf, sems, 0)
    for c in copies:
        c.start()
    for c in copies:
        c.wait()
    gsum = jnp.zeros((1, D), F32)
    for half in range(2):
        sl = slice(HALF * half, HALF * (half + 1))
        dn = dot(hid[sl, :], wd_o[...])
        proj = ap[sl, :].astype(F32)
        mid = tok[sl, :].astype(F32) + proj * rms_factor(proj) * gains[1:2, :]
        fac = rms_factor(dn)
        out_o[sl, :] = (mid + dn * fac * gains[3:4, :]).astype(BF16)
        back, terms = norm_back(dn, fac, gains[3:4, :], cot[sl, :].astype(F32))
        dd_o[sl, :] = back.astype(BF16)
        gsum = gsum + terms
    gain_o[...] = jnp.broadcast_to(gsum, (8, D))
    for y in range(2):
        for part, o in ((core, keep_o), (1 - core, send_o)):
            at = pl.ds(pl.multiple_of((2 * y + part) * rf, rf), rf)
            g = dot(hid[:, at], dd_o[...], TN).astype(BF16)
            for j in range(D // 128):
                o[y, j] = g[:, 128 * j : 128 * (j + 1)]


def down_part(me, hid, tok, cot, ap, gains, pieces):
    t = tok.shape[0]
    return pl.pallas_call(
        down_kernel,
        out_shape=(
            sds((t, D)),
            sds((t, D)),
            sds((FF, D)),
            sds((2, D // 128, FF // 4, 128)),
            sds((2, D // 128, FF // 4, 128)),
            sds((8, D), F32),
        ),
        in_specs=[SM] + [VM] * 5 + [HM] * 6,
        out_specs=(VM,) * 6,
        scratch_shapes=[pltpu.SemaphoreType.DMA((6,))],
        compiler_params=params(),
        cost_estimate=cost(4 * t * D * FF, 20e6),
        name="down",
    )(me, hid, tok, cot, ap, gains, *pieces)


def fb_kernel(half, me_ref, nm, dd, a_i, b_i, wd, *rest):
    gates, ups, rest = rest[:6], rest[6:12], rest[12:]
    first = half == 0
    if first:
        keep_o, send_o, dnm_o, wg, wu, gs, sems = rest
    else:
        dnm_i, keep_o, send_o, dnm_o, wg, wu, gs, sems = rest
    core = me_ref[ME] % 2

    copies = []
    for k, (pieces, buf) in enumerate(((gates, wg), (ups, wu))):
        copies += place_copies(
            me_ref, pieces, lambda w: w.at[:, pl.ds(FH * half, FH)], buf, D // 4, sems, 6 * k
        )
    for c in copies:
        c.start()
    gr = D // 4
    for i in range(FH // WIDE):
        cs = slice(WIDE * i, WIDE * (i + 1))
        at = slice(FH * half + WIDE * i, FH * half + WIDE * (i + 1))
        dh = dot(dd[...], wd[at, :], NT).astype(BF16)
        dg = dh * b_i[:, at]
        du = dh * a_i[:, at]
        for k, d in enumerate((dg, du)):
            gs[k] = dot(nm[...], d, TN).astype(BF16)
            for y in range(2):
                for part, o in ((core, keep_o), (1 - core, send_o)):
                    rows = pl.ds(pl.multiple_of((2 * y + part) * gr, gr), gr)
                    for j in range(WIDE // 128):
                        to = WIDE // 128 * i + j
                        o[y, k, to] = gs[k, rows, 128 * j : 128 * (j + 1)]
        if i == 0:
            for c in copies:
                c.wait()
        back = dot(dg, wg[:, cs], NT) + dot(du, wu[:, cs], NT)
        if i > 0:
            dnm_o[...] += back
        elif first:
            dnm_o[...] = back
        else:
            dnm_o[...] = dnm_i[...] + back


def fb(me, nm, dd, a, b, wd, gates, ups, part, dnm):
    t = nm.shape[0]
    extra = () if dnm is None else (dnm,)

    def body(*refs):
        fb_kernel(part, *refs)

    return pl.pallas_call(
        body,
        out_shape=(sds((2, 2, FH // 128, D // 4, 128)),) * 2 + (sds((t, D), F32),),
        in_specs=[SM] + [VM] * 5 + [HM] * 12 + [VM] * len(extra),
        out_specs=(VM,) * 3,
        scratch_shapes=[
            pltpu.VMEM((D, FH), BF16),
            pltpu.VMEM((D, FH), BF16),
            pltpu.VMEM((2, D, WIDE), BF16),
            pltpu.SemaphoreType.DMA((12,)),
        ],
        compiler_params=params(16),
        cost_estimate=cost(10 * t * D * FH, 16e6),
        name="fb",
    )(me, nm, dd, a, b, wd, *gates, *ups, *extra)


def fe_kernel(me_ref, o_lo, o_hi, tok, cot, gains, ap, dnm, w0, w1, w2, w3, keep_o, send_o, do_o, dmid_o, gain_o, wo, datt, sems):
    ro = HEADS * HEAD_DIM // 4
    copies = place_copies(me_ref, (w0, w1, w2, w3), lambda w: w, wo, ro, sems, 0)
    for c in copies:
        c.start()
    gm = jnp.zeros((1, D), F32)
    ga = jnp.zeros((1, D), F32)
    for half in range(2):
        sl = slice(HALF * half, HALF * (half + 1))
        proj = ap[sl, :].astype(F32)
        pfac = rms_factor(proj)
        mid = tok[sl, :].astype(F32) + proj * pfac * gains[1:2, :]
        back, terms = norm_back(mid, rms_factor(mid), gains[2:3, :], dnm[sl, :])
        dmid = cot[sl, :].astype(F32) + back
        gm = gm + terms
        dmid_o[sl, :] = dmid.astype(BF16)
        back, terms = norm_back(proj, pfac, gains[1:2, :], dmid)
        ga = ga + terms
        datt[sl, :] = back.astype(BF16)
    gain_o[0:8, :] = jnp.broadcast_to(gm, (8, D))
    gain_o[8:16, :] = jnp.broadcast_to(ga, (8, D))
    for c in copies:
        c.wait()
    for h in range(HEADS):
        at = slice(HEAD_DIM * h, HEAD_DIM * (h + 1))
        do_o[h] = dot(datt[...], wo[at, :], NT).astype(BF16)
    core = me_ref[ME] % 2
    for y in range(2):
        for part, o in ((core, keep_o), (1 - core, send_o)):
            cs = pl.ds(pl.multiple_of((2 * y + part) * HEAD_DIM, HEAD_DIM), HEAD_DIM)
            g = dot(o_lo[:, cs], datt[:HALF, :], TN) + dot(o_hi[:, cs], datt[HALF:, :], TN)
            g = g.astype(BF16)
            for j in range(D // 128):
                o[y, j] = g[:, 128 * j : 128 * (j + 1)]


def fe(me, o_lo, o_hi, tok, cot, gains, ap, dnm, outs):
    t = tok.shape[0]
    return pl.pallas_call(
        fe_kernel,
        out_shape=(
            sds((2, D // 128, HEAD_DIM, 128)),
            sds((2, D // 128, HEAD_DIM, 128)),
            sds((HEADS, t, HEAD_DIM)),
            sds((t, D)),
            sds((16, D), F32),
        ),
        in_specs=[SM] + [VM] * 7 + [HM] * 4,
        out_specs=(VM,) * 5,
        scratch_shapes=[
            pltpu.VMEM((HEADS * HEAD_DIM, D), BF16),
            pltpu.VMEM((t, D), BF16),
            pltpu.SemaphoreType.DMA((4,)),
        ],
        compiler_params=params(),
        cost_estimate=cost(4 * t * D * 1024, 14e6),
        name="fe",
    )(me, o_lo, o_hi, tok, cot, gains, ap, dnm, *outs)


LAST = 2048


def post_kernel(
    me_ref, nin, dq_lo, dq_hi, kv_a, kv_b, kv_c, kv_d, kraw,
    gains, cos_ref, sin_ref, gq_lo, gq_hi, gmid, gdown,
    dkv, keep_o, send_o,
    gs, sums, small,
):
    rows = D // 4
    hd = HEAD_DIM // 2
    gk = jnp.zeros((1, HEAD_DIM), F32)
    for half, (first, second) in enumerate(((kv_a, kv_b), (kv_c, kv_d))):
        sl = slice(HALF * half, HALF * (half + 1))
        both = first[...].astype(F32) + second[...].astype(F32)
        cos = cos_ref[sl, :]
        sin = sin_ref[sl, :]
        d1 = both[:, :hd]
        d2 = both[:, hd:HEAD_DIM]
        inc = jnp.concatenate([d1 * cos + d2 * sin, d2 * cos - d1 * sin], axis=-1)
        raw = kraw[sl, :].astype(F32)
        back, terms = norm_back(raw, rms_factor(raw), gains[5:6, :HEAD_DIM], inc)
        gk = gk + terms
        dkv[sl, :HEAD_DIM] = back.astype(BF16)
        dkv[sl, HEAD_DIM:] = both[:, HEAD_DIM:].astype(BF16)

    core = me_ref[ME] % 2

    def put(slot, g):
        gs[slot] = g.astype(BF16)
        for y in range(2):
            for part, o in ((core, keep_o), (1 - core, send_o)):
                at = pl.ds(pl.multiple_of((2 * y + part) * rows, rows), rows)
                for j in range(2):
                    to = (2 * slot + j) * rows
                    o[y, to : to + rows, :] = gs[slot, at, 128 * j : 128 * (j + 1)]

    for h in range(HEADS):
        cs = slice(HEAD_DIM * h, HEAD_DIM * (h + 1))
        put(h, dot(nin[:HALF, :], dq_lo[:, cs], TN) + dot(nin[HALF:, :], dq_hi[:, cs], TN))
    put(HEADS, dot(nin[...], dkv[:, :HEAD_DIM], TN))
    put(HEADS + 1, dot(nin[...], dkv[:, HEAD_DIM:], TN))
    sums[...] = jnp.zeros_like(sums)
    small[...] = jnp.zeros_like(small)
    sums[1:2, :] = gmid[8:9, :]
    sums[2:3, :] = gmid[0:1, :]
    sums[3:4, :] = gdown[0:1, :]
    small[4:5, :] = gq_lo[0:1, :] + gq_hi[0:1, :]
    small[5:6, :] = gk
    gd = D // 4
    gh = HEAD_DIM // 4
    base = 12 * rows
    for y in range(2):
        for part, o in ((core, keep_o), (1 - core, send_o)):
            s = 2 * y + part
            row = lax.broadcasted_iota(jnp.int32, (D, HEAD_DIM), 0)
            col = lax.broadcasted_iota(jnp.int32, (D, HEAD_DIM), 1)
            place = ((row == col + s * gd) & (col < gd)).astype(BF16)
            g = dot(sums[...].astype(BF16), place)
            row = lax.broadcasted_iota(jnp.int32, (HEAD_DIM, HEAD_DIM), 0)
            col = lax.broadcasted_iota(jnp.int32, (HEAD_DIM, HEAD_DIM), 1)
            place = ((row == col + s * gh) & (col < gh)).astype(BF16)
            g = (g + dot(small[...].astype(BF16), place)).astype(BF16)
            o[y, base : base + 16, :] = g[:, :128]
            o[y, base + 16 : base + 32, :] = g[:, 128:]
            o[y, base + 32 :, :] = jnp.zeros((LAST - base - 32, 128), BF16)


def post(me, nin, dqs, kvs, kraw, gains, cos, sin, sums):
    t = nin.shape[0]
    return pl.pallas_call(
        post_kernel,
        out_shape=(
            sds((t, 2 * HEAD_DIM)),
            sds((2, LAST, 128)),
            sds((2, LAST, 128)),
        ),
        in_specs=[SM] + [VM] * 15,
        out_specs=(VM,) * 3,
        scratch_shapes=[
            pltpu.VMEM((HEADS + 2, D, HEAD_DIM), BF16),
            pltpu.VMEM((16, D), F32),
            pltpu.VMEM((16, HEAD_DIM), F32),
        ],
        compiler_params=params(),
        cost_estimate=cost(2e9, 10e6),
        name="post",
    )(me, nin, *dqs, *kvs, kraw, gains, cos, sin, *sums)


def last_kernel(me_ref, tok, dmid, dq_lo, dq_hi, dkv, gains, q0, q1, q2, q3, k0, k1, k2, k3, gt_o, wq, wkv, sems):
    rows = D // 4
    copies = place_copies(me_ref, (q0, q1, q2, q3), whole, wq, rows, sems, 0)
    copies += place_copies(
        me_ref, (k0, k1, k2, k3), lambda w: w.at[pl.ds(0, rows)], wkv, rows, sems, 4
    )
    for c in copies:
        c.start()
    for c in copies:
        c.wait()
    for half, dq in enumerate((dq_lo, dq_hi)):
        for r in range(0, HALF, RB):
            rs = slice(HALF * half + r, HALF * half + r + RB)
            dnin = dot(dq[r : r + RB, :], wq[...], NT) + dot(dkv[rs, :], wkv[...], NT)
            x = tok[rs, :].astype(F32)
            back, _ = norm_back(x, rms_factor(x), gains[0:1, :], dnin)
            gt_o[rs, :] = (dmid[rs, :].astype(F32) + back).astype(BF16)


def last(me, tok, dmid, dqs, dkv, gains, qs, kvgs):
    t = tok.shape[0]
    return pl.pallas_call(
        last_kernel,
        out_shape=hbm((t, D)),
        in_specs=[SM] + [VM] * 6 + [HM] * 8,
        out_specs=VM,
        scratch_shapes=[
            pltpu.VMEM((D, HEADS * HEAD_DIM), BF16),
            pltpu.VMEM((D, 2 * HEAD_DIM), BF16),
            pltpu.SemaphoreType.DMA((8,)),
        ],
        compiler_params=params(),
        cost_estimate=cost(2e9, 8e6),
        name="last",
    )(me, tok, dmid, *dqs, dkv, gains, *qs, *kvgs)


def flip(x, axis, bit):
    n = lax.axis_size(axis)
    return lax.ppermute(x, axis, [(i, i ^ bit) for i in range(n)])


def pick(x, index, axis=0):
    return lax.dynamic_index_in_dim(x, index, axis, keepdims=False)


def after(x, *first):
    return lax.optimization_barrier((x,) + first)[0]


def joined(a, b):
    return (a.astype(F32) + b.astype(F32)).astype(BF16)


def small_call(body, name, out_rows, scalars, *arrays, scratch=()):
    size = sum(a.size for a in arrays)
    return pl.pallas_call(
        body,
        out_shape=tuple(sds(r + (128,)) for r in out_rows),
        in_specs=[SM] + [VM] * len(arrays),
        out_specs=(VM,) * len(out_rows),
        scratch_shapes=scratch,
        compiler_params=params(),
        cost_estimate=cost(size, 4 * size),
        name=name,
    )(scalars, *arrays)


def mix_first(scalars, keeps, gots):
    n = len(keeps)
    sizes = [k.shape[1] for k in keeps]
    rows = sum(sizes)

    def body(s, *refs):
        ks, gs = refs[:n], refs[n : 2 * n]
        send, keep, total = refs[2 * n :]
        at = 0
        for k, g, size in zip(ks, gs, sizes):
            for y in range(2):
                total[y, at : at + size, :] = joined(k[y], g[y])
            at += size
        even, y, x = s[EVEN], s[YBIT], s[XBIT]
        for t in range(2):
            for o, flip_it in ((send, 1), (keep, 0)):
                own_y = flip_it + y - 2 * flip_it * y
                own_x = flip_it + x - 2 * flip_it * x
                row = even * own_y + (1 - even) * t
                half = even * t + (1 - even) * own_x
                o[t] = total[row, pl.ds(pl.multiple_of(half * (rows // 2), 16), rows // 2), :]

    shape = (2, rows // 2)
    return small_call(
        body, "mix_first", (shape, shape), scalars, *keeps, *gots,
        scratch=[pltpu.VMEM((2, rows, 128), BF16)],
    )


def mix_half(info, index, keep, got):
    keep = keep.reshape(2, -1, 128)
    got = got.reshape(2, -1, 128)

    def body(i, k, g, send, kept):
        own = i[index]
        send[...] = joined(k[1 - own], g[1 - own])
        kept[...] = joined(k[own], g[own])

    shape = (keep.shape[1],)
    return small_call(body, "mix_half", (shape, shape), info, keep, got)


def mix_sum(info, keep, got):
    def body(i, k, g, o):
        o[...] = joined(k[...], g[...])

    return small_call(body, "mix_sum", (keep.shape[:1],), info, keep, got)[0]


def mix_both(info, index, own, other):
    rows = own.shape[0]

    def body(i, a, b, o):
        o[i[index]] = a[...]
        o[1 - i[index]] = b[...]

    return small_call(body, "mix_both", ((2, rows),), info, own, other)[0].reshape(2 * rows, 128)


class Place:
    def __init__(self, first_pos):
        shard = lax.axis_index("shard")
        seq = lax.axis_index("seq")
        self.n_shard = lax.axis_size("shard")
        self.n = lax.axis_size("seq") * self.n_shard
        core = shard & 1
        y = shard >> 1
        x = seq & 1
        bits = []
        bit = 1
        while bit < lax.axis_size("seq"):
            bits.append(bit)
            bit *= 2
        self.far = [self.n_shard * b for b in bits]
        here = [(seq >> i) & 1 for i in range(len(bits))]
        flag = (first_pos > 0).astype(jnp.int32)
        second = jnp.where(core == 0, x, y)
        self.token = ()
        self.info = jnp.stack([shard, x, flag, 1 - core, y, second] + here).astype(jnp.int32)

    def send(self, x, even, odd):
        pairs = [(i, i ^ (even if i % 2 == 0 else odd)) for i in range(self.n)]
        return lax.ppermute(x, ("seq", "shard"), pairs)


ORDER = ("d", "da", "da", "dab", "da", "b", "acbcbcbccb")


class Chain:
    def __init__(self, place):
        self.place = place
        self.keeps = []
        self.gots = []
        self.keep = None
        n = len(place.far)
        self.steps = [self.start, self.second]
        self.steps += [lambda i=i: self.halve(i) for i in range(1, n - 1)]
        self.steps += [self.exchange]
        self.steps += [lambda i=i: self.double(i) for i in range(n - 2, 1, -1)]
        self.steps += [self.spread]
        self.count = len(self.steps)

    def add(self, keep, send):
        self.keeps.append(keep.reshape(2, -1, 128))
        self.gots.append(self.place.send(send.reshape(2, -1, 128), 1, 1))

    def wait(self, *first):
        if not first:
            return
        if len(self.steps) == self.count:
            self.gots = [after(g, *first) for g in self.gots]
        else:
            self.got = after(self.got, *first)

    def step(self):
        if self.keep is None:
            self.keeps[0] = self.turn(self.keeps[0])
        else:
            self.keep = self.turn(self.keep)
        return self.steps.pop(0)()

    def go(self, out, even, odd):
        self.got = self.place.send(out, even, odd)
        self.place.token = (out,)

    def turn(self, x):
        return after(x, *self.place.token) if self.place.token else x

    def collect(self):
        self.place.token = tuple(self.parts)

    def start(self):
        out, self.keep = mix_first(self.place.info, self.keeps, self.gots)
        self.go(out, 2, self.place.far[0])
        return out

    def second(self):
        out, self.keep = mix_half(self.place.info, SECOND, self.keep, self.got)
        self.go(out, self.place.far[0], 2)
        return out

    def halve(self, i):
        keep, got = self.keep, self.got
        out, self.keep = mix_half(self.place.info, HERE + i, keep, got)
        self.go(out, self.place.far[i], self.place.far[i])
        return out

    def exchange(self):
        self.keep = mix_sum(self.place.info, self.keep, self.got)
        self.go(self.keep, self.place.far[-1], self.place.far[-1])
        return self.keep

    def settle(self, i):
        if i == len(self.place.far) - 2:
            self.keep = mix_sum(self.place.info, self.keep, self.got)
        else:
            self.keep = mix_both(self.place.info, HERE + i + 1, self.keep, self.got)

    def spread(self):
        self.settle(1)
        x, z = self.place.far[:2]
        self.place.token = (self.keep,)
        self.parts = [self.keep] + [self.place.send(self.keep, f, f) for f in (x, z, x + z)]

    def double(self, i):
        self.settle(i)
        self.go(self.keep, self.place.far[i], self.place.far[i])
        return self.keep


def gather_parts(info, parts, total):
    x, z = info[HERE], info[HERE + 1]
    for part, (i, j) in zip(parts, ((x, z), (1 - x, z), (x, 1 - z), (1 - x, 1 - z))):
        total[2 * i + j] = part[...]


def spread(o, total, at, rows, blocks):
    half = total.shape[1]
    for j in range(blocks):
        done = 0
        while done < rows:
            part, row = divmod(at + j * rows + done, half)
            n = min(rows - done, half - row)
            o[done : done + n, 128 * j : 128 * (j + 1)] = total[part, row : row + n, :].astype(o.dtype)
            done += n


def finish_one(info, parts):
    def body(i, *refs):
        down, total = refs[4:]
        gather_parts(i, refs[:4], total)
        spread(down, total, 0, FF // 4, D // 128)

    return pl.pallas_call(
        body,
        out_shape=hbm((FF // 4, D), F32),
        in_specs=[SM] + [VM] * 4,
        out_specs=VM,
        scratch_shapes=[pltpu.VMEM((4,) + parts[0].shape, BF16)],
        compiler_params=params(),
        cost_estimate=cost(1e7, 1e7),
        name="finish_one",
    )(info, *parts)


def finish_two(info, parts_a, parts_b):
    gr = D // 4
    blocks = FH // 128

    def body(i, *refs):
        gate, up, out, total_a, total_b = refs[8:]
        gather_parts(i, refs[:4], total_a)
        gather_parts(i, refs[4:8], total_b)
        for k, total in enumerate((total_a, total_b)):
            spread(gate.at[:, pl.ds(FH * k, FH)], total, 0, gr, blocks)
            spread(up.at[:, pl.ds(FH * k, FH)], total, gr * blocks, gr, blocks)
        spread(out, total_b, 2 * gr * blocks, HEAD_DIM, D // 128)

    return pl.pallas_call(
        body,
        out_shape=(hbm((gr, FF), F32), hbm((gr, FF), F32), hbm((HEAD_DIM, D), F32)),
        in_specs=[SM] + [VM] * 8,
        out_specs=(VM,) * 3,
        scratch_shapes=[
            pltpu.VMEM((4,) + parts_a[0].shape, BF16),
            pltpu.VMEM((4,) + parts_b[0].shape, BF16),
        ],
        compiler_params=params(),
        cost_estimate=cost(1e7, 1e7),
        name="finish_two",
    )(info, *parts_a, *parts_b)


def finish_three(info, parts, query_w, key_w, value_w, gain):
    gr = D // 4

    def body(i, *refs):
        wq, wk, wv, g, query, key, value, gains, first, total, prod = refs[4:]
        gather_parts(i, refs[:4], total)
        spread(query, total, 0, gr, 8)
        spread(key, total, 8 * gr, gr, 2)
        spread(value, total, 10 * gr, gr, 2)
        spread(gains, total, 12 * gr, 16, 2)
        base = HEADS * HEAD_DIM
        prod[:, :base] = query[...] * wq[...].astype(F32)
        prod[:, base : base + HEAD_DIM] = key[...] * wk[...].astype(F32)
        prod[:, base + HEAD_DIM :] = value[...] * wv[...].astype(F32)
        p = prod[...]
        high = p.astype(BF16)
        low = (p - high.astype(F32)).astype(BF16)
        ones = jnp.ones((16, 6 * HEAD_DIM), BF16)
        first[...] = (dot(ones, high, NT) + dot(ones, low, NT)) / g[...].astype(F32).reshape(1, -1)

    return pl.pallas_call(
        body,
        out_shape=(
            hbm((gr, HEADS * HEAD_DIM), F32),
            hbm((gr, HEAD_DIM), F32),
            hbm((gr, HEAD_DIM), F32),
            sds((16, HEAD_DIM), F32),
            sds((16, gr), F32),
        ),
        in_specs=[SM] + [VM] * 8,
        out_specs=(VM,) * 5,
        scratch_shapes=[
            pltpu.VMEM((4,) + parts[0].shape, BF16),
            pltpu.VMEM((gr, 6 * HEAD_DIM), F32),
        ],
        compiler_params=params(),
        cost_estimate=cost(1e7, 1e7),
        name="finish_three",
    )(info, *parts, query_w, key_w, value_w, gain)


def shards(
    tokens,
    query_weight,
    key_weight,
    value_weight,
    out_weight,
    gate_weight,
    up_weight,
    down_weight,
    input_gain,
    query_gain,
    key_gain,
    attended_gain,
    middle_gain,
    output_gain,
    cotangent,
):
    n_seq = lax.axis_size("seq")
    n_shard = lax.axis_size("shard")
    shard = lax.axis_index("shard")
    count = tokens.shape[0]
    total = count * n_seq * n_shard
    length = min(SEQ_CAP, total)
    rank = lax.axis_index("seq") * n_shard + shard
    first_pos = rank * count % length
    place = Place(first_pos)
    me = flag = place.info
    gd = D // 4
    gh = HEAD_DIM // 4

    kvg = pack(
        me,
        key_weight,
        value_weight,
        input_gain,
        attended_gain,
        middle_gain,
        output_gain,
        query_gain,
        key_gain,
    )
    def near(x):
        return flip(x, "shard", 1)

    def far(x):
        return flip(x, "shard", 2)

    q_far = far(query_weight)
    kvg_far = far(kvg)
    kvgs = (kvg, near(kvg), kvg_far, near(kvg_far))
    q_near = near(query_weight)
    out_near, gate_near, up_near, down_near = (
        near(out_weight), near(gate_weight), near(up_weight), near(down_weight)
    )

    def relay(x):
        return flip(x, "seq", 1)

    gate_half, up_half, down_half = halves(me, gate_weight, up_weight, down_weight)

    positions = first_pos + jnp.arange(count, dtype=jnp.int32)
    hd = HEAD_DIM // 2
    freq = ROPE_BASE ** (-(jnp.arange(hd, dtype=F32) * 2.0 / HEAD_DIM))
    angles = positions.astype(F32)[:, None] * freq[None, :]
    cos = jnp.cos(angles)
    sin = jnp.sin(angles)

    gains = gains_of(me, kvgs)
    kvgs = pinned(*kvgs)
    nin, kraw, kv_lo, kv_hi = pre_kv(me, tokens, gains, cos, sin, kvgs)
    ranks = n_seq * n_shard
    per_seq = length // count
    pairs = [(i, i + 1) for i in range(ranks - 1) if (i + 1) % per_seq]
    halo = lax.ppermute(kv_hi, ("seq", "shard"), pairs)
    out_far = far(out_weight)
    gate_a = far(gate_half)
    q_far = after(q_far, nin)
    qs_w = pinned(query_weight, q_near, q_far, near(q_far))
    up_a = far(after(up_half, gate_a))
    gate_b = relay(gate_a)
    qraw, qs = pre_q(me, nin, gains, cos, sin, qs_w)
    qs = after(qs, out_far, gate_a)
    o_hi, pm_hi, p1_hi = att(flag, qs, kv_lo, kv_hi, False, 1)
    o_lo, pm_lo, p1_lo = att(flag, after(qs, o_hi), halo, kv_lo, True, 0)
    gate_b = after(gate_b, o_lo)
    up_a = after(up_a, o_lo)
    down_a = far(after(down_half, up_a))
    up_b = relay(up_a)
    outs = pinned(out_weight, out_near, out_far, near(out_far))
    ap, nm = mid_part(me, o_lo, o_hi, tokens, gains, outs)
    gates = pinned(gate_weight, gate_near, gate_a, gate_b, near(gate_a), near(gate_b))
    act, slope = ff(me, nm, gates)
    up_b = after(up_b, act)
    down_a = after(down_a, act)
    down_b = relay(down_a)
    ups = pinned(up_weight, up_near, up_a, up_b, near(up_a), near(up_b))
    hid, bact = ff(me, nm, ups, (act, slope))
    down_b = after(down_b, hid)
    downs = pinned(down_weight, down_near, down_a, down_b, near(down_a), near(down_b))
    block_out, dd, wd, keep, send, gain_down = down_part(
        me, hid, tokens, cotangent, ap, gains, downs
    )
    chains = {name: Chain(place) for name in "abcd"}

    def advance(order, *first):
        for name in order:
            chain = chains[name.lower()]
            if name.isupper():
                chain.parts = [after(x, *first) for x in chain.parts]
                chain.collect()
            elif chain.steps:
                chain.wait(*first)
                chain.step()

    chains["d"].add(keep, send)
    keep, send, dnm = fb(me, nm, dd, act, bact, wd, gates, ups, 0, None)
    chains["a"].add(keep, send)
    advance(ORDER[0], dnm)
    dnm = after(dnm, *place.token)
    keep, send, dnm = fb(me, nm, dd, act, bact, wd, gates, ups, 1, dnm)
    chains["b"].add(keep, send)
    advance(ORDER[1], dnm)
    keep, send, d_o, d_mid, gain_mid = fe(
        me, o_lo, o_hi, tokens, cotangent, gains, ap, after(dnm, *place.token), outs
    )
    chains["b"].add(keep, send)
    advance(ORDER[2], d_o)
    dq_lo, kv_back, kv_a, gq_lo = att_back(
        qs, qraw, halo, kv_lo, pm_lo, p1_lo, after(d_o, *place.token), gains, cos, sin, 0
    )
    returned = lax.ppermute(kv_back, ("seq", "shard"), [(j, i) for i, j in pairs])
    advance(ORDER[3], dq_lo)
    dq_hi, kv_b, kv_c, gq_hi = att_back(
        qs, qraw, kv_lo, kv_hi, pm_hi, p1_hi, after(d_o, dq_lo, *place.token), gains, cos, sin, 1
    )
    advance(ORDER[4], dq_hi)
    dkv, keep, send = post(
        me,
        nin,
        (dq_lo, after(dq_hi, *place.token)),
        (kv_a, kv_b, kv_c, returned),
        kraw,
        gains,
        cos,
        sin,
        (gq_lo, gq_hi, gain_mid, gain_down),
    )
    chains["c"].add(keep, send)
    advance(ORDER[5], keep)
    grad_tokens = last(
        me, tokens, d_mid, (dq_lo, dq_hi), after(dkv, *place.token), gains, qs_w, kvgs
    )
    advance(ORDER[6], grad_tokens)
    for name in "dacb":
        advance(name * len(chains[name].steps))
    r_down = finish_one(me, chains["d"].parts)
    r_query, r_key, r_value, tail, first = finish_three(
        me,
        chains["c"].parts,
        query_weight,
        key_weight,
        value_weight,
        input_gain,
    )
    r_gate, r_up, r_out = finish_two(me, chains["a"].parts, chains["b"].parts)
    return (
        block_out,
        grad_tokens,
        r_query,
        r_key,
        r_value,
        r_out,
        r_gate,
        r_up,
        r_down,
        first[0],
        tail[4, :gh],
        tail[5, :gh],
        tail[1, :gd],
        tail[2, :gd],
        tail[3, :gd],
    )


def solution(mesh):
    token = P(("seq", "shard"), None)
    matrix = P("shard", None)
    vector = P("shard")
    in_specs = (token,) + (matrix,) * 7 + (vector,) * 6 + (token,)
    out_specs = (token, token) + (matrix,) * 7 + (vector,) * 6
    return jax.shard_map(shards, mesh=mesh, in_specs=in_specs, out_specs=out_specs, check_vma=False)
```

```python
import jax
import jax.numpy as jnp
from jax import lax
from jax.experimental import pallas as pl
from jax.experimental.pallas import tpu as pltpu
from jax.sharding import PartitionSpec as P

D = 640
HEADS = 4
HEAD_DIM = 256
FF = 2048
WINDOW = 512
SEQ_CAP = 8192
HALF = 512
QB = 256
ROWS = HEADS * QB
CHUNK = 512

EPS = 1e-06
ROPE_BASE = 10000.0
LOG2E = 1.4426950408889634
LN2 = 0.6931471805599453
SCALE = HEAD_DIM**-0.5

F32 = jnp.float32
BF16 = jnp.bfloat16
VM = pl.BlockSpec(memory_space=pltpu.VMEM)
SM = pl.BlockSpec(memory_space=pltpu.SMEM)
HM = pl.BlockSpec(memory_space=pltpu.HBM)
NN = (((1,), (0,)), ((), ()))
NT = (((1,), (1,)), ((), ()))
TN = (((0,), (0,)), ((), ()))


def dot(a, b, dims=NN):
    return lax.dot_general(a, b, dims, preferred_element_type=F32)


def params(mib=14):
    return pltpu.CompilerParams(vmem_limit_bytes=mib * 2**20)


def sds(shape, dtype=BF16):
    return jax.ShapeDtypeStruct(shape, dtype)


def cost(flops, nbytes):
    return pl.CostEstimate(flops=int(flops), bytes_accessed=int(nbytes), transcendentals=0)


def rms_factor(v):
    return lax.rsqrt(jnp.mean(v * v, axis=-1, keepdims=True) + EPS)


def norm_back(v, factor, gain, incoming):
    united = v * factor
    scaled = incoming * gain
    back = factor * (scaled - united * jnp.mean(scaled * united, axis=-1, keepdims=True))
    return back, jnp.sum(incoming * united, axis=0, keepdims=True)


def offsets(me, rows):
    return (
        me * rows,
        (me + 1 - 2 * (me % 2)) * rows,
        ((me + 2) % 4) * rows,
        (3 - me) * rows,
    )


def hbm(shape, dtype=BF16):
    return pltpu.HBM(shape, dtype)


ME, XBIT, FLAG, EVEN, YBIT, SECOND, HERE = range(7)


def pin(x):
    return pltpu.with_memory_space_constraint(x, pltpu.HBM)


def pinned(*arrays):
    return tuple(pin(x) for x in arrays)


def whole(piece):
    return piece


def place_copies(me_ref, pieces, src_of, buf, rows, sems, first):
    me, b = me_ref[ME], me_ref[XBIT]
    spots = [(p, o, rows) for p, o in zip(pieces, offsets(me, rows))]
    if len(pieces) == 6:
        part = rows // 2
        far, last = spots[2][1], spots[3][1]
        spots = spots[:2]
        for base, p in ((far, pieces[2:4]), (last, pieces[4:6])):
            spots.append((p[0], base + b * part, part))
            spots.append((p[1], base + (1 - b) * part, part))
    copies = []
    for k, (piece, off, n) in enumerate(spots):
        copies.append(
            pltpu.make_async_copy(
                src_of(piece), buf.at[pl.ds(pl.multiple_of(off, 16), n)], sems.at[first + k]
            )
        )
    return copies


def pack_kernel(info, k, v, g0, g1, g2, g3, g4, g5, out, r0, r1, r2, r3, r4, r5, sems):
    rows = D // 4
    gains = (g0, g1, g2, g3, g4, g5)
    places = (r0, r1, r2, r3, r4, r5)
    copies = [
        pltpu.make_async_copy(k, out.at[pl.ds(0, rows), pl.ds(0, HEAD_DIM)], sems.at[0]),
        pltpu.make_async_copy(v, out.at[pl.ds(0, rows), pl.ds(HEAD_DIM, HEAD_DIM)], sems.at[1]),
    ]
    for i in range(6):
        copies.append(pltpu.make_async_copy(gains[i], places[i], sems.at[2 + i]))
    for c in copies:
        c.start()
    out[rows:, :] = jnp.zeros((16, 2 * HEAD_DIM), BF16)
    for c in copies:
        c.wait()
    for i, r in enumerate(places):
        out[rows + i : rows + i + 1, : r.shape[0]] = r[...].reshape(1, -1)


def pack(info, k, v, *gains):
    return pl.pallas_call(
        pack_kernel,
        out_shape=sds((D // 4 + 16, 2 * HEAD_DIM)),
        in_specs=[SM] + [HM] * 8,
        out_specs=VM,
        scratch_shapes=[pltpu.VMEM(g.shape, BF16) for g in gains] + [pltpu.SemaphoreType.DMA((8,))],
        compiler_params=params(),
        cost_estimate=cost(1e6, 4e5),
        name="pack",
    )(info, *(pin(w) for w in (k, v) + gains))


def halves_kernel(info, *refs):
    n = len(refs) // 2
    ins, outs, sems = refs[:n], refs[n : 2 * n], refs[2 * n]
    copies = []
    for i, (w, o) in enumerate(zip(ins, outs)):
        rows = w.shape[0] // 2
        at = pl.multiple_of(info[XBIT] * rows, 16)
        copies.append(pltpu.make_async_copy(w.at[pl.ds(at, rows)], o, sems.at[i]))
    for c in copies:
        c.start()
    for c in copies:
        c.wait()


def halves(info, *weights):
    return pl.pallas_call(
        halves_kernel,
        out_shape=tuple(sds((w.shape[0] // 2, w.shape[1])) for w in weights),
        in_specs=[SM] + [HM] * len(weights),
        out_specs=(VM,) * len(weights),
        scratch_shapes=[pltpu.SemaphoreType.DMA((len(weights),))],
        compiler_params=params(),
        cost_estimate=cost(1e6, 2e6),
        name="halves",
    )(info, *(pin(w) for w in weights))


def gains_kernel(me_ref, g0, g1, g2, g3, out):
    gd = D // 4
    gh = HEAD_DIM // 4
    wide = jnp.zeros((16, D), F32)
    small = jnp.zeros((16, HEAD_DIM), F32)
    spots = offsets(me_ref[ME], 1)
    for spot, g in zip(spots, (g0, g1, g2, g3)):
        piece = g[...]
        row = lax.broadcasted_iota(jnp.int32, (HEAD_DIM, D), 0)
        col = lax.broadcasted_iota(jnp.int32, (HEAD_DIM, D), 1)
        place = ((col == row + spot * gd) & (row < gd)).astype(BF16)
        wide = wide + dot(piece, place)
        row = lax.broadcasted_iota(jnp.int32, (HEAD_DIM, HEAD_DIM), 0)
        col = lax.broadcasted_iota(jnp.int32, (HEAD_DIM, HEAD_DIM), 1)
        place = ((col == row + spot * gh) & (row < gh)).astype(BF16)
        small = small + dot(piece, place)
    out[0:4, :] = wide[0:4, :]
    out[4:8, :] = jnp.zeros((4, D), F32)
    out[4:8, :HEAD_DIM] = small[4:8, :]


def gains_of(me, pieces):
    part = pl.BlockSpec((16, HEAD_DIM), lambda i: (D // 4 // 16, 0))
    return pl.pallas_call(
        gains_kernel,
        grid=(1,),
        out_shape=sds((8, D), F32),
        in_specs=[SM] + [part] * 4,
        out_specs=VM,
        compiler_params=params(),
        cost_estimate=cost(1e8, 1e5),
        name="gains",
    )(me, *pieces)


def rotated(u, cos, sin):
    hd = HEAD_DIM // 2
    u1 = u[:, :hd]
    u2 = u[:, hd:]
    return (u1 * cos - u2 * sin).astype(BF16), (u2 * cos + u1 * sin).astype(BF16)


def pre_kv_kernel(me_ref, tok, gains, cos_ref, sin_ref, w0, w1, w2, w3, nin_o, kraw_o, lo_o, hi_o, wbuf, sems):
    rows = D // 4
    copies = place_copies(
        me_ref, (w0, w1, w2, w3), lambda w: w.at[pl.ds(0, rows)], wbuf, rows, sems, 0
    )
    for c in copies:
        c.start()
    hd = HEAD_DIM // 2
    x = tok[...].astype(F32)
    nin = (x * rms_factor(x) * gains[0:1, :]).astype(BF16)
    nin_o[...] = nin
    for c in copies:
        c.wait()
    k = dot(nin, wbuf[:, :HEAD_DIM])
    kraw_o[...] = k.astype(BF16)
    r1, r2 = rotated(k * rms_factor(k) * gains[5:6, :HEAD_DIM], cos_ref[...], sin_ref[...])
    v = dot(nin, wbuf[:, HEAD_DIM:]).astype(BF16)
    for half, o in enumerate((lo_o, hi_o)):
        sl = slice(HALF * half, HALF * (half + 1))
        o[:, :hd] = r1[sl]
        o[:, hd:HEAD_DIM] = r2[sl]
        o[:, HEAD_DIM:] = v[sl]


def pre_kv(me, tok, gains, cos, sin, pieces):
    t = tok.shape[0]
    return pl.pallas_call(
        pre_kv_kernel,
        out_shape=(
            sds((t, D)),
            sds((t, HEAD_DIM)),
            sds((HALF, 2 * HEAD_DIM)),
            sds((HALF, 2 * HEAD_DIM)),
        ),
        in_specs=[SM, VM, VM, VM, VM, HM, HM, HM, HM],
        out_specs=(VM,) * 4,
        scratch_shapes=[pltpu.VMEM((D, 2 * HEAD_DIM), BF16), pltpu.SemaphoreType.DMA((4,))],
        compiler_params=params(),
        cost_estimate=cost(2 * t * D * 512, 5e6),
        name="pre_kv",
    )(me, tok, gains, cos, sin, *pieces)


def pre_q_kernel(me_ref, nin_i, gains, cos_ref, sin_ref, w0, w1, w2, w3, qraw_o, qs_o, wbuf, sems):
    rows = D // 4
    hd = HEAD_DIM // 2

    @pl.when(pl.program_id(0) == 0)
    def _():
        copies = place_copies(
            me_ref, (w0, w1, w2, w3), lambda w: w.at[pl.ds(0, rows)], wbuf, rows, sems, 0
        )
        for c in copies:
            c.start()
        for c in copies:
            c.wait()

    q = dot(nin_i[...], wbuf[:, pl.ds(pl.multiple_of(pl.program_id(0) * HEAD_DIM, HEAD_DIM), HEAD_DIM)])
    qraw_o[0] = q.astype(BF16)
    u = q * (rms_factor(q) * (SCALE * LOG2E)) * gains[4:5, :HEAD_DIM]
    r1, r2 = rotated(u, cos_ref[...], sin_ref[...])
    qs_o[0, :, :hd] = r1
    qs_o[0, :, hd:] = r2


def pre_q(me, nin, gains, cos, sin, pieces):
    t = nin.shape[0]
    head = pl.BlockSpec((1, t, HEAD_DIM), lambda h: (h, 0, 0))
    return pl.pallas_call(
        pre_q_kernel,
        grid=(HEADS,),
        out_shape=(hbm((HEADS, t, HEAD_DIM)), sds((HEADS, t, HEAD_DIM))),
        in_specs=[SM, VM, VM, VM, VM, HM, HM, HM, HM],
        out_specs=(head, head),
        scratch_shapes=[pltpu.VMEM((D, HEADS * HEAD_DIM), BF16), pltpu.SemaphoreType.DMA((4,))],
        compiler_params=params(),
        cost_estimate=cost(2 * t * D * 1024, 5e6),
        name="pre_q",
    )(me, nin, gains, cos, sin, *pieces)


def key_blocks(j, kvp, kvs, lo, hi):
    blocks = (kvp[0:QB, lo:hi], kvp[QB : 2 * QB, lo:hi], kvs[0:QB, lo:hi], kvs[QB : 2 * QB, lo:hi])
    return blocks[j : j + 3]


def upper_mask():
    row = lax.broadcasted_iota(jnp.int32, (HEADS, QB, QB), 1).reshape(ROWS, QB)
    col = lax.broadcasted_iota(jnp.int32, (ROWS, QB), 1)
    return col > row


def att_kernel(masked, flag_ref, qs, kvp, kvs, o_o, pm_o, p1_o):
    upper = upper_mask()
    for j in range(2):
        sl = slice(QB * j, QB * (j + 1))
        q = qs[:, sl, :].reshape(ROWS, HEAD_DIM)
        k0, k1, k2 = key_blocks(j, kvp, kvs, 0, HEAD_DIM)
        v0, v1, v2 = key_blocks(j, kvp, kvs, HEAD_DIM, 2 * HEAD_DIM)
        em = jnp.exp2(jnp.where(upper, dot(q, k0, NT), dot(q, k2, NT)))
        e1 = jnp.exp2(dot(q, k1, NT))
        if masked:
            keep = flag_ref[FLAG].astype(F32)
            em = em * jnp.where(upper, keep, 1.0)
            if j == 0:
                e1 = e1 * keep
        inv = 1.0 / jnp.sum(em + e1, axis=-1, keepdims=True)
        pm = (em * inv).astype(BF16)
        p1 = (e1 * inv).astype(BF16)
        zero = jnp.zeros_like(pm)
        out = dot(p1, v1) + dot(jnp.where(upper, pm, zero), v0) + dot(jnp.where(upper, zero, pm), v2)
        pm_o[:, sl, :] = pm.reshape(HEADS, QB, QB)
        p1_o[:, sl, :] = p1.reshape(HEADS, QB, QB)
        for h in range(HEADS):
            o_o[sl, HEAD_DIM * h : HEAD_DIM * (h + 1)] = out[QB * h : QB * (h + 1), :].astype(BF16)


def half_spec(half):
    return pl.BlockSpec((HEADS, HALF, HEAD_DIM), lambda i: (0, half, 0))


def att(flag, qs, kvp, kvs, masked, half):
    shp = sds((HEADS, HALF, HEAD_DIM))

    def body(*refs):
        att_kernel(masked, *refs)

    return pl.pallas_call(
        body,
        grid=(1,),
        out_shape=(sds((HALF, HEADS * HEAD_DIM)), shp, shp),
        in_specs=[SM, half_spec(half), VM, VM],
        out_specs=(VM,) * 3,
        compiler_params=params(),
        cost_estimate=cost(12e9 / 4, 5e6),
        name="att",
    )(flag, qs, kvp, kvs)


def att_back_kernel(qs, qraw, kvp, kvs, pm_i, p1_i, do_i, gains, cos_ref, sin_ref, dq_o, dkvp_o, dkvs_o, gain_o, acc):
    upper = upper_mask()
    hd = HEAD_DIM // 2
    acc[...] = jnp.zeros_like(acc)
    gsum = jnp.zeros((1, HEAD_DIM), F32)
    for j in range(2):
        sl = slice(QB * j, QB * (j + 1))
        q = qs[:, sl, :].reshape(ROWS, HEAD_DIM)
        do = do_i[:, sl, :].reshape(ROWS, HEAD_DIM)
        k0, k1, k2 = key_blocks(j, kvp, kvs, 0, HEAD_DIM)
        v0, v1, v2 = key_blocks(j, kvp, kvs, HEAD_DIM, 2 * HEAD_DIM)
        pmb = pm_i[:, sl, :].reshape(ROWS, QB)
        p1b = p1_i[:, sl, :].reshape(ROWS, QB)
        dpm = jnp.where(upper, dot(do, v0, NT), dot(do, v2, NT))
        dp1 = dot(do, v1, NT)
        pm = pmb.astype(F32)
        p1 = p1b.astype(F32)
        total = jnp.sum(pm * dpm + p1 * dp1, axis=-1, keepdims=True)
        dsm = (pm * (dpm - total)).astype(BF16)
        ds1 = (p1 * (dp1 - total)).astype(BF16)
        zero = jnp.zeros_like(dsm)
        ds0 = jnp.where(upper, dsm, zero)
        ds2 = jnp.where(upper, zero, dsm)
        p0 = jnp.where(upper, pmb, zero)
        p2 = jnp.where(upper, zero, pmb)
        for t, (ds, p) in enumerate(((ds0, p0), (ds1, p1b), (ds2, p2))):
            at = slice(QB * (j + t), QB * (j + t + 1))
            acc[at, :HEAD_DIM] += dot(ds, q, TN) * LN2
            acc[at, HEAD_DIM:] += dot(p, do, TN)
        dq = (dot(ds0, k0) + dot(ds1, k1) + dot(ds2, k2)) * SCALE
        cos = cos_ref[sl, :]
        sin = sin_ref[sl, :]
        gain = gains[4:5, :HEAD_DIM]
        for h in range(HEADS):
            d1 = dq[QB * h : QB * (h + 1), :hd]
            d2 = dq[QB * h : QB * (h + 1), hd:]
            inc = jnp.concatenate([d1 * cos + d2 * sin, d2 * cos - d1 * sin], axis=-1)
            raw = qraw[h, sl, :].astype(F32)
            back, terms = norm_back(raw, rms_factor(raw), gain, inc)
            gsum = gsum + terms
            dq_o[sl, HEAD_DIM * h : HEAD_DIM * (h + 1)] = back.astype(BF16)
    dkvp_o[...] = acc[:HALF, :].astype(BF16)
    dkvs_o[...] = acc[HALF:, :]
    gain_o[...] = jnp.broadcast_to(gsum, (8, HEAD_DIM))


def att_back(qs, qraw, kvp, kvs, pm, p1, do, gains, cos, sin, half):
    dospec = half_spec(half)
    tab = pl.BlockSpec((HALF, HEAD_DIM // 2), lambda i: (half, 0))
    return pl.pallas_call(
        att_back_kernel,
        grid=(1,),
        out_shape=(
            sds((HALF, HEADS * HEAD_DIM)),
            sds((HALF, 2 * HEAD_DIM)),
            sds((HALF, 2 * HEAD_DIM), F32),
            sds((8, HEAD_DIM), F32),
        ),
        in_specs=[dospec, dospec, VM, VM, VM, VM, dospec, VM, tab, tab],
        out_specs=(VM,) * 4,
        scratch_shapes=[pltpu.VMEM((2 * HALF, 2 * HEAD_DIM), F32)],
        compiler_params=params(),
        cost_estimate=cost(24e9 / 4, 9e6),
        name="att_back",
    )(qs, qraw, kvp, kvs, pm, p1, do, gains, cos, sin)


def mid_kernel(me_ref, o_lo, o_hi, tok, gains, w0, w1, w2, w3, ap_o, nm_o, wo, sems):
    ro = HEADS * HEAD_DIM // 4
    copies = place_copies(me_ref, (w0, w1, w2, w3), lambda w: w, wo, ro, sems, 0)
    for c in copies:
        c.start()
    for c in copies:
        c.wait()
    for half, o in enumerate((o_lo, o_hi)):
        sl = slice(HALF * half, HALF * (half + 1))
        proj = dot(o[...], wo[...])
        ap_o[sl, :] = proj.astype(BF16)
        mid = tok[sl, :].astype(F32) + proj * rms_factor(proj) * gains[1:2, :]
        nm_o[sl, :] = (mid * rms_factor(mid) * gains[2:3, :]).astype(BF16)


def mid_part(me, o_lo, o_hi, tok, gains, outs):
    t = tok.shape[0]
    return pl.pallas_call(
        mid_kernel,
        out_shape=(sds((t, D)), sds((t, D))),
        in_specs=[SM] + [VM] * 4 + [HM] * 4,
        out_specs=(VM, VM),
        scratch_shapes=[
            pltpu.VMEM((HEADS * HEAD_DIM, D), BF16),
            pltpu.SemaphoreType.DMA((4,)),
        ],
        compiler_params=params(),
        cost_estimate=cost(2 * t * D * 1024, 8e6),
        name="mid",
    )(me, o_lo, o_hi, tok, gains, *outs)


FH = FF // 2
STEP = 512
WIDE = 512
RB = 512


def by_columns(me_ref, pieces, buf, sems, body):
    def copies(i):
        at = pl.ds(pl.multiple_of(i * STEP, STEP), STEP)
        return place_copies(
            me_ref, pieces, lambda w: w.at[:, at], buf.at[:, at], D // 4, sems, 6 * i
        )

    for i in range(FF // STEP):
        for c in copies(i):
            c.start()

    def step(i, carry):
        for c in copies(i):
            c.wait()
        body(pl.ds(pl.multiple_of(i * STEP, STEP), STEP))
        return carry

    lax.fori_loop(0, FF // STEP, step, 0)


def gate_kernel(me_ref, nm, *rest):
    pieces, (a_o, s_o, wg, sems) = rest[:6], rest[6:]
    c0 = 0.7978845608028654
    c1 = 0.044715 * c0

    def body(cs):
        for r in range(0, nm.shape[0], RB):
            rs = slice(r, r + RB)
            g = dot(nm[rs, :], wg[:, cs]).astype(BF16)
            g2 = g * g
            t = jnp.tanh(g * (c0 + c1 * g2))
            h = 0.5 + 0.5 * t
            a = g * h
            a_o[rs, cs] = a
            s_o[rs, cs] = h + a * (1.0 - h) * (2.0 * c0 + (6.0 * c1) * g2)

    by_columns(me_ref, pieces, wg, sems, body)


def up_kernel(me_ref, nm, a_i, s_i, *rest):
    pieces, (hid_o, b_o, wu, sems) = rest[:6], rest[6:]

    def body(cs):
        for r in range(0, nm.shape[0], RB):
            rs = slice(r, r + RB)
            u = dot(nm[rs, :], wu[:, cs]).astype(BF16)
            hid_o[rs, cs] = a_i[rs, cs] * u
            b_o[rs, cs] = u * s_i[rs, cs]

    by_columns(me_ref, pieces, wu, sems, body)


def ff(me, nm, pieces, before=()):
    t = nm.shape[0]
    return pl.pallas_call(
        up_kernel if before else gate_kernel,
        out_shape=(sds((t, FF)),) * 2,
        in_specs=[SM, VM] + [VM] * len(before) + [HM] * 6,
        out_specs=(VM,) * 2,
        scratch_shapes=[pltpu.VMEM((D, FF), BF16), pltpu.SemaphoreType.DMA((6 * FF // STEP,))],
        compiler_params=params(),
        cost_estimate=cost(2 * t * D * FF, 12e6),
        name="up" if before else "gate",
    )(me, nm, *before, *pieces)


def down_kernel(me_ref, hid, tok, cot, ap, gains, *rest):
    pieces, (out_o, dd_o, wd_o, keep_o, send_o, gain_o, sems) = rest[:6], rest[6:]
    rf = FF // 4
    core = me_ref[ME] % 2
    copies = place_copies(me_ref, pieces, whole, wd_o, rf, sems, 0)
    for c in copies:
        c.start()
    for c in copies:
        c.wait()
    gsum = jnp.zeros((1, D), F32)
    for half in range(2):
        sl = slice(HALF * half, HALF * (half + 1))
        dn = dot(hid[sl, :], wd_o[...])
        proj = ap[sl, :].astype(F32)
        mid = tok[sl, :].astype(F32) + proj * rms_factor(proj) * gains[1:2, :]
        fac = rms_factor(dn)
        out_o[sl, :] = (mid + dn * fac * gains[3:4, :]).astype(BF16)
        back, terms = norm_back(dn, fac, gains[3:4, :], cot[sl, :].astype(F32))
        dd_o[sl, :] = back.astype(BF16)
        gsum = gsum + terms
    gain_o[...] = jnp.broadcast_to(gsum, (8, D))
    for y in range(2):
        for part, o in ((core, keep_o), (1 - core, send_o)):
            at = pl.ds(pl.multiple_of((2 * y + part) * rf, rf), rf)
            g = dot(hid[:, at], dd_o[...], TN).astype(BF16)
            for j in range(D // 128):
                o[y, j] = g[:, 128 * j : 128 * (j + 1)]


def down_part(me, hid, tok, cot, ap, gains, pieces):
    t = tok.shape[0]
    return pl.pallas_call(
        down_kernel,
        out_shape=(
            sds((t, D)),
            sds((t, D)),
            sds((FF, D)),
            sds((2, D // 128, FF // 4, 128)),
            sds((2, D // 128, FF // 4, 128)),
            sds((8, D), F32),
        ),
        in_specs=[SM] + [VM] * 5 + [HM] * 6,
        out_specs=(VM,) * 6,
        scratch_shapes=[pltpu.SemaphoreType.DMA((6,))],
        compiler_params=params(),
        cost_estimate=cost(4 * t * D * FF, 20e6),
        name="down",
    )(me, hid, tok, cot, ap, gains, *pieces)


def fb_kernel(half, me_ref, nm, dd, a_i, b_i, wd, *rest):
    gates, ups, rest = rest[:6], rest[6:12], rest[12:]
    first = half == 0
    if first:
        keep_o, send_o, dnm_o, wg, wu, gs, sems = rest
    else:
        dnm_i, keep_o, send_o, dnm_o, wg, wu, gs, sems = rest
    core = me_ref[ME] % 2

    copies = []
    for k, (pieces, buf) in enumerate(((gates, wg), (ups, wu))):
        copies += place_copies(
            me_ref, pieces, lambda w: w.at[:, pl.ds(FH * half, FH)], buf, D // 4, sems, 6 * k
        )
    for c in copies:
        c.start()
    gr = D // 4
    for i in range(FH // WIDE):
        cs = slice(WIDE * i, WIDE * (i + 1))
        at = slice(FH * half + WIDE * i, FH * half + WIDE * (i + 1))
        dh = dot(dd[...], wd[at, :], NT).astype(BF16)
        dg = dh * b_i[:, at]
        du = dh * a_i[:, at]
        for k, d in enumerate((dg, du)):
            gs[k] = dot(nm[...], d, TN).astype(BF16)
            for y in range(2):
                for part, o in ((core, keep_o), (1 - core, send_o)):
                    rows = pl.ds(pl.multiple_of((2 * y + part) * gr, gr), gr)
                    for j in range(WIDE // 128):
                        to = WIDE // 128 * i + j
                        o[y, k, to] = gs[k, rows, 128 * j : 128 * (j + 1)]
        if i == 0:
            for c in copies:
                c.wait()
        back = dot(dg, wg[:, cs], NT) + dot(du, wu[:, cs], NT)
        if i > 0:
            dnm_o[...] += back
        elif first:
            dnm_o[...] = back
        else:
            dnm_o[...] = dnm_i[...] + back


def fb(me, nm, dd, a, b, wd, gates, ups, part, dnm):
    t = nm.shape[0]
    extra = () if dnm is None else (dnm,)

    def body(*refs):
        fb_kernel(part, *refs)

    return pl.pallas_call(
        body,
        out_shape=(sds((2, 2, FH // 128, D // 4, 128)),) * 2 + (sds((t, D), F32),),
        in_specs=[SM] + [VM] * 5 + [HM] * 12 + [VM] * len(extra),
        out_specs=(VM,) * 3,
        scratch_shapes=[
            pltpu.VMEM((D, FH), BF16),
            pltpu.VMEM((D, FH), BF16),
            pltpu.VMEM((2, D, WIDE), BF16),
            pltpu.SemaphoreType.DMA((12,)),
        ],
        compiler_params=params(16),
        cost_estimate=cost(10 * t * D * FH, 16e6),
        name="fb",
    )(me, nm, dd, a, b, wd, *gates, *ups, *extra)


def fe_kernel(me_ref, o_lo, o_hi, tok, cot, gains, ap, dnm, w0, w1, w2, w3, keep_o, send_o, do_o, dmid_o, gain_o, wo, datt, sems):
    ro = HEADS * HEAD_DIM // 4
    copies = place_copies(me_ref, (w0, w1, w2, w3), lambda w: w, wo, ro, sems, 0)
    for c in copies:
        c.start()
    gm = jnp.zeros((1, D), F32)
    ga = jnp.zeros((1, D), F32)
    for half in range(2):
        sl = slice(HALF * half, HALF * (half + 1))
        proj = ap[sl, :].astype(F32)
        pfac = rms_factor(proj)
        mid = tok[sl, :].astype(F32) + proj * pfac * gains[1:2, :]
        back, terms = norm_back(mid, rms_factor(mid), gains[2:3, :], dnm[sl, :])
        dmid = cot[sl, :].astype(F32) + back
        gm = gm + terms
        dmid_o[sl, :] = dmid.astype(BF16)
        back, terms = norm_back(proj, pfac, gains[1:2, :], dmid)
        ga = ga + terms
        datt[sl, :] = back.astype(BF16)
    gain_o[0:8, :] = jnp.broadcast_to(gm, (8, D))
    gain_o[8:16, :] = jnp.broadcast_to(ga, (8, D))
    for c in copies:
        c.wait()
    for h in range(HEADS):
        at = slice(HEAD_DIM * h, HEAD_DIM * (h + 1))
        do_o[h] = dot(datt[...], wo[at, :], NT).astype(BF16)
    core = me_ref[ME] % 2
    for y in range(2):
        for part, o in ((core, keep_o), (1 - core, send_o)):
            cs = pl.ds(pl.multiple_of((2 * y + part) * HEAD_DIM, HEAD_DIM), HEAD_DIM)
            g = dot(o_lo[:, cs], datt[:HALF, :], TN) + dot(o_hi[:, cs], datt[HALF:, :], TN)
            g = g.astype(BF16)
            for j in range(D // 128):
                o[y, j] = g[:, 128 * j : 128 * (j + 1)]


def fe(me, o_lo, o_hi, tok, cot, gains, ap, dnm, outs):
    t = tok.shape[0]
    return pl.pallas_call(
        fe_kernel,
        out_shape=(
            sds((2, D // 128, HEAD_DIM, 128)),
            sds((2, D // 128, HEAD_DIM, 128)),
            sds((HEADS, t, HEAD_DIM)),
            sds((t, D)),
            sds((16, D), F32),
        ),
        in_specs=[SM] + [VM] * 7 + [HM] * 4,
        out_specs=(VM,) * 5,
        scratch_shapes=[
            pltpu.VMEM((HEADS * HEAD_DIM, D), BF16),
            pltpu.VMEM((t, D), BF16),
            pltpu.SemaphoreType.DMA((4,)),
        ],
        compiler_params=params(),
        cost_estimate=cost(4 * t * D * 1024, 14e6),
        name="fe",
    )(me, o_lo, o_hi, tok, cot, gains, ap, dnm, *outs)


LAST = 2048


def post_kernel(
    me_ref, nin, dq_lo, dq_hi, kv_a, kv_b, kv_c, kv_d, kraw,
    gains, cos_ref, sin_ref, gq_lo, gq_hi, gmid, gdown,
    dkv, keep_o, send_o,
    gs, sums, small,
):
    rows = D // 4
    hd = HEAD_DIM // 2
    gk = jnp.zeros((1, HEAD_DIM), F32)
    for half, (first, second) in enumerate(((kv_a, kv_b), (kv_c, kv_d))):
        sl = slice(HALF * half, HALF * (half + 1))
        both = first[...].astype(F32) + second[...].astype(F32)
        cos = cos_ref[sl, :]
        sin = sin_ref[sl, :]
        d1 = both[:, :hd]
        d2 = both[:, hd:HEAD_DIM]
        inc = jnp.concatenate([d1 * cos + d2 * sin, d2 * cos - d1 * sin], axis=-1)
        raw = kraw[sl, :].astype(F32)
        back, terms = norm_back(raw, rms_factor(raw), gains[5:6, :HEAD_DIM], inc)
        gk = gk + terms
        dkv[sl, :HEAD_DIM] = back.astype(BF16)
        dkv[sl, HEAD_DIM:] = both[:, HEAD_DIM:].astype(BF16)

    core = me_ref[ME] % 2

    def put(slot, g):
        gs[slot] = g.astype(BF16)
        for y in range(2):
            for part, o in ((core, keep_o), (1 - core, send_o)):
                at = pl.ds(pl.multiple_of((2 * y + part) * rows, rows), rows)
                for j in range(2):
                    to = (2 * slot + j) * rows
                    o[y, to : to + rows, :] = gs[slot, at, 128 * j : 128 * (j + 1)]

    for h in range(HEADS):
        cs = slice(HEAD_DIM * h, HEAD_DIM * (h + 1))
        put(h, dot(nin[:HALF, :], dq_lo[:, cs], TN) + dot(nin[HALF:, :], dq_hi[:, cs], TN))
    put(HEADS, dot(nin[...], dkv[:, :HEAD_DIM], TN))
    put(HEADS + 1, dot(nin[...], dkv[:, HEAD_DIM:], TN))
    sums[...] = jnp.zeros_like(sums)
    small[...] = jnp.zeros_like(small)
    sums[1:2, :] = gmid[8:9, :]
    sums[2:3, :] = gmid[0:1, :]
    sums[3:4, :] = gdown[0:1, :]
    small[4:5, :] = gq_lo[0:1, :] + gq_hi[0:1, :]
    small[5:6, :] = gk
    gd = D // 4
    gh = HEAD_DIM // 4
    base = 12 * rows
    for y in range(2):
        for part, o in ((core, keep_o), (1 - core, send_o)):
            s = 2 * y + part
            row = lax.broadcasted_iota(jnp.int32, (D, HEAD_DIM), 0)
            col = lax.broadcasted_iota(jnp.int32, (D, HEAD_DIM), 1)
            place = ((row == col + s * gd) & (col < gd)).astype(BF16)
            g = dot(sums[...].astype(BF16), place)
            row = lax.broadcasted_iota(jnp.int32, (HEAD_DIM, HEAD_DIM), 0)
            col = lax.broadcasted_iota(jnp.int32, (HEAD_DIM, HEAD_DIM), 1)
            place = ((row == col + s * gh) & (col < gh)).astype(BF16)
            g = (g + dot(small[...].astype(BF16), place)).astype(BF16)
            o[y, base : base + 16, :] = g[:, :128]
            o[y, base + 16 : base + 32, :] = g[:, 128:]
            o[y, base + 32 :, :] = jnp.zeros((LAST - base - 32, 128), BF16)


def post(me, nin, dqs, kvs, kraw, gains, cos, sin, sums):
    t = nin.shape[0]
    return pl.pallas_call(
        post_kernel,
        out_shape=(
            sds((t, 2 * HEAD_DIM)),
            sds((2, LAST, 128)),
            sds((2, LAST, 128)),
        ),
        in_specs=[SM] + [VM] * 15,
        out_specs=(VM,) * 3,
        scratch_shapes=[
            pltpu.VMEM((HEADS + 2, D, HEAD_DIM), BF16),
            pltpu.VMEM((16, D), F32),
            pltpu.VMEM((16, HEAD_DIM), F32),
        ],
        compiler_params=params(),
        cost_estimate=cost(2e9, 10e6),
        name="post",
    )(me, nin, *dqs, *kvs, kraw, gains, cos, sin, *sums)


def last_kernel(me_ref, tok, dmid, dq_lo, dq_hi, dkv, gains, q0, q1, q2, q3, k0, k1, k2, k3, gt_o, wq, wkv, sems):
    rows = D // 4
    copies = place_copies(me_ref, (q0, q1, q2, q3), whole, wq, rows, sems, 0)
    copies += place_copies(
        me_ref, (k0, k1, k2, k3), lambda w: w.at[pl.ds(0, rows)], wkv, rows, sems, 4
    )
    for c in copies:
        c.start()
    for c in copies:
        c.wait()
    for half, dq in enumerate((dq_lo, dq_hi)):
        for r in range(0, HALF, RB):
            rs = slice(HALF * half + r, HALF * half + r + RB)
            dnin = dot(dq[r : r + RB, :], wq[...], NT) + dot(dkv[rs, :], wkv[...], NT)
            x = tok[rs, :].astype(F32)
            back, _ = norm_back(x, rms_factor(x), gains[0:1, :], dnin)
            gt_o[rs, :] = (dmid[rs, :].astype(F32) + back).astype(BF16)


def last(me, tok, dmid, dqs, dkv, gains, qs, kvgs):
    t = tok.shape[0]
    return pl.pallas_call(
        last_kernel,
        out_shape=hbm((t, D)),
        in_specs=[SM] + [VM] * 6 + [HM] * 8,
        out_specs=VM,
        scratch_shapes=[
            pltpu.VMEM((D, HEADS * HEAD_DIM), BF16),
            pltpu.VMEM((D, 2 * HEAD_DIM), BF16),
            pltpu.SemaphoreType.DMA((8,)),
        ],
        compiler_params=params(),
        cost_estimate=cost(2e9, 8e6),
        name="last",
    )(me, tok, dmid, *dqs, dkv, gains, *qs, *kvgs)


def flip(x, axis, bit):
    n = lax.axis_size(axis)
    return lax.ppermute(x, axis, [(i, i ^ bit) for i in range(n)])


def pick(x, index, axis=0):
    return lax.dynamic_index_in_dim(x, index, axis, keepdims=False)


def after(x, *first):
    return lax.optimization_barrier((x,) + first)[0]


def joined(a, b):
    return (a.astype(F32) + b.astype(F32)).astype(BF16)


def small_call(body, name, out_rows, scalars, *arrays, scratch=()):
    size = sum(a.size for a in arrays)
    return pl.pallas_call(
        body,
        out_shape=tuple(sds(r + (128,)) for r in out_rows),
        in_specs=[SM] + [VM] * len(arrays),
        out_specs=(VM,) * len(out_rows),
        scratch_shapes=scratch,
        compiler_params=params(),
        cost_estimate=cost(size, 4 * size),
        name=name,
    )(scalars, *arrays)


def mix_first(scalars, keeps, gots):
    n = len(keeps)
    sizes = [k.shape[1] for k in keeps]
    rows = sum(sizes)

    def body(s, *refs):
        ks, gs = refs[:n], refs[n : 2 * n]
        send, keep, total = refs[2 * n :]
        at = 0
        for k, g, size in zip(ks, gs, sizes):
            for y in range(2):
                total[y, at : at + size, :] = joined(k[y], g[y])
            at += size
        even, y, x = s[EVEN], s[YBIT], s[XBIT]
        for t in range(2):
            for o, flip_it in ((send, 1), (keep, 0)):
                own_y = flip_it + y - 2 * flip_it * y
                own_x = flip_it + x - 2 * flip_it * x
                row = even * own_y + (1 - even) * t
                half = even * t + (1 - even) * own_x
                o[t] = total[row, pl.ds(pl.multiple_of(half * (rows // 2), 16), rows // 2), :]

    shape = (2, rows // 2)
    return small_call(
        body, "mix_first", (shape, shape), scalars, *keeps, *gots,
        scratch=[pltpu.VMEM((2, rows, 128), BF16)],
    )


def mix_half(info, index, keep, got):
    keep = keep.reshape(2, -1, 128)
    got = got.reshape(2, -1, 128)

    def body(i, k, g, send, kept):
        own = i[index]
        send[...] = joined(k[1 - own], g[1 - own])
        kept[...] = joined(k[own], g[own])

    shape = (keep.shape[1],)
    return small_call(body, "mix_half", (shape, shape), info, keep, got)


def mix_sum(info, keep, got):
    def body(i, k, g, o):
        o[...] = joined(k[...], g[...])

    return small_call(body, "mix_sum", (keep.shape[:1],), info, keep, got)[0]


def mix_both(info, index, own, other):
    rows = own.shape[0]

    def body(i, a, b, o):
        o[i[index]] = a[...]
        o[1 - i[index]] = b[...]

    return small_call(body, "mix_both", ((2, rows),), info, own, other)[0].reshape(2 * rows, 128)


class Place:
    def __init__(self, first_pos):
        shard = lax.axis_index("shard")
        seq = lax.axis_index("seq")
        self.n_shard = lax.axis_size("shard")
        self.n = lax.axis_size("seq") * self.n_shard
        core = shard & 1
        y = shard >> 1
        x = seq & 1
        bits = []
        bit = 1
        while bit < lax.axis_size("seq"):
            bits.append(bit)
            bit *= 2
        self.far = [self.n_shard * b for b in bits]
        here = [(seq >> i) & 1 for i in range(len(bits))]
        flag = (first_pos > 0).astype(jnp.int32)
        second = jnp.where(core == 0, x, y)
        self.token = ()
        self.info = jnp.stack([shard, x, flag, 1 - core, y, second] + here).astype(jnp.int32)

    def send(self, x, even, odd):
        pairs = [(i, i ^ (even if i % 2 == 0 else odd)) for i in range(self.n)]
        return lax.ppermute(x, ("seq", "shard"), pairs)


ORDER = ("d", "da", "da", "dab", "da", "b", "acbcbcbccb")


class Chain:
    def __init__(self, place):
        self.place = place
        self.keeps = []
        self.gots = []
        self.keep = None
        n = len(place.far)
        self.steps = [self.start, self.second]
        self.steps += [lambda i=i: self.halve(i) for i in range(1, n - 1)]
        self.steps += [self.exchange]
        self.steps += [lambda i=i: self.double(i) for i in range(n - 2, 1, -1)]
        self.steps += [self.spread]
        self.count = len(self.steps)

    def add(self, keep, send):
        self.keeps.append(keep.reshape(2, -1, 128))
        self.gots.append(self.place.send(send.reshape(2, -1, 128), 1, 1))

    def wait(self, *first):
        if not first:
            return
        if len(self.steps) == self.count:
            self.gots = [after(g, *first) for g in self.gots]
        else:
            self.got = after(self.got, *first)

    def step(self):
        if self.keep is None:
            self.keeps[0] = self.turn(self.keeps[0])
        else:
            self.keep = self.turn(self.keep)
        return self.steps.pop(0)()

    def go(self, out, even, odd):
        self.got = self.place.send(out, even, odd)
        self.place.token = (out,)

    def turn(self, x):
        return after(x, *self.place.token) if self.place.token else x

    def collect(self):
        self.place.token = tuple(self.parts)

    def start(self):
        out, self.keep = mix_first(self.place.info, self.keeps, self.gots)
        self.go(out, 2, self.place.far[0])
        return out

    def second(self):
        out, self.keep = mix_half(self.place.info, SECOND, self.keep, self.got)
        self.go(out, self.place.far[0], 2)
        return out

    def halve(self, i):
        keep, got = self.keep, self.got
        out, self.keep = mix_half(self.place.info, HERE + i, keep, got)
        self.go(out, self.place.far[i], self.place.far[i])
        return out

    def exchange(self):
        self.keep = mix_sum(self.place.info, self.keep, self.got)
        self.go(self.keep, self.place.far[-1], self.place.far[-1])
        return self.keep

    def settle(self, i):
        if i == len(self.place.far) - 2:
            self.keep = mix_sum(self.place.info, self.keep, self.got)
        else:
            self.keep = mix_both(self.place.info, HERE + i + 1, self.keep, self.got)

    def spread(self):
        self.settle(1)
        x, z = self.place.far[:2]
        self.place.token = (self.keep,)
        self.parts = [self.keep] + [self.place.send(self.keep, f, f) for f in (x, z, x + z)]

    def double(self, i):
        self.settle(i)
        self.go(self.keep, self.place.far[i], self.place.far[i])
        return self.keep


def gather_parts(info, parts, total):
    x, z = info[HERE], info[HERE + 1]
    for part, (i, j) in zip(parts, ((x, z), (1 - x, z), (x, 1 - z), (1 - x, 1 - z))):
        total[2 * i + j] = part[...]


def spread(o, total, at, rows, blocks):
    half = total.shape[1]
    for j in range(blocks):
        done = 0
        while done < rows:
            part, row = divmod(at + j * rows + done, half)
            n = min(rows - done, half - row)
            o[done : done + n, 128 * j : 128 * (j + 1)] = total[part, row : row + n, :].astype(o.dtype)
            done += n


def finish_one(info, parts):
    def body(i, *refs):
        down, total = refs[4:]
        gather_parts(i, refs[:4], total)
        spread(down, total, 0, FF // 4, D // 128)

    return pl.pallas_call(
        body,
        out_shape=hbm((FF // 4, D), F32),
        in_specs=[SM] + [VM] * 4,
        out_specs=VM,
        scratch_shapes=[pltpu.VMEM((4,) + parts[0].shape, BF16)],
        compiler_params=params(),
        cost_estimate=cost(1e7, 1e7),
        name="finish_one",
    )(info, *parts)


def finish_two(info, parts_a, parts_b):
    gr = D // 4
    blocks = FH // 128

    def body(i, *refs):
        gate, up, out, total_a, total_b = refs[8:]
        gather_parts(i, refs[:4], total_a)
        gather_parts(i, refs[4:8], total_b)
        for k, total in enumerate((total_a, total_b)):
            spread(gate.at[:, pl.ds(FH * k, FH)], total, 0, gr, blocks)
            spread(up.at[:, pl.ds(FH * k, FH)], total, gr * blocks, gr, blocks)
        spread(out, total_b, 2 * gr * blocks, HEAD_DIM, D // 128)

    return pl.pallas_call(
        body,
        out_shape=(hbm((gr, FF), F32), hbm((gr, FF), F32), hbm((HEAD_DIM, D), F32)),
        in_specs=[SM] + [VM] * 8,
        out_specs=(VM,) * 3,
        scratch_shapes=[
            pltpu.VMEM((4,) + parts_a[0].shape, BF16),
            pltpu.VMEM((4,) + parts_b[0].shape, BF16),
        ],
        compiler_params=params(),
        cost_estimate=cost(1e7, 1e7),
        name="finish_two",
    )(info, *parts_a, *parts_b)


def finish_three(info, parts, query_w, key_w, value_w, gain):
    gr = D // 4

    def body(i, *refs):
        wq, wk, wv, g, query, key, value = refs[4:11]
        first, g_query, g_key, g_att, g_mid, g_out, total, prod, gains = refs[11:]
        gather_parts(i, refs[:4], total)
        spread(query, total, 0, gr, 8)
        spread(key, total, 8 * gr, gr, 2)
        spread(value, total, 10 * gr, gr, 2)
        spread(gains, total, 12 * gr, 16, 2)
        base = HEADS * HEAD_DIM
        prod[:, :base] = query[...] * wq[...].astype(F32)
        prod[:, base : base + HEAD_DIM] = key[...] * wk[...].astype(F32)
        prod[:, base + HEAD_DIM :] = value[...] * wv[...].astype(F32)
        p = prod[...]
        high = p.astype(BF16)
        low = (p - high.astype(F32)).astype(BF16)
        ones = jnp.ones((16, 6 * HEAD_DIM), BF16)
        summed = dot(ones, high, NT) + dot(ones, low, NT)
        first[...] = summed[0:1, :].reshape(-1) / g[...].astype(F32)
        for row, o in ((1, g_att), (2, g_mid), (3, g_out), (4, g_query), (5, g_key)):
            o[...] = gains[row : row + 1, : o.shape[0]].reshape(-1)

    return pl.pallas_call(
        body,
        out_shape=(
            hbm((gr, HEADS * HEAD_DIM), F32),
            hbm((gr, HEAD_DIM), F32),
            hbm((gr, HEAD_DIM), F32),
            sds((gr,), F32),
            sds((HEAD_DIM // 4,), F32),
            sds((HEAD_DIM // 4,), F32),
            sds((gr,), F32),
            sds((gr,), F32),
            sds((gr,), F32),
        ),
        in_specs=[SM] + [VM] * 8,
        out_specs=(VM,) * 9,
        scratch_shapes=[
            pltpu.VMEM((4,) + parts[0].shape, BF16),
            pltpu.VMEM((gr, 6 * HEAD_DIM), F32),
            pltpu.VMEM((16, HEAD_DIM), F32),
        ],
        compiler_params=params(),
        cost_estimate=cost(1e7, 1e7),
        name="finish_three",
    )(info, *parts, query_w, key_w, value_w, gain)


def shards(
    tokens,
    query_weight,
    key_weight,
    value_weight,
    out_weight,
    gate_weight,
    up_weight,
    down_weight,
    input_gain,
    query_gain,
    key_gain,
    attended_gain,
    middle_gain,
    output_gain,
    cotangent,
):
    n_seq = lax.axis_size("seq")
    n_shard = lax.axis_size("shard")
    shard = lax.axis_index("shard")
    count = tokens.shape[0]
    total = count * n_seq * n_shard
    length = min(SEQ_CAP, total)
    rank = lax.axis_index("seq") * n_shard + shard
    first_pos = rank * count % length
    place = Place(first_pos)
    me = flag = place.info
    gd = D // 4
    gh = HEAD_DIM // 4

    kvg = pack(
        me,
        key_weight,
        value_weight,
        input_gain,
        attended_gain,
        middle_gain,
        output_gain,
        query_gain,
        key_gain,
    )
    def near(x):
        return flip(x, "shard", 1)

    def far(x):
        return flip(x, "shard", 2)

    q_far = far(query_weight)
    kvg_far = far(kvg)
    kvgs = (kvg, near(kvg), kvg_far, near(kvg_far))
    q_near = near(query_weight)
    out_near, gate_near, up_near, down_near = (
        near(out_weight), near(gate_weight), near(up_weight), near(down_weight)
    )

    def relay(x):
        return flip(x, "seq", 1)

    gate_half, up_half, down_half = halves(me, gate_weight, up_weight, down_weight)

    positions = first_pos + jnp.arange(count, dtype=jnp.int32)
    hd = HEAD_DIM // 2
    freq = ROPE_BASE ** (-(jnp.arange(hd, dtype=F32) * 2.0 / HEAD_DIM))
    angles = positions.astype(F32)[:, None] * freq[None, :]
    cos = jnp.cos(angles)
    sin = jnp.sin(angles)

    gains = gains_of(me, kvgs)
    kvgs = pinned(*kvgs)
    nin, kraw, kv_lo, kv_hi = pre_kv(me, tokens, gains, cos, sin, kvgs)
    ranks = n_seq * n_shard
    per_seq = length // count
    pairs = [(i, i + 1) for i in range(ranks - 1) if (i + 1) % per_seq]
    halo = lax.ppermute(kv_hi, ("seq", "shard"), pairs)
    out_far = far(out_weight)
    gate_a = far(gate_half)
    q_far = after(q_far, nin)
    qs_w = pinned(query_weight, q_near, q_far, near(q_far))
    up_a = far(after(up_half, gate_a))
    gate_b = relay(gate_a)
    qraw, qs = pre_q(me, nin, gains, cos, sin, qs_w)
    qs = after(qs, out_far, gate_a)
    o_hi, pm_hi, p1_hi = att(flag, qs, kv_lo, kv_hi, False, 1)
    o_lo, pm_lo, p1_lo = att(flag, after(qs, o_hi), halo, kv_lo, True, 0)
    gate_b = after(gate_b, o_lo)
    up_a = after(up_a, o_lo)
    down_a = far(after(down_half, up_a))
    up_b = relay(up_a)
    outs = pinned(out_weight, out_near, out_far, near(out_far))
    ap, nm = mid_part(me, o_lo, o_hi, tokens, gains, outs)
    gates = pinned(gate_weight, gate_near, gate_a, gate_b, near(gate_a), near(gate_b))
    act, slope = ff(me, nm, gates)
    up_b = after(up_b, act)
    down_a = after(down_a, act)
    down_b = relay(down_a)
    ups = pinned(up_weight, up_near, up_a, up_b, near(up_a), near(up_b))
    hid, bact = ff(me, nm, ups, (act, slope))
    down_b = after(down_b, hid)
    downs = pinned(down_weight, down_near, down_a, down_b, near(down_a), near(down_b))
    block_out, dd, wd, keep, send, gain_down = down_part(
        me, hid, tokens, cotangent, ap, gains, downs
    )
    chains = {name: Chain(place) for name in "abcd"}

    def advance(order, *first):
        for name in order:
            chain = chains[name.lower()]
            if name.isupper():
                chain.parts = [after(x, *first) for x in chain.parts]
                chain.collect()
            elif chain.steps:
                chain.wait(*first)
                chain.step()

    chains["d"].add(keep, send)
    keep, send, dnm = fb(me, nm, dd, act, bact, wd, gates, ups, 0, None)
    chains["a"].add(keep, send)
    advance(ORDER[0], dnm)
    dnm = after(dnm, *place.token)
    keep, send, dnm = fb(me, nm, dd, act, bact, wd, gates, ups, 1, dnm)
    chains["b"].add(keep, send)
    advance(ORDER[1], dnm)
    keep, send, d_o, d_mid, gain_mid = fe(
        me, o_lo, o_hi, tokens, cotangent, gains, ap, after(dnm, *place.token), outs
    )
    chains["b"].add(keep, send)
    advance(ORDER[2], d_o)
    dq_lo, kv_back, kv_a, gq_lo = att_back(
        qs, qraw, halo, kv_lo, pm_lo, p1_lo, after(d_o, *place.token), gains, cos, sin, 0
    )
    returned = lax.ppermute(kv_back, ("seq", "shard"), [(j, i) for i, j in pairs])
    advance(ORDER[3], dq_lo)
    dq_hi, kv_b, kv_c, gq_hi = att_back(
        qs, qraw, kv_lo, kv_hi, pm_hi, p1_hi, after(d_o, dq_lo, *place.token), gains, cos, sin, 1
    )
    advance(ORDER[4], dq_hi)
    dkv, keep, send = post(
        me,
        nin,
        (dq_lo, after(dq_hi, *place.token)),
        (kv_a, kv_b, kv_c, returned),
        kraw,
        gains,
        cos,
        sin,
        (gq_lo, gq_hi, gain_mid, gain_down),
    )
    chains["c"].add(keep, send)
    advance(ORDER[5], keep)
    grad_tokens = last(
        me, tokens, d_mid, (dq_lo, dq_hi), after(dkv, *place.token), gains, qs_w, kvgs
    )
    advance(ORDER[6], grad_tokens)
    for name in "dacb":
        advance(name * len(chains[name].steps))
    r_down = finish_one(me, chains["d"].parts)
    r_query, r_key, r_value, *r_gains = finish_three(
        me,
        chains["c"].parts,
        query_weight,
        key_weight,
        value_weight,
        input_gain,
    )
    r_gate, r_up, r_out = finish_two(me, chains["a"].parts, chains["b"].parts)
    return (
        block_out,
        grad_tokens,
        r_query,
        r_key,
        r_value,
        r_out,
        r_gate,
        r_up,
        r_down,
        *r_gains,
    )


def solution(mesh):
    token = P(("seq", "shard"), None)
    matrix = P("shard", None)
    vector = P("shard")
    in_specs = (token,) + (matrix,) * 7 + (vector,) * 6 + (token,)
    out_specs = (token, token) + (matrix,) * 7 + (vector,) * 6
    return jax.shard_map(shards, mesh=mesh, in_specs=in_specs, out_specs=out_specs, check_vma=False)
```

```python
import jax
import jax.numpy as jnp
from jax import lax
from jax.experimental import pallas as pl
from jax.experimental.pallas import tpu as pltpu
from jax.sharding import PartitionSpec as P

D = 640
HEADS = 4
HEAD_DIM = 256
FF = 2048
WINDOW = 512
SEQ_CAP = 8192
HALF = 512
QB = 256
ROWS = HEADS * QB
CHUNK = 512

EPS = 1e-06
ROPE_BASE = 10000.0
LOG2E = 1.4426950408889634
LN2 = 0.6931471805599453
SCALE = HEAD_DIM**-0.5

F32 = jnp.float32
BF16 = jnp.bfloat16
VM = pl.BlockSpec(memory_space=pltpu.VMEM)
SM = pl.BlockSpec(memory_space=pltpu.SMEM)
HM = pl.BlockSpec(memory_space=pltpu.HBM)
NN = (((1,), (0,)), ((), ()))
NT = (((1,), (1,)), ((), ()))
TN = (((0,), (0,)), ((), ()))


def dot(a, b, dims=NN):
    return lax.dot_general(a, b, dims, preferred_element_type=F32)


def params(mib=14):
    return pltpu.CompilerParams(vmem_limit_bytes=mib * 2**20)


def sds(shape, dtype=BF16):
    return jax.ShapeDtypeStruct(shape, dtype)


def cost(flops, nbytes):
    return pl.CostEstimate(flops=int(1.5 * flops), bytes_accessed=int(1.5 * nbytes), transcendentals=0)


def rms_factor(v):
    return lax.rsqrt(jnp.mean(v * v, axis=-1, keepdims=True) + EPS)


def norm_back(v, factor, gain, incoming):
    united = v * factor
    scaled = incoming * gain
    back = factor * (scaled - united * jnp.mean(scaled * united, axis=-1, keepdims=True))
    return back, jnp.sum(incoming * united, axis=0, keepdims=True)


def offsets(me, rows):
    return (
        me * rows,
        (me + 1 - 2 * (me % 2)) * rows,
        ((me + 2) % 4) * rows,
        (3 - me) * rows,
    )


def hbm(shape, dtype=BF16):
    return pltpu.HBM(shape, dtype)


ME, XBIT, FLAG, EVEN, YBIT, SECOND, HERE = range(7)


def pin(x):
    return pltpu.with_memory_space_constraint(x, pltpu.HBM)


def pinned(*arrays):
    return tuple(pin(x) for x in arrays)


def whole(piece):
    return piece


def place_copies(me_ref, pieces, src_of, buf, rows, sems, first):
    me, b = me_ref[ME], me_ref[XBIT]
    spots = [(p, o, rows) for p, o in zip(pieces, offsets(me, rows))]
    if len(pieces) == 6:
        part = rows // 2
        far, last = spots[2][1], spots[3][1]
        spots = spots[:2]
        for base, p in ((far, pieces[2:4]), (last, pieces[4:6])):
            spots.append((p[0], base + b * part, part))
            spots.append((p[1], base + (1 - b) * part, part))
    copies = []
    for k, (piece, off, n) in enumerate(spots):
        copies.append(
            pltpu.make_async_copy(
                src_of(piece), buf.at[pl.ds(pl.multiple_of(off, 16), n)], sems.at[first + k]
            )
        )
    return copies


def pack_kernel(info, k, v, g0, g1, g2, g3, g4, g5, out, r0, r1, r2, r3, r4, r5, sems):
    rows = D // 4
    gains = (g0, g1, g2, g3, g4, g5)
    places = (r0, r1, r2, r3, r4, r5)
    copies = [
        pltpu.make_async_copy(k, out.at[pl.ds(0, rows), pl.ds(0, HEAD_DIM)], sems.at[0]),
        pltpu.make_async_copy(v, out.at[pl.ds(0, rows), pl.ds(HEAD_DIM, HEAD_DIM)], sems.at[1]),
    ]
    for i in range(6):
        copies.append(pltpu.make_async_copy(gains[i], places[i], sems.at[2 + i]))
    for c in copies:
        c.start()
    out[rows:, :] = jnp.zeros((16, 2 * HEAD_DIM), BF16)
    for c in copies:
        c.wait()
    for i, r in enumerate(places):
        out[rows + i : rows + i + 1, : r.shape[0]] = r[...].reshape(1, -1)


def pack(info, k, v, *gains):
    return pl.pallas_call(
        pack_kernel,
        out_shape=sds((D // 4 + 16, 2 * HEAD_DIM)),
        in_specs=[SM] + [HM] * 8,
        out_specs=VM,
        scratch_shapes=[pltpu.VMEM(g.shape, BF16) for g in gains] + [pltpu.SemaphoreType.DMA((8,))],
        compiler_params=params(),
        cost_estimate=cost(1e6, 4e5),
        name="pack",
    )(info, *(pin(w) for w in (k, v) + gains))


def halves_kernel(info, *refs):
    n = len(refs) // 2
    ins, outs, sems = refs[:n], refs[n : 2 * n], refs[2 * n]
    copies = []
    for i, (w, o) in enumerate(zip(ins, outs)):
        rows = w.shape[0] // 2
        at = pl.multiple_of(info[XBIT] * rows, 16)
        copies.append(pltpu.make_async_copy(w.at[pl.ds(at, rows)], o, sems.at[i]))
    for c in copies:
        c.start()
    for c in copies:
        c.wait()


def halves(info, *weights):
    return pl.pallas_call(
        halves_kernel,
        out_shape=tuple(sds((w.shape[0] // 2, w.shape[1])) for w in weights),
        in_specs=[SM] + [HM] * len(weights),
        out_specs=(VM,) * len(weights),
        scratch_shapes=[pltpu.SemaphoreType.DMA((len(weights),))],
        compiler_params=params(),
        cost_estimate=cost(1e6, 2e6),
        name="halves",
    )(info, *(pin(w) for w in weights))


def gains_kernel(me_ref, g0, g1, g2, g3, out):
    gd = D // 4
    gh = HEAD_DIM // 4
    wide = jnp.zeros((16, D), F32)
    small = jnp.zeros((16, HEAD_DIM), F32)
    spots = offsets(me_ref[ME], 1)
    for spot, g in zip(spots, (g0, g1, g2, g3)):
        piece = g[...]
        row = lax.broadcasted_iota(jnp.int32, (HEAD_DIM, D), 0)
        col = lax.broadcasted_iota(jnp.int32, (HEAD_DIM, D), 1)
        place = ((col == row + spot * gd) & (row < gd)).astype(BF16)
        wide = wide + dot(piece, place)
        row = lax.broadcasted_iota(jnp.int32, (HEAD_DIM, HEAD_DIM), 0)
        col = lax.broadcasted_iota(jnp.int32, (HEAD_DIM, HEAD_DIM), 1)
        place = ((col == row + spot * gh) & (row < gh)).astype(BF16)
        small = small + dot(piece, place)
    out[0:4, :] = wide[0:4, :]
    out[4:8, :] = jnp.zeros((4, D), F32)
    out[4:8, :HEAD_DIM] = small[4:8, :]


def gains_of(me, pieces):
    part = pl.BlockSpec((16, HEAD_DIM), lambda i: (D // 4 // 16, 0))
    return pl.pallas_call(
        gains_kernel,
        grid=(1,),
        out_shape=sds((8, D), F32),
        in_specs=[SM] + [part] * 4,
        out_specs=VM,
        compiler_params=params(),
        cost_estimate=cost(1e8, 1e5),
        name="gains",
    )(me, *pieces)


def rotated(u, cos, sin):
    hd = HEAD_DIM // 2
    u1 = u[:, :hd]
    u2 = u[:, hd:]
    return (u1 * cos - u2 * sin).astype(BF16), (u2 * cos + u1 * sin).astype(BF16)


def pre_kv_kernel(me_ref, tok, gains, cos_ref, sin_ref, w0, w1, w2, w3, nin_o, kraw_o, lo_o, hi_o, wbuf, sems):
    rows = D // 4
    copies = place_copies(
        me_ref, (w0, w1, w2, w3), lambda w: w.at[pl.ds(0, rows)], wbuf, rows, sems, 0
    )
    for c in copies:
        c.start()
    hd = HEAD_DIM // 2
    x = tok[...].astype(F32)
    nin = (x * rms_factor(x) * gains[0:1, :]).astype(BF16)
    nin_o[...] = nin
    for c in copies:
        c.wait()
    k = dot(nin, wbuf[:, :HEAD_DIM])
    kraw_o[...] = k.astype(BF16)
    r1, r2 = rotated(k * rms_factor(k) * gains[5:6, :HEAD_DIM], cos_ref[...], sin_ref[...])
    v = dot(nin, wbuf[:, HEAD_DIM:]).astype(BF16)
    for half, o in enumerate((lo_o, hi_o)):
        sl = slice(HALF * half, HALF * (half + 1))
        o[:, :hd] = r1[sl]
        o[:, hd:HEAD_DIM] = r2[sl]
        o[:, HEAD_DIM:] = v[sl]


def pre_kv(me, tok, gains, cos, sin, pieces):
    t = tok.shape[0]
    return pl.pallas_call(
        pre_kv_kernel,
        out_shape=(
            sds((t, D)),
            sds((t, HEAD_DIM)),
            sds((HALF, 2 * HEAD_DIM)),
            sds((HALF, 2 * HEAD_DIM)),
        ),
        in_specs=[SM, VM, VM, VM, VM, HM, HM, HM, HM],
        out_specs=(VM,) * 4,
        scratch_shapes=[pltpu.VMEM((D, 2 * HEAD_DIM), BF16), pltpu.SemaphoreType.DMA((4,))],
        compiler_params=params(),
        cost_estimate=cost(2 * t * D * 512, 5e6),
        name="pre_kv",
    )(me, tok, gains, cos, sin, *pieces)


def pre_q_kernel(me_ref, nin_i, gains, cos_ref, sin_ref, w0, w1, w2, w3, qraw_o, qs_o, wbuf, sems):
    rows = D // 4
    hd = HEAD_DIM // 2

    @pl.when(pl.program_id(0) == 0)
    def _():
        copies = place_copies(
            me_ref, (w0, w1, w2, w3), lambda w: w.at[pl.ds(0, rows)], wbuf, rows, sems, 0
        )
        for c in copies:
            c.start()
        for c in copies:
            c.wait()

    q = dot(nin_i[...], wbuf[:, pl.ds(pl.multiple_of(pl.program_id(0) * HEAD_DIM, HEAD_DIM), HEAD_DIM)])
    qraw_o[0] = q.astype(BF16)
    u = q * (rms_factor(q) * (SCALE * LOG2E)) * gains[4:5, :HEAD_DIM]
    r1, r2 = rotated(u, cos_ref[...], sin_ref[...])
    qs_o[0, :, :hd] = r1
    qs_o[0, :, hd:] = r2


def pre_q(me, nin, gains, cos, sin, pieces):
    t = nin.shape[0]
    head = pl.BlockSpec((1, t, HEAD_DIM), lambda h: (h, 0, 0))
    return pl.pallas_call(
        pre_q_kernel,
        grid=(HEADS,),
        out_shape=(hbm((HEADS, t, HEAD_DIM)), sds((HEADS, t, HEAD_DIM))),
        in_specs=[SM, VM, VM, VM, VM, HM, HM, HM, HM],
        out_specs=(head, head),
        scratch_shapes=[pltpu.VMEM((D, HEADS * HEAD_DIM), BF16), pltpu.SemaphoreType.DMA((4,))],
        compiler_params=params(),
        cost_estimate=cost(2 * t * D * 1024, 5e6),
        name="pre_q",
    )(me, nin, gains, cos, sin, *pieces)


def key_blocks(j, kvp, kvs, lo, hi):
    blocks = (kvp[0:QB, lo:hi], kvp[QB : 2 * QB, lo:hi], kvs[0:QB, lo:hi], kvs[QB : 2 * QB, lo:hi])
    return blocks[j : j + 3]


def upper_mask():
    row = lax.broadcasted_iota(jnp.int32, (HEADS, QB, QB), 1).reshape(ROWS, QB)
    col = lax.broadcasted_iota(jnp.int32, (ROWS, QB), 1)
    return col > row


def att_kernel(masked, flag_ref, qs, kvp, kvs, o_o, pm_o, p1_o):
    upper = upper_mask()
    for j in range(2):
        sl = slice(QB * j, QB * (j + 1))
        q = qs[:, sl, :].reshape(ROWS, HEAD_DIM)
        k0, k1, k2 = key_blocks(j, kvp, kvs, 0, HEAD_DIM)
        v0, v1, v2 = key_blocks(j, kvp, kvs, HEAD_DIM, 2 * HEAD_DIM)
        em = jnp.exp2(jnp.where(upper, dot(q, k0, NT), dot(q, k2, NT)))
        e1 = jnp.exp2(dot(q, k1, NT))
        if masked:
            keep = flag_ref[FLAG].astype(F32)
            em = em * jnp.where(upper, keep, 1.0)
            if j == 0:
                e1 = e1 * keep
        inv = 1.0 / jnp.sum(em + e1, axis=-1, keepdims=True)
        pm = (em * inv).astype(BF16)
        p1 = (e1 * inv).astype(BF16)
        zero = jnp.zeros_like(pm)
        out = dot(p1, v1) + dot(jnp.where(upper, pm, zero), v0) + dot(jnp.where(upper, zero, pm), v2)
        pm_o[:, sl, :] = pm.reshape(HEADS, QB, QB)
        p1_o[:, sl, :] = p1.reshape(HEADS, QB, QB)
        for h in range(HEADS):
            o_o[sl, HEAD_DIM * h : HEAD_DIM * (h + 1)] = out[QB * h : QB * (h + 1), :].astype(BF16)


def half_spec(half):
    return pl.BlockSpec((HEADS, HALF, HEAD_DIM), lambda i: (0, half, 0))


def att(flag, qs, kvp, kvs, masked, half):
    shp = sds((HEADS, HALF, HEAD_DIM))

    def body(*refs):
        att_kernel(masked, *refs)

    return pl.pallas_call(
        body,
        grid=(1,),
        out_shape=(sds((HALF, HEADS * HEAD_DIM)), shp, shp),
        in_specs=[SM, half_spec(half), VM, VM],
        out_specs=(VM,) * 3,
        compiler_params=params(),
        cost_estimate=cost(12e9 / 4, 5e6),
        name="att",
    )(flag, qs, kvp, kvs)


def att_back_kernel(qs, qraw, kvp, kvs, pm_i, p1_i, do_i, gains, cos_ref, sin_ref, dq_o, dkvp_o, dkvs_o, gain_o, acc):
    upper = upper_mask()
    hd = HEAD_DIM // 2
    acc[...] = jnp.zeros_like(acc)
    gsum = jnp.zeros((1, HEAD_DIM), F32)
    for j in range(2):
        sl = slice(QB * j, QB * (j + 1))
        q = qs[:, sl, :].reshape(ROWS, HEAD_DIM)
        do = do_i[:, sl, :].reshape(ROWS, HEAD_DIM)
        k0, k1, k2 = key_blocks(j, kvp, kvs, 0, HEAD_DIM)
        v0, v1, v2 = key_blocks(j, kvp, kvs, HEAD_DIM, 2 * HEAD_DIM)
        pmb = pm_i[:, sl, :].reshape(ROWS, QB)
        p1b = p1_i[:, sl, :].reshape(ROWS, QB)
        dpm = jnp.where(upper, dot(do, v0, NT), dot(do, v2, NT))
        dp1 = dot(do, v1, NT)
        pm = pmb.astype(F32)
        p1 = p1b.astype(F32)
        total = jnp.sum(pm * dpm + p1 * dp1, axis=-1, keepdims=True)
        dsm = (pm * (dpm - total)).astype(BF16)
        ds1 = (p1 * (dp1 - total)).astype(BF16)
        zero = jnp.zeros_like(dsm)
        ds0 = jnp.where(upper, dsm, zero)
        ds2 = jnp.where(upper, zero, dsm)
        p0 = jnp.where(upper, pmb, zero)
        p2 = jnp.where(upper, zero, pmb)
        for t, (ds, p) in enumerate(((ds0, p0), (ds1, p1b), (ds2, p2))):
            at = slice(QB * (j + t), QB * (j + t + 1))
            acc[at, :HEAD_DIM] += dot(ds, q, TN) * LN2
            acc[at, HEAD_DIM:] += dot(p, do, TN)
        dq = (dot(ds0, k0) + dot(ds1, k1) + dot(ds2, k2)) * SCALE
        cos = cos_ref[sl, :]
        sin = sin_ref[sl, :]
        gain = gains[4:5, :HEAD_DIM]
        for h in range(HEADS):
            d1 = dq[QB * h : QB * (h + 1), :hd]
            d2 = dq[QB * h : QB * (h + 1), hd:]
            inc = jnp.concatenate([d1 * cos + d2 * sin, d2 * cos - d1 * sin], axis=-1)
            raw = qraw[h, sl, :].astype(F32)
            back, terms = norm_back(raw, rms_factor(raw), gain, inc)
            gsum = gsum + terms
            dq_o[sl, HEAD_DIM * h : HEAD_DIM * (h + 1)] = back.astype(BF16)
    dkvp_o[...] = acc[:HALF, :].astype(BF16)
    dkvs_o[...] = acc[HALF:, :]
    gain_o[...] = jnp.broadcast_to(gsum, (8, HEAD_DIM))


def att_back(qs, qraw, kvp, kvs, pm, p1, do, gains, cos, sin, half):
    dospec = half_spec(half)
    tab = pl.BlockSpec((HALF, HEAD_DIM // 2), lambda i: (half, 0))
    return pl.pallas_call(
        att_back_kernel,
        grid=(1,),
        out_shape=(
            sds((HALF, HEADS * HEAD_DIM)),
            sds((HALF, 2 * HEAD_DIM)),
            sds((HALF, 2 * HEAD_DIM), F32),
            sds((8, HEAD_DIM), F32),
        ),
        in_specs=[dospec, dospec, VM, VM, VM, VM, dospec, VM, tab, tab],
        out_specs=(VM,) * 4,
        scratch_shapes=[pltpu.VMEM((2 * HALF, 2 * HEAD_DIM), F32)],
        compiler_params=params(),
        cost_estimate=cost(24e9 / 4, 9e6),
        name="att_back",
    )(qs, qraw, kvp, kvs, pm, p1, do, gains, cos, sin)


def mid_kernel(me_ref, o_lo, o_hi, tok, gains, w0, w1, w2, w3, ap_o, nm_o, wo, sems):
    ro = HEADS * HEAD_DIM // 4
    copies = place_copies(me_ref, (w0, w1, w2, w3), lambda w: w, wo, ro, sems, 0)
    for c in copies:
        c.start()
    for c in copies:
        c.wait()
    for half, o in enumerate((o_lo, o_hi)):
        sl = slice(HALF * half, HALF * (half + 1))
        proj = dot(o[...], wo[...])
        ap_o[sl, :] = proj.astype(BF16)
        mid = tok[sl, :].astype(F32) + proj * rms_factor(proj) * gains[1:2, :]
        nm_o[sl, :] = (mid * rms_factor(mid) * gains[2:3, :]).astype(BF16)


def mid_part(me, o_lo, o_hi, tok, gains, outs):
    t = tok.shape[0]
    return pl.pallas_call(
        mid_kernel,
        out_shape=(sds((t, D)), sds((t, D))),
        in_specs=[SM] + [VM] * 4 + [HM] * 4,
        out_specs=(VM, VM),
        scratch_shapes=[
            pltpu.VMEM((HEADS * HEAD_DIM, D), BF16),
            pltpu.SemaphoreType.DMA((4,)),
        ],
        compiler_params=params(),
        cost_estimate=cost(2 * t * D * 1024, 8e6),
        name="mid",
    )(me, o_lo, o_hi, tok, gains, *outs)


FH = FF // 2
STEP = 512
WIDE = 512
RB = 512


def by_columns(me_ref, pieces, buf, sems, body):
    def copies(i):
        at = pl.ds(pl.multiple_of(i * STEP, STEP), STEP)
        return place_copies(
            me_ref, pieces, lambda w: w.at[:, at], buf.at[:, at], D // 4, sems, 6 * i
        )

    for i in range(FF // STEP):
        for c in copies(i):
            c.start()

    def step(i, carry):
        for c in copies(i):
            c.wait()
        body(pl.ds(pl.multiple_of(i * STEP, STEP), STEP))
        return carry

    lax.fori_loop(0, FF // STEP, step, 0)


def gate_kernel(me_ref, nm, *rest):
    pieces, (a_o, s_o, wg, sems) = rest[:6], rest[6:]
    c0 = 0.7978845608028654
    c1 = 0.044715 * c0

    def body(cs):
        for r in range(0, nm.shape[0], RB):
            rs = slice(r, r + RB)
            g = dot(nm[rs, :], wg[:, cs]).astype(BF16)
            g2 = g * g
            t = jnp.tanh(g * (c0 + c1 * g2))
            h = 0.5 + 0.5 * t
            a = g * h
            a_o[rs, cs] = a
            s_o[rs, cs] = h + a * (1.0 - h) * (2.0 * c0 + (6.0 * c1) * g2)

    by_columns(me_ref, pieces, wg, sems, body)


def up_kernel(me_ref, nm, a_i, s_i, *rest):
    pieces, (hid_o, b_o, wu, sems) = rest[:6], rest[6:]

    def body(cs):
        for r in range(0, nm.shape[0], RB):
            rs = slice(r, r + RB)
            u = dot(nm[rs, :], wu[:, cs]).astype(BF16)
            hid_o[rs, cs] = a_i[rs, cs] * u
            b_o[rs, cs] = u * s_i[rs, cs]

    by_columns(me_ref, pieces, wu, sems, body)


def ff(me, nm, pieces, before=()):
    t = nm.shape[0]
    return pl.pallas_call(
        up_kernel if before else gate_kernel,
        out_shape=(sds((t, FF)),) * 2,
        in_specs=[SM, VM] + [VM] * len(before) + [HM] * 6,
        out_specs=(VM,) * 2,
        scratch_shapes=[pltpu.VMEM((D, FF), BF16), pltpu.SemaphoreType.DMA((6 * FF // STEP,))],
        compiler_params=params(),
        cost_estimate=cost(2 * t * D * FF, 12e6),
        name="up" if before else "gate",
    )(me, nm, *before, *pieces)


def down_kernel(me_ref, hid, tok, cot, ap, gains, *rest):
    pieces, (out_o, dd_o, wd_o, keep_o, send_o, gain_o, sems) = rest[:6], rest[6:]
    rf = FF // 4
    core = me_ref[ME] % 2
    copies = place_copies(me_ref, pieces, whole, wd_o, rf, sems, 0)
    for c in copies:
        c.start()
    for c in copies:
        c.wait()
    gsum = jnp.zeros((1, D), F32)
    for half in range(2):
        sl = slice(HALF * half, HALF * (half + 1))
        dn = dot(hid[sl, :], wd_o[...])
        proj = ap[sl, :].astype(F32)
        mid = tok[sl, :].astype(F32) + proj * rms_factor(proj) * gains[1:2, :]
        fac = rms_factor(dn)
        out_o[sl, :] = (mid + dn * fac * gains[3:4, :]).astype(BF16)
        back, terms = norm_back(dn, fac, gains[3:4, :], cot[sl, :].astype(F32))
        dd_o[sl, :] = back.astype(BF16)
        gsum = gsum + terms
    gain_o[...] = jnp.broadcast_to(gsum, (8, D))
    for y in range(2):
        for part, o in ((core, keep_o), (1 - core, send_o)):
            at = pl.ds(pl.multiple_of((2 * y + part) * rf, rf), rf)
            g = dot(hid[:, at], dd_o[...], TN).astype(BF16)
            for j in range(D // 128):
                o[y, j] = g[:, 128 * j : 128 * (j + 1)]


def down_part(me, hid, tok, cot, ap, gains, pieces):
    t = tok.shape[0]
    return pl.pallas_call(
        down_kernel,
        out_shape=(
            sds((t, D)),
            sds((t, D)),
            sds((FF, D)),
            sds((2, D // 128, FF // 4, 128)),
            sds((2, D // 128, FF // 4, 128)),
            sds((8, D), F32),
        ),
        in_specs=[SM] + [VM] * 5 + [HM] * 6,
        out_specs=(VM,) * 6,
        scratch_shapes=[pltpu.SemaphoreType.DMA((6,))],
        compiler_params=params(),
        cost_estimate=cost(4 * t * D * FF, 20e6),
        name="down",
    )(me, hid, tok, cot, ap, gains, *pieces)


def fb_kernel(half, me_ref, nm, dd, a_i, b_i, wd, *rest):
    gates, ups, rest = rest[:6], rest[6:12], rest[12:]
    first = half == 0
    if first:
        keep_o, send_o, dnm_o, wg, wu, gs, sems = rest
    else:
        dnm_i, keep_o, send_o, dnm_o, wg, wu, gs, sems = rest
    core = me_ref[ME] % 2

    copies = []
    for k, (pieces, buf) in enumerate(((gates, wg), (ups, wu))):
        copies += place_copies(
            me_ref, pieces, lambda w: w.at[:, pl.ds(FH * half, FH)], buf, D // 4, sems, 6 * k
        )
    for c in copies:
        c.start()
    gr = D // 4
    for i in range(FH // WIDE):
        cs = slice(WIDE * i, WIDE * (i + 1))
        at = slice(FH * half + WIDE * i, FH * half + WIDE * (i + 1))
        dh = dot(dd[...], wd[at, :], NT).astype(BF16)
        dg = dh * b_i[:, at]
        du = dh * a_i[:, at]
        for k, d in enumerate((dg, du)):
            gs[k] = dot(nm[...], d, TN).astype(BF16)
            for y in range(2):
                for part, o in ((core, keep_o), (1 - core, send_o)):
                    rows = pl.ds(pl.multiple_of((2 * y + part) * gr, gr), gr)
                    for j in range(WIDE // 128):
                        to = WIDE // 128 * i + j
                        o[y, k, to] = gs[k, rows, 128 * j : 128 * (j + 1)]
        if i == 0:
            for c in copies:
                c.wait()
        back = dot(dg, wg[:, cs], NT) + dot(du, wu[:, cs], NT)
        if i > 0:
            dnm_o[...] += back
        elif first:
            dnm_o[...] = back
        else:
            dnm_o[...] = dnm_i[...] + back


def fb(me, nm, dd, a, b, wd, gates, ups, part, dnm):
    t = nm.shape[0]
    extra = () if dnm is None else (dnm,)

    def body(*refs):
        fb_kernel(part, *refs)

    return pl.pallas_call(
        body,
        out_shape=(sds((2, 2, FH // 128, D // 4, 128)),) * 2 + (sds((t, D), F32),),
        in_specs=[SM] + [VM] * 5 + [HM] * 12 + [VM] * len(extra),
        out_specs=(VM,) * 3,
        scratch_shapes=[
            pltpu.VMEM((D, FH), BF16),
            pltpu.VMEM((D, FH), BF16),
            pltpu.VMEM((2, D, WIDE), BF16),
            pltpu.SemaphoreType.DMA((12,)),
        ],
        compiler_params=params(16),
        cost_estimate=cost(10 * t * D * FH, 16e6),
        name="fb",
    )(me, nm, dd, a, b, wd, *gates, *ups, *extra)


def fe_kernel(me_ref, o_lo, o_hi, tok, cot, gains, ap, dnm, w0, w1, w2, w3, keep_o, send_o, do_o, dmid_o, gain_o, wo, datt, sems):
    ro = HEADS * HEAD_DIM // 4
    copies = place_copies(me_ref, (w0, w1, w2, w3), lambda w: w, wo, ro, sems, 0)
    for c in copies:
        c.start()
    gm = jnp.zeros((1, D), F32)
    ga = jnp.zeros((1, D), F32)
    for half in range(2):
        sl = slice(HALF * half, HALF * (half + 1))
        proj = ap[sl, :].astype(F32)
        pfac = rms_factor(proj)
        mid = tok[sl, :].astype(F32) + proj * pfac * gains[1:2, :]
        back, terms = norm_back(mid, rms_factor(mid), gains[2:3, :], dnm[sl, :])
        dmid = cot[sl, :].astype(F32) + back
        gm = gm + terms
        dmid_o[sl, :] = dmid.astype(BF16)
        back, terms = norm_back(proj, pfac, gains[1:2, :], dmid)
        ga = ga + terms
        datt[sl, :] = back.astype(BF16)
    gain_o[0:8, :] = jnp.broadcast_to(gm, (8, D))
    gain_o[8:16, :] = jnp.broadcast_to(ga, (8, D))
    for c in copies:
        c.wait()
    for h in range(HEADS):
        at = slice(HEAD_DIM * h, HEAD_DIM * (h + 1))
        do_o[h] = dot(datt[...], wo[at, :], NT).astype(BF16)
    core = me_ref[ME] % 2
    for y in range(2):
        for part, o in ((core, keep_o), (1 - core, send_o)):
            cs = pl.ds(pl.multiple_of((2 * y + part) * HEAD_DIM, HEAD_DIM), HEAD_DIM)
            g = dot(o_lo[:, cs], datt[:HALF, :], TN) + dot(o_hi[:, cs], datt[HALF:, :], TN)
            g = g.astype(BF16)
            for j in range(D // 128):
                o[y, j] = g[:, 128 * j : 128 * (j + 1)]


def fe(me, o_lo, o_hi, tok, cot, gains, ap, dnm, outs):
    t = tok.shape[0]
    return pl.pallas_call(
        fe_kernel,
        out_shape=(
            sds((2, D // 128, HEAD_DIM, 128)),
            sds((2, D // 128, HEAD_DIM, 128)),
            sds((HEADS, t, HEAD_DIM)),
            sds((t, D)),
            sds((16, D), F32),
        ),
        in_specs=[SM] + [VM] * 7 + [HM] * 4,
        out_specs=(VM,) * 5,
        scratch_shapes=[
            pltpu.VMEM((HEADS * HEAD_DIM, D), BF16),
            pltpu.VMEM((t, D), BF16),
            pltpu.SemaphoreType.DMA((4,)),
        ],
        compiler_params=params(),
        cost_estimate=cost(4 * t * D * 1024, 14e6),
        name="fe",
    )(me, o_lo, o_hi, tok, cot, gains, ap, dnm, *outs)


LAST = 2048


def post_kernel(
    me_ref, nin, dq_lo, dq_hi, kv_a, kv_b, kv_c, kv_d, kraw,
    gains, cos_ref, sin_ref, gq_lo, gq_hi, gmid, gdown,
    dkv, keep_o, send_o,
    gs, sums, small,
):
    rows = D // 4
    hd = HEAD_DIM // 2
    gk = jnp.zeros((1, HEAD_DIM), F32)
    for half, (first, second) in enumerate(((kv_a, kv_b), (kv_c, kv_d))):
        sl = slice(HALF * half, HALF * (half + 1))
        both = first[...].astype(F32) + second[...].astype(F32)
        cos = cos_ref[sl, :]
        sin = sin_ref[sl, :]
        d1 = both[:, :hd]
        d2 = both[:, hd:HEAD_DIM]
        inc = jnp.concatenate([d1 * cos + d2 * sin, d2 * cos - d1 * sin], axis=-1)
        raw = kraw[sl, :].astype(F32)
        back, terms = norm_back(raw, rms_factor(raw), gains[5:6, :HEAD_DIM], inc)
        gk = gk + terms
        dkv[sl, :HEAD_DIM] = back.astype(BF16)
        dkv[sl, HEAD_DIM:] = both[:, HEAD_DIM:].astype(BF16)

    core = me_ref[ME] % 2

    def put(slot, g):
        gs[slot] = g.astype(BF16)
        for y in range(2):
            for part, o in ((core, keep_o), (1 - core, send_o)):
                at = pl.ds(pl.multiple_of((2 * y + part) * rows, rows), rows)
                for j in range(2):
                    to = (2 * slot + j) * rows
                    o[y, to : to + rows, :] = gs[slot, at, 128 * j : 128 * (j + 1)]

    for h in range(HEADS):
        cs = slice(HEAD_DIM * h, HEAD_DIM * (h + 1))
        put(h, dot(nin[:HALF, :], dq_lo[:, cs], TN) + dot(nin[HALF:, :], dq_hi[:, cs], TN))
    put(HEADS, dot(nin[...], dkv[:, :HEAD_DIM], TN))
    put(HEADS + 1, dot(nin[...], dkv[:, HEAD_DIM:], TN))
    sums[...] = jnp.zeros_like(sums)
    small[...] = jnp.zeros_like(small)
    sums[1:2, :] = gmid[8:9, :]
    sums[2:3, :] = gmid[0:1, :]
    sums[3:4, :] = gdown[0:1, :]
    small[4:5, :] = gq_lo[0:1, :] + gq_hi[0:1, :]
    small[5:6, :] = gk
    gd = D // 4
    gh = HEAD_DIM // 4
    base = 12 * rows
    for y in range(2):
        for part, o in ((core, keep_o), (1 - core, send_o)):
            s = 2 * y + part
            row = lax.broadcasted_iota(jnp.int32, (D, HEAD_DIM), 0)
            col = lax.broadcasted_iota(jnp.int32, (D, HEAD_DIM), 1)
            place = ((row == col + s * gd) & (col < gd)).astype(BF16)
            g = dot(sums[...].astype(BF16), place)
            row = lax.broadcasted_iota(jnp.int32, (HEAD_DIM, HEAD_DIM), 0)
            col = lax.broadcasted_iota(jnp.int32, (HEAD_DIM, HEAD_DIM), 1)
            place = ((row == col + s * gh) & (col < gh)).astype(BF16)
            g = (g + dot(small[...].astype(BF16), place)).astype(BF16)
            o[y, base : base + 16, :] = g[:, :128]
            o[y, base + 16 : base + 32, :] = g[:, 128:]
            o[y, base + 32 :, :] = jnp.zeros((LAST - base - 32, 128), BF16)


def post(me, nin, dqs, kvs, kraw, gains, cos, sin, sums):
    t = nin.shape[0]
    return pl.pallas_call(
        post_kernel,
        out_shape=(
            sds((t, 2 * HEAD_DIM)),
            sds((2, LAST, 128)),
            sds((2, LAST, 128)),
        ),
        in_specs=[SM] + [VM] * 15,
        out_specs=(VM,) * 3,
        scratch_shapes=[
            pltpu.VMEM((HEADS + 2, D, HEAD_DIM), BF16),
            pltpu.VMEM((16, D), F32),
            pltpu.VMEM((16, HEAD_DIM), F32),
        ],
        compiler_params=params(),
        cost_estimate=cost(2e9, 10e6),
        name="post",
    )(me, nin, *dqs, *kvs, kraw, gains, cos, sin, *sums)


def last_kernel(me_ref, tok, dmid, dq_lo, dq_hi, dkv, gains, q0, q1, q2, q3, k0, k1, k2, k3, gt_o, wq, wkv, sems):
    rows = D // 4
    copies = place_copies(me_ref, (q0, q1, q2, q3), whole, wq, rows, sems, 0)
    copies += place_copies(
        me_ref, (k0, k1, k2, k3), lambda w: w.at[pl.ds(0, rows)], wkv, rows, sems, 4
    )
    for c in copies:
        c.start()
    for c in copies:
        c.wait()
    for half, dq in enumerate((dq_lo, dq_hi)):
        for r in range(0, HALF, RB):
            rs = slice(HALF * half + r, HALF * half + r + RB)
            dnin = dot(dq[r : r + RB, :], wq[...], NT) + dot(dkv[rs, :], wkv[...], NT)
            x = tok[rs, :].astype(F32)
            back, _ = norm_back(x, rms_factor(x), gains[0:1, :], dnin)
            gt_o[rs, :] = (dmid[rs, :].astype(F32) + back).astype(BF16)


def last(me, tok, dmid, dqs, dkv, gains, qs, kvgs):
    t = tok.shape[0]
    return pl.pallas_call(
        last_kernel,
        out_shape=hbm((t, D)),
        in_specs=[SM] + [VM] * 6 + [HM] * 8,
        out_specs=VM,
        scratch_shapes=[
            pltpu.VMEM((D, HEADS * HEAD_DIM), BF16),
            pltpu.VMEM((D, 2 * HEAD_DIM), BF16),
            pltpu.SemaphoreType.DMA((8,)),
        ],
        compiler_params=params(),
        cost_estimate=cost(2e9, 8e6),
        name="last",
    )(me, tok, dmid, *dqs, dkv, gains, *qs, *kvgs)


def flip(x, axis, bit):
    n = lax.axis_size(axis)
    return lax.ppermute(x, axis, [(i, i ^ bit) for i in range(n)])


def pick(x, index, axis=0):
    return lax.dynamic_index_in_dim(x, index, axis, keepdims=False)


def after(x, *first):
    return lax.optimization_barrier((x,) + first)[0]


def joined(a, b):
    return (a.astype(F32) + b.astype(F32)).astype(BF16)


def small_call(body, name, out_rows, scalars, *arrays, scratch=()):
    size = sum(a.size for a in arrays)
    return pl.pallas_call(
        body,
        out_shape=tuple(sds(r + (128,)) for r in out_rows),
        in_specs=[SM] + [VM] * len(arrays),
        out_specs=(VM,) * len(out_rows),
        scratch_shapes=scratch,
        compiler_params=params(),
        cost_estimate=cost(size, 4 * size),
        name=name,
    )(scalars, *arrays)


def mix_first(scalars, keeps, gots):
    n = len(keeps)
    sizes = [k.shape[1] for k in keeps]
    rows = sum(sizes)

    def body(s, *refs):
        ks, gs = refs[:n], refs[n : 2 * n]
        send, keep, total = refs[2 * n :]
        at = 0
        for k, g, size in zip(ks, gs, sizes):
            for y in range(2):
                total[y, at : at + size, :] = joined(k[y], g[y])
            at += size
        even, y, x = s[EVEN], s[YBIT], s[XBIT]
        for t in range(2):
            for o, flip_it in ((send, 1), (keep, 0)):
                own_y = flip_it + y - 2 * flip_it * y
                own_x = flip_it + x - 2 * flip_it * x
                row = even * own_y + (1 - even) * t
                half = even * t + (1 - even) * own_x
                o[t] = total[row, pl.ds(pl.multiple_of(half * (rows // 2), 16), rows // 2), :]

    shape = (2, rows // 2)
    return small_call(
        body, "mix_first", (shape, shape), scalars, *keeps, *gots,
        scratch=[pltpu.VMEM((2, rows, 128), BF16)],
    )


def mix_half(info, index, keep, got):
    keep = keep.reshape(2, -1, 128)
    got = got.reshape(2, -1, 128)

    def body(i, k, g, send, kept):
        own = i[index]
        send[...] = joined(k[1 - own], g[1 - own])
        kept[...] = joined(k[own], g[own])

    shape = (keep.shape[1],)
    return small_call(body, "mix_half", (shape, shape), info, keep, got)


def mix_sum(info, keep, got):
    def body(i, k, g, o):
        o[...] = joined(k[...], g[...])

    return small_call(body, "mix_sum", (keep.shape[:1],), info, keep, got)[0]


def mix_both(info, index, own, other):
    rows = own.shape[0]

    def body(i, a, b, o):
        o[i[index]] = a[...]
        o[1 - i[index]] = b[...]

    return small_call(body, "mix_both", ((2, rows),), info, own, other)[0].reshape(2 * rows, 128)


class Place:
    def __init__(self, first_pos):
        shard = lax.axis_index("shard")
        seq = lax.axis_index("seq")
        self.n_shard = lax.axis_size("shard")
        self.n = lax.axis_size("seq") * self.n_shard
        core = shard & 1
        y = shard >> 1
        x = seq & 1
        bits = []
        bit = 1
        while bit < lax.axis_size("seq"):
            bits.append(bit)
            bit *= 2
        self.far = [self.n_shard * b for b in bits]
        here = [(seq >> i) & 1 for i in range(len(bits))]
        flag = (first_pos > 0).astype(jnp.int32)
        second = jnp.where(core == 0, x, y)
        self.token = ()
        self.info = jnp.stack([shard, x, flag, 1 - core, y, second] + here).astype(jnp.int32)

    def send(self, x, even, odd):
        pairs = [(i, i ^ (even if i % 2 == 0 else odd)) for i in range(self.n)]
        return lax.ppermute(x, ("seq", "shard"), pairs)


ORDER = ("d", "da", "da", "dab", "da", "b", "acbcbcbccb")


class Chain:
    def __init__(self, place):
        self.place = place
        self.keeps = []
        self.gots = []
        self.keep = None
        n = len(place.far)
        self.steps = [self.start, self.second]
        self.steps += [lambda i=i: self.halve(i) for i in range(1, n - 1)]
        self.steps += [self.exchange]
        self.steps += [lambda i=i: self.double(i) for i in range(n - 2, 1, -1)]
        self.steps += [self.spread]
        self.count = len(self.steps)

    def add(self, keep, send):
        self.keeps.append(keep.reshape(2, -1, 128))
        self.gots.append(self.place.send(send.reshape(2, -1, 128), 1, 1))

    def wait(self, *first):
        if not first:
            return
        if len(self.steps) == self.count:
            self.gots = [after(g, *first) for g in self.gots]
        else:
            self.got = after(self.got, *first)

    def step(self):
        if self.keep is None:
            self.keeps[0] = self.turn(self.keeps[0])
        else:
            self.keep = self.turn(self.keep)
        return self.steps.pop(0)()

    def go(self, out, even, odd):
        self.got = self.place.send(out, even, odd)
        self.place.token = (out,)

    def turn(self, x):
        return after(x, *self.place.token) if self.place.token else x

    def collect(self):
        self.place.token = tuple(self.parts)

    def start(self):
        out, self.keep = mix_first(self.place.info, self.keeps, self.gots)
        self.go(out, 2, self.place.far[0])
        return out

    def second(self):
        out, self.keep = mix_half(self.place.info, SECOND, self.keep, self.got)
        self.go(out, self.place.far[0], 2)
        return out

    def halve(self, i):
        keep, got = self.keep, self.got
        out, self.keep = mix_half(self.place.info, HERE + i, keep, got)
        self.go(out, self.place.far[i], self.place.far[i])
        return out

    def exchange(self):
        self.keep = mix_sum(self.place.info, self.keep, self.got)
        self.go(self.keep, self.place.far[-1], self.place.far[-1])
        return self.keep

    def settle(self, i):
        if i == len(self.place.far) - 2:
            self.keep = mix_sum(self.place.info, self.keep, self.got)
        else:
            self.keep = mix_both(self.place.info, HERE + i + 1, self.keep, self.got)

    def spread(self):
        self.settle(1)
        x, z = self.place.far[:2]
        self.place.token = (self.keep,)
        self.parts = [self.keep] + [self.place.send(self.keep, f, f) for f in (x, z, x + z)]

    def double(self, i):
        self.settle(i)
        self.go(self.keep, self.place.far[i], self.place.far[i])
        return self.keep


def gather_parts(info, parts, total):
    x, z = info[HERE], info[HERE + 1]
    for part, (i, j) in zip(parts, ((x, z), (1 - x, z), (x, 1 - z), (1 - x, 1 - z))):
        total[2 * i + j] = part[...]


def spread(o, total, at, rows, blocks):
    half = total.shape[1]
    for j in range(blocks):
        done = 0
        while done < rows:
            part, row = divmod(at + j * rows + done, half)
            n = min(rows - done, half - row)
            o[done : done + n, 128 * j : 128 * (j + 1)] = total[part, row : row + n, :].astype(o.dtype)
            done += n


def finish_one(info, parts):
    def body(i, *refs):
        down, total = refs[4:]
        gather_parts(i, refs[:4], total)
        spread(down, total, 0, FF // 4, D // 128)

    return pl.pallas_call(
        body,
        out_shape=hbm((FF // 4, D), F32),
        in_specs=[SM] + [VM] * 4,
        out_specs=VM,
        scratch_shapes=[pltpu.VMEM((4,) + parts[0].shape, BF16)],
        compiler_params=params(),
        cost_estimate=cost(1e7, 1e7),
        name="finish_one",
    )(info, *parts)


def finish_two(info, parts_a, parts_b):
    gr = D // 4
    blocks = FH // 128

    def body(i, *refs):
        gate, up, out, total_a, total_b = refs[8:]
        gather_parts(i, refs[:4], total_a)
        gather_parts(i, refs[4:8], total_b)
        for k, total in enumerate((total_a, total_b)):
            spread(gate.at[:, pl.ds(FH * k, FH)], total, 0, gr, blocks)
            spread(up.at[:, pl.ds(FH * k, FH)], total, gr * blocks, gr, blocks)
        spread(out, total_b, 2 * gr * blocks, HEAD_DIM, D // 128)

    return pl.pallas_call(
        body,
        out_shape=(hbm((gr, FF), F32), hbm((gr, FF), F32), hbm((HEAD_DIM, D), F32)),
        in_specs=[SM] + [VM] * 8,
        out_specs=(VM,) * 3,
        scratch_shapes=[
            pltpu.VMEM((4,) + parts_a[0].shape, BF16),
            pltpu.VMEM((4,) + parts_b[0].shape, BF16),
        ],
        compiler_params=params(),
        cost_estimate=cost(1e7, 1e7),
        name="finish_two",
    )(info, *parts_a, *parts_b)


def finish_three(info, parts, query_w, key_w, value_w, gain):
    gr = D // 4

    def body(i, *refs):
        wq, wk, wv, g, query, key, value = refs[4:11]
        first, g_query, g_key, g_att, g_mid, g_out, total, prod, gains = refs[11:]
        gather_parts(i, refs[:4], total)
        spread(query, total, 0, gr, 8)
        spread(key, total, 8 * gr, gr, 2)
        spread(value, total, 10 * gr, gr, 2)
        spread(gains, total, 12 * gr, 16, 2)
        base = HEADS * HEAD_DIM
        prod[:, :base] = query[...] * wq[...].astype(F32)
        prod[:, base : base + HEAD_DIM] = key[...] * wk[...].astype(F32)
        prod[:, base + HEAD_DIM :] = value[...] * wv[...].astype(F32)
        p = prod[...]
        high = p.astype(BF16)
        low = (p - high.astype(F32)).astype(BF16)
        ones = jnp.ones((16, 6 * HEAD_DIM), BF16)
        summed = dot(ones, high, NT) + dot(ones, low, NT)
        first[...] = summed[0:1, :].reshape(-1) / g[...].astype(F32)
        for row, o in ((1, g_att), (2, g_mid), (3, g_out), (4, g_query), (5, g_key)):
            o[...] = gains[row : row + 1, : o.shape[0]].reshape(-1)

    return pl.pallas_call(
        body,
        out_shape=(
            hbm((gr, HEADS * HEAD_DIM), F32),
            hbm((gr, HEAD_DIM), F32),
            hbm((gr, HEAD_DIM), F32),
            sds((gr,), F32),
            sds((HEAD_DIM // 4,), F32),
            sds((HEAD_DIM // 4,), F32),
            sds((gr,), F32),
            sds((gr,), F32),
            sds((gr,), F32),
        ),
        in_specs=[SM] + [VM] * 8,
        out_specs=(VM,) * 9,
        scratch_shapes=[
            pltpu.VMEM((4,) + parts[0].shape, BF16),
            pltpu.VMEM((gr, 6 * HEAD_DIM), F32),
            pltpu.VMEM((16, HEAD_DIM), F32),
        ],
        compiler_params=params(),
        cost_estimate=cost(1e7, 1e7),
        name="finish_three",
    )(info, *parts, query_w, key_w, value_w, gain)


def shards(
    tokens,
    query_weight,
    key_weight,
    value_weight,
    out_weight,
    gate_weight,
    up_weight,
    down_weight,
    input_gain,
    query_gain,
    key_gain,
    attended_gain,
    middle_gain,
    output_gain,
    cotangent,
):
    n_seq = lax.axis_size("seq")
    n_shard = lax.axis_size("shard")
    shard = lax.axis_index("shard")
    count = tokens.shape[0]
    total = count * n_seq * n_shard
    length = min(SEQ_CAP, total)
    rank = lax.axis_index("seq") * n_shard + shard
    first_pos = rank * count % length
    place = Place(first_pos)
    me = flag = place.info
    gd = D // 4
    gh = HEAD_DIM // 4

    kvg = pack(
        me,
        key_weight,
        value_weight,
        input_gain,
        attended_gain,
        middle_gain,
        output_gain,
        query_gain,
        key_gain,
    )
    def near(x):
        return flip(x, "shard", 1)

    def far(x):
        return flip(x, "shard", 2)

    q_far = far(query_weight)
    kvg_far = far(kvg)
    kvgs = (kvg, near(kvg), kvg_far, near(kvg_far))
    q_near = near(query_weight)
    out_near, gate_near, up_near, down_near = (
        near(out_weight), near(gate_weight), near(up_weight), near(down_weight)
    )

    def relay(x):
        return flip(x, "seq", 1)

    gate_half, up_half, down_half = halves(me, gate_weight, up_weight, down_weight)

    positions = first_pos + jnp.arange(count, dtype=jnp.int32)
    hd = HEAD_DIM // 2
    freq = ROPE_BASE ** (-(jnp.arange(hd, dtype=F32) * 2.0 / HEAD_DIM))
    angles = positions.astype(F32)[:, None] * freq[None, :]
    cos = jnp.cos(angles)
    sin = jnp.sin(angles)

    gains = gains_of(me, kvgs)
    kvgs = pinned(*kvgs)
    nin, kraw, kv_lo, kv_hi = pre_kv(me, tokens, gains, cos, sin, kvgs)
    ranks = n_seq * n_shard
    per_seq = length // count
    pairs = [(i, i + 1) for i in range(ranks - 1) if (i + 1) % per_seq]
    halo = lax.ppermute(kv_hi, ("seq", "shard"), pairs)
    out_far = far(out_weight)
    gate_a = far(gate_half)
    q_far = after(q_far, nin)
    qs_w = pinned(query_weight, q_near, q_far, near(q_far))
    up_a = far(after(up_half, gate_a))
    gate_b = relay(gate_a)
    qraw, qs = pre_q(me, nin, gains, cos, sin, qs_w)
    qs = after(qs, out_far, gate_a)
    o_hi, pm_hi, p1_hi = att(flag, qs, kv_lo, kv_hi, False, 1)
    o_lo, pm_lo, p1_lo = att(flag, after(qs, o_hi), halo, kv_lo, True, 0)
    gate_b = after(gate_b, o_lo)
    up_a = after(up_a, o_lo)
    down_a = far(after(down_half, up_a))
    up_b = relay(up_a)
    outs = pinned(out_weight, out_near, out_far, near(out_far))
    ap, nm = mid_part(me, o_lo, o_hi, tokens, gains, outs)
    gates = pinned(gate_weight, gate_near, gate_a, gate_b, near(gate_a), near(gate_b))
    act, slope = ff(me, nm, gates)
    up_b = after(up_b, act)
    down_a = after(down_a, act)
    down_b = relay(down_a)
    ups = pinned(up_weight, up_near, up_a, up_b, near(up_a), near(up_b))
    hid, bact = ff(me, nm, ups, (act, slope))
    down_b = after(down_b, hid)
    downs = pinned(down_weight, down_near, down_a, down_b, near(down_a), near(down_b))
    block_out, dd, wd, keep, send, gain_down = down_part(
        me, hid, tokens, cotangent, ap, gains, downs
    )
    chains = {name: Chain(place) for name in "abcd"}

    def advance(order, *first):
        for name in order:
            chain = chains[name.lower()]
            if name.isupper():
                chain.parts = [after(x, *first) for x in chain.parts]
                chain.collect()
            elif chain.steps:
                chain.wait(*first)
                chain.step()

    chains["d"].add(keep, send)
    keep, send, dnm = fb(me, nm, dd, act, bact, wd, gates, ups, 0, None)
    chains["a"].add(keep, send)
    advance(ORDER[0], dnm)
    dnm = after(dnm, *place.token)
    keep, send, dnm = fb(me, nm, dd, act, bact, wd, gates, ups, 1, dnm)
    chains["b"].add(keep, send)
    advance(ORDER[1], dnm)
    keep, send, d_o, d_mid, gain_mid = fe(
        me, o_lo, o_hi, tokens, cotangent, gains, ap, after(dnm, *place.token), outs
    )
    chains["b"].add(keep, send)
    advance(ORDER[2], d_o)
    dq_lo, kv_back, kv_a, gq_lo = att_back(
        qs, qraw, halo, kv_lo, pm_lo, p1_lo, after(d_o, *place.token), gains, cos, sin, 0
    )
    returned = lax.ppermute(kv_back, ("seq", "shard"), [(j, i) for i, j in pairs])
    advance(ORDER[3], dq_lo)
    dq_hi, kv_b, kv_c, gq_hi = att_back(
        qs, qraw, kv_lo, kv_hi, pm_hi, p1_hi, after(d_o, dq_lo, *place.token), gains, cos, sin, 1
    )
    advance(ORDER[4], dq_hi)
    dkv, keep, send = post(
        me,
        nin,
        (dq_lo, after(dq_hi, *place.token)),
        (kv_a, kv_b, kv_c, returned),
        kraw,
        gains,
        cos,
        sin,
        (gq_lo, gq_hi, gain_mid, gain_down),
    )
    chains["c"].add(keep, send)
    advance(ORDER[5], keep)
    grad_tokens = last(
        me, tokens, d_mid, (dq_lo, dq_hi), after(dkv, *place.token), gains, qs_w, kvgs
    )
    advance(ORDER[6], grad_tokens)
    for name in "dacb":
        advance(name * len(chains[name].steps))
    r_down = finish_one(me, chains["d"].parts)
    r_query, r_key, r_value, *r_gains = finish_three(
        me,
        chains["c"].parts,
        query_weight,
        key_weight,
        value_weight,
        input_gain,
    )
    r_gate, r_up, r_out = finish_two(me, chains["a"].parts, chains["b"].parts)
    return (
        block_out,
        grad_tokens,
        r_query,
        r_key,
        r_value,
        r_out,
        r_gate,
        r_up,
        r_down,
        *r_gains,
    )


def solution(mesh):
    token = P(("seq", "shard"), None)
    matrix = P("shard", None)
    vector = P("shard")
    in_specs = (token,) + (matrix,) * 7 + (vector,) * 6 + (token,)
    out_specs = (token, token) + (matrix,) * 7 + (vector,) * 6
    return jax.shard_map(shards, mesh=mesh, in_specs=in_specs, out_specs=out_specs, check_vma=False)
```
